128 devices in a mesh: blocks: 128 (over y, z, x, core).
Axes of the slice: x: 4, y: 4, z: 4, core: 2. Of those that a mesh axis runs over, the one named last changes fastest.
Arguments:
- spectra: float32 [4608, 66, 512], P('blocks'), may hold values from 0.05 to 2
- courant: float32 [4608, 3, 512], P('blocks'), may hold values from 0.05 to 0.3
- kernel: bfloat16 [66, 4356], replicated, may hold values from -0.09375 to 0.09375
- old_count: int32 [128], replicated, may hold values from 12 to 36, as said below
- new_count: int32 [128], replicated, may hold values from 12 to 36, as said below
- upwind: int32 [3072, 3], replicated, may hold values from 0 to 3071, as said below
Outputs:
- updated: float32 [4608, 66, 512], P('blocks')
The draws below stay inside these ranges and needn't reach their ends.
Inputs may be any that keep to these rules, and one draw needn't show every extreme that they name: `old_count`: each count lies in the stated range and both ends are reached in the old and in the new layout; the counts sum to 3072; between the two layouts every device boundary along the curve moves by at most 12 blocks, and in every draw some boundary moves by exactly 12 blocks toward higher devices and another by exactly 12 toward lower devices. `new_count`: as old_count, for the new layout. Blocks form aligned runs of 12 along the curve, each run one cross-section of the grid; upwind[b, 0] = b - s * 12 cyclically over 3072, where s is +1 or -1 and depends only on b's position within its run, both signs occurring; upwind[b, 1] and upwind[b, 2] lie in the same run as b, arranged alike in every run; every block is upwind of exactly one block per direction.
All inputs are finite; a program needn't handle non-finite values.
Results may differ from the reference program's by a relative error of at most 0.0022.
Values sent between devices are 32-bit elements; how exact they have to be, the bound alone decides.
No kernel may reach another device: no remote copies, remote signals or barrier semaphores. Data moves between devices by JAX's collectives and lax.ppermute only.
A program may use at most 128 MiB of HBM per device.

```python
import math
import jax
import jax.numpy as jnp
from jax import lax

BLK_DEV = 24
HALF = 12
CAP = 36
NB = 3072
SLOTS = 4608
BINS = 66
EDGE = 8
CELLS = 512
PAIRS = 4356
N_BLOCKS = 128


def boundary_offsets(key):
    base = jax.random.fold_in(key, 4099)
    key_mag, key_sign, key_spot, key_pos = jax.random.split(base, 4)
    device_ids = jnp.arange(N_BLOCKS, dtype=jnp.int32)
    magnitude = jax.random.randint(key_mag, (N_BLOCKS,), HALF // 2, HALF + 1)
    spread_draw = jax.random.randint(key_pos, (N_BLOCKS,), 0, HALF + 1)
    higher = magnitude + spread_draw % (HALF - magnitude + 1)
    lower = higher - magnitude
    upward = jax.random.randint(key_sign, (N_BLOCKS,), 0, 2) == 1
    older = jnp.where(upward, higher, lower)
    newer = jnp.where(upward, lower, higher)
    chosen = jax.random.randint(key_spot, (), 1, N_BLOCKS - 2)
    older = jnp.where(device_ids == 0, 0, older)
    newer = jnp.where(device_ids == 0, 0, newer)
    older = jnp.where(device_ids == chosen - 1, 0, older)
    older = jnp.where(device_ids == chosen, HALF, older)
    older = jnp.where(device_ids == chosen + 1, 0, older)
    newer = jnp.where(device_ids == chosen, 0, newer)
    newer = jnp.where(device_ids == chosen + 1, HALF, newer)
    newer = jnp.where(device_ids == chosen + 2, 0, newer)
    return (older, newer)


def counts_from(offsets):
    return (BLK_DEV + offsets - jnp.roll(offsets, -1)).astype(jnp.int32)


def draw_old_count(key, part):
    return counts_from(boundary_offsets(key)[0])


def draw_new_count(key, part):
    return counts_from(boundary_offsets(key)[1])


def draw_upwind(key, part):
    order = jax.random.permutation(jax.random.fold_in(key, 811), HALF).astype(jnp.int32)
    inverse = jnp.argsort(order).astype(jnp.int32)
    signs = jax.random.randint(jax.random.fold_in(key, 907), (HALF,), 0, 2).astype(jnp.int32) * 2 - 1
    signs = signs.at[order[0]].set(1)
    signs = signs.at[order[1]].set(-1)
    blocks = N_BLOCKS * BLK_DEV
    sections = blocks // HALF
    block_ids = jnp.arange(blocks, dtype=jnp.int32)
    section = block_ids // HALF
    position = block_ids % HALF
    cross = inverse[position]
    across = cross // 2
    depth = cross % 2
    rows_across = HALF // 2
    x_up = (section - signs[position]) % sections * HALF + position
    y_up = section * HALF + order[(across - 1) % rows_across * 2 + depth]
    z_up = section * HALF + order[across * 2 + (1 - depth)]
    return jnp.stack([x_up, y_up, z_up], axis=1).astype(jnp.int32)


def levels(key, dims, cuts, least, high):
    factor_of = 1.0
    for dim, shards_of in cuts:
        draws = jax.random.uniform(jax.random.fold_in(jax.random.fold_in(key, 6), dim), (shards_of,), jnp.float32, least / len(cuts), high / len(cuts))
        factor_of = factor_of * jnp.repeat(jnp.exp(draws), dims[dim] // shards_of).reshape((-1,) + (1,) * (len(dims) - 1 - dim))
    return factor_of


def normal_values(stream_key, extent, scale, most, held_as=jnp.bfloat16):
    entries = scale * jax.random.normal(stream_key, extent, jnp.float32)
    return jnp.clip(entries, min=-most, max=most).astype(held_as)


def setup_inputs(seed: int = 0) -> dict:
    keys = jax.random.split(jax.random.key(seed), 7)
    return {
        "spectra": jnp.clip(jnp.exp(math.log(2.0) - 3.6888794 * jax.random.uniform(keys[0], (SLOTS, BINS, CELLS), jnp.float32) ** levels(keys[0], (SLOTS, BINS, CELLS), ((0, 128),), -0.2, 0.2)), 0.05, 2.0),
        "courant": jnp.clip(0.05 + 0.25 * jax.random.uniform(keys[1], (SLOTS, 3, CELLS), jnp.float32) ** levels(keys[1], (SLOTS, 3, CELLS), ((0, 128),), -0.2, 0.2), 0.05, 0.3),
        "kernel": normal_values(keys[2], (BINS, PAIRS), PAIRS ** -0.5, 0.09375),
        "old_count": draw_old_count(jax.random.fold_in(keys[6], 71), 0),
        "new_count": draw_new_count(jax.random.fold_in(keys[6], 71), 0),
        "upwind": draw_upwind(jax.random.fold_in(keys[6], 71), 0),
    }


def exclusive(counts):
    return jnp.cumsum(counts) - counts


def minmod_value(lower, outer):
    return 0.5 * (jnp.sign(lower) + jnp.sign(outer)) * jnp.minimum(jnp.abs(lower), jnp.abs(outer))


def limited(outer, speeds, upwind_value):
    return speeds * (outer + 0.5 * (1.0 - speeds) * minmod_value(outer - upwind_value, outer))


def slots_of(counts):
    starts = exclusive(counts)
    block_ids = jnp.arange(NB, dtype=jnp.int32)
    owner_ids = jnp.sum((block_ids[:, None] >= starts[None, :]).astype(jnp.int32), axis=1) - 1
    return (owner_ids * CAP + block_ids - starts[owner_ids]).astype(jnp.int32)


def reference(spectra, courant, kernel, old_count, new_count, upwind):
    old_slot = slots_of(old_count)
    state = spectra[old_slot].reshape(NB, BINS, EDGE, EDGE, EDGE)
    speeds = courant[old_slot].reshape(NB, 3, EDGE, EDGE, EDGE)
    fluxes = [speeds[:, direction][:, None] * state for direction in range(3)]
    first = state
    for direction in range(3):
        cell_axis = 2 + direction
        face_in = lax.index_in_dim(fluxes[direction], EDGE - 1, cell_axis, keepdims=True)[upwind[:, direction]]
        inflow = jnp.concatenate([face_in, lax.slice_in_dim(fluxes[direction], 0, EDGE - 1, axis=cell_axis)], axis=cell_axis)
        first = first - fluxes[direction] + inflow
    second = first
    for direction in range(3):
        cell_axis = 2 + direction
        layer_in = lax.index_in_dim(first, EDGE - 1, cell_axis, keepdims=True)[upwind[:, direction]]
        upwind_value = jnp.concatenate([layer_in, lax.slice_in_dim(first, 0, EDGE - 1, axis=cell_axis)], axis=cell_axis)
        cell_flux = limited(first, speeds[:, direction][:, None], upwind_value)
        face_in = lax.index_in_dim(cell_flux, EDGE - 1, cell_axis, keepdims=True)[upwind[:, direction]]
        inflow = jnp.concatenate([face_in, lax.slice_in_dim(cell_flux, 0, EDGE - 1, axis=cell_axis)], axis=cell_axis)
        second = second - cell_flux + inflow
    grouped = second.reshape(NB, BINS, CELLS)

    def coalesce(block):
        pair_terms = (block[:, None, :] * block[None, :, :]).reshape(PAIRS, CELLS).astype(jnp.bfloat16)
        return block + jnp.dot(kernel, pair_terms, preferred_element_type=jnp.float32)

    coalesced = lax.map(coalesce, grouped)
    new_slot = slots_of(new_count)
    return jnp.zeros((SLOTS, BINS, CELLS), jnp.float32).at[new_slot].set(coalesced)
```

```python
import functools

import jax
import jax.numpy as jnp
from jax import lax
from jax.experimental import pallas as pl
from jax.experimental.pallas import tpu as pltpu
from jax.sharding import PartitionSpec as P

RUN = 12
BINS = 66
CELLS = 512
HALF = 256
LANES = 128
PACKED = 72
FULL = 64
TERMS = 2304
FACES = 18
F32 = jnp.float32
VMEM = pl.BlockSpec(memory_space=pltpu.VMEM)
SMEM = pl.BlockSpec(memory_space=pltpu.SMEM)
OLD0, OLD1, MID0, MID1, NEW0, NEW1 = range(6)


def params(mib):
    return pltpu.CompilerParams(vmem_limit_bytes=mib * 2**20)


def lanes():
    return lax.broadcasted_iota(jnp.int32, (1, LANES), 1)


def span(v):
    return slice(v * LANES, (v + 1) * LANES)


def upper():
    return lanes() >= 64


def last_y():
    return lanes() // 8 % 8 == 7


def last_z():
    return lanes() % 8 == 7


def swap(x):
    return pltpu.roll(x, 64, 1)


def step_y(x):
    return jnp.where(lanes() // 8 % 8 == 0, pltpu.roll(x, 72, 1), pltpu.roll(x, 8, 1))


def step_z(x):
    return jnp.where(lanes() % 8 == 0, pltpu.roll(x, 121, 1), pltpu.roll(x, 1, 1))


def minmod(a, e):
    return jnp.maximum(jnp.minimum(a, e), 0.0) + jnp.minimum(jnp.maximum(a, e), 0.0)


def limited(q, c, before):
    return c * (q + (0.5 * (1.0 - c)) * minmod(q - before, q))


def upwind_of(table, position):
    back = table[3 * position] < RUN + position
    return back, table[3 * position + 1] - RUN, table[3 * position + 2] - RUN


def donor(q, c, q_prev, cx_prev, q_y, c_y, q_z, c_z):
    cx, cy, cz = c[0:1], c[1:2], c[2:3]
    up, ly, lz = upper(), last_y(), last_z()
    in_x = swap(jnp.where(up, cx_prev, cx) * jnp.where(up, q_prev, q))
    in_y = step_y(jnp.where(ly, c_y[1:2], cy) * jnp.where(ly, q_y, q))
    in_z = step_z(jnp.where(lz, c_z[2:3], cz) * jnp.where(lz, q_z, q))
    return (1.0 - (cx + cy + cz)) * q + in_x + in_y + in_z


def fetch(block, scal, spectra, courant, low, high, rows, q_dst, c_dst, at):
    own0, own1 = scal[OLD0], scal[OLD1]

    @pl.when((block >= own0) & (block < own1))
    def _():
        q_dst[at] = spectra[block - own0]
        c_dst[at, 0:3] = courant[block - own0]

    @pl.when(block < own0)
    def _():
        i = block - own0 + RUN
        q_dst[at] = low[i, 0:BINS]
        c_dst[at, 0:3] = low[i, BINS : BINS + 3]

    @pl.when(block >= own1)
    def _():
        i = block - own1
        q_dst[at] = high[i, 0:BINS]
        c_dst[at, 0:3] = high[i, BINS : BINS + 3]


def pack_kernel(scal, tail_q, tail_c, head_q, head_c, up, down):
    pad = jnp.zeros((1, PACKED - BINS - 3, CELLS), F32)
    up[...] = jnp.concatenate([tail_q[...], tail_c[...], pad], axis=1)
    down[...] = jnp.concatenate([head_q[...], head_c[...], pad], axis=1)


def pack(spectra, courant, tail_start):
    def tail(i, scal):
        return (scal[0] + i, 0, 0)

    def head(i, scal):
        return (i, 0, 0)

    return pl.pallas_call(
        pack_kernel,
        grid_spec=pltpu.PrefetchScalarGridSpec(
            num_scalar_prefetch=1,
            grid=(RUN,),
            in_specs=[
                pl.BlockSpec((1, BINS, CELLS), tail),
                pl.BlockSpec((1, 3, CELLS), tail),
                pl.BlockSpec((1, BINS, CELLS), head),
                pl.BlockSpec((1, 3, CELLS), head),
            ],
            out_specs=[pl.BlockSpec((1, PACKED, CELLS), head)] * 2,
        ),
        out_shape=[jax.ShapeDtypeStruct((RUN, PACKED, CELLS), F32)] * 2,
        compiler_params=params(24),
    )(tail_start, spectra, courant, spectra, courant)


def face_kernel(scal, table, spectra, courant, low, high, up, down, q0, cs):
    count = scal[MID1] - scal[MID0]

    def gather(j, _):
        first = scal[MID0] + jnp.where(j < RUN, j, count - 2 * RUN + j)
        fetch(first, scal, spectra, courant, low, high, BINS, q0, cs, j)
        return 0

    lax.fori_loop(0, 2 * RUN, gather, 0)

    def face(j, position):
        _, y, z = upwind_of(table, position)
        uy, uz = y + (j - position), z + (j - position)
        s, t = span(1), span(0)
        q, c = q0[j, :, s], cs[j, :, s]
        q1 = donor(q, c, q0[j, :, t], cs[j, 0:1, t], q0[uy, :, s], cs[uy, :, s], q0[uz, :, s], cs[uz, :, s])
        other = swap(q1)
        return jnp.where(upper(), limited(q1, c[0:1], other), other), c[0:1] * q

    for base, out in ((0, down), (RUN, up)):

        def pair(i, _, base=base, out=out):
            a0, b0 = face(base + 2 * i, 2 * i)
            a1, b1 = face(base + 2 * i + 1, 2 * i + 1)
            out[2 * i, 0:BINS] = a0
            out[2 * i + 1, 0:BINS] = a1
            out[RUN + i, 0:BINS] = jnp.where(upper(), b1, swap(b0))
            return 0

        lax.fori_loop(0, RUN // 2, pair, 0)


def faces(scal, table, spectra, courant, low, high):
    capacity = spectra.shape[0]

    def half(*dims):
        return pl.BlockSpec(dims + (HALF,), lambda i: (0, 0, 1))

    return pl.pallas_call(
        face_kernel,
        grid=(1,),
        in_specs=[
            SMEM,
            SMEM,
            half(capacity, BINS),
            half(capacity, 3),
            half(RUN, PACKED),
            half(RUN, PACKED),
        ],
        out_specs=[VMEM] * 2,
        out_shape=[jax.ShapeDtypeStruct((FACES, PACKED, LANES), F32)] * 2,
        scratch_shapes=[pltpu.VMEM((2 * RUN, BINS, HALF), F32), pltpu.VMEM((2 * RUN, 3, HALF), F32)],
        compiler_params=params(24),
    )(scal, table, spectra, courant, low, high)


def pair_terms(q):
    wide = q.shape[1]
    group = [q[8 * g : 8 * g + 8, :] for g in range(8)]
    row = [jnp.broadcast_to(q[i : i + 1, :], (8, wide)) for i in range(BINS)]
    out = [row[i] * group[g] for i in range(56) for g in range(i // 8 + 1, 8)]
    out += [row[i] * group[g] for i in (64, 65) for g in range(8)]
    for s in range(5):
        out += [x * (pltpu.roll(x, s, 0) if s else x) for x in group]
    at = lax.broadcasted_iota(jnp.int32, (8, wide), 0)
    rest = jnp.where(at < 2, row[64], row[65]) * jnp.where(at < 1, row[64], row[65])
    out.append(jnp.where(at < 3, rest, 0.0))
    return out + [jnp.zeros((8, wide), F32)] * (TERMS // 8 - len(out))


def symmetric_kernel(kernel):
    k = kernel.astype(F32).reshape(BINS, BINS, BINS)
    both = k + jnp.swapaxes(k, 1, 2)
    parts = [both[:, 8 * g : 8 * g + 8, 8 * g + 8 : FULL].reshape(BINS, -1) for g in range(7)]
    parts.append(both[:, FULL:BINS, 0:FULL].reshape(BINS, -1))
    diag = jnp.stack([both[:, 8 * g : 8 * g + 8, 8 * g : 8 * g + 8] for g in range(8)], axis=1)
    r = jnp.arange(8)
    for s in range(5):
        at = (r[None, :] == (r[:, None] - s) % 8).astype(F32)
        if s == 0:
            at = 0.5 * at
        if s == 4:
            at = at * (r[:, None] < 4)
        parts.append((diag * at).sum(axis=3).reshape(BINS, -1))
    parts.append(jnp.stack([k[:, 64, 64], both[:, 64, 65], k[:, 65, 65]], axis=1))
    used = sum(p.shape[1] for p in parts)
    parts.append(jnp.zeros((BINS, TERMS - used), F32))
    return jnp.pad(jnp.concatenate(parts, axis=1), ((0, 80 - BINS), (0, 0))).astype(jnp.bfloat16)


def coalesce(q, sym):
    terms = pair_terms(q)
    packed = [
        jnp.concatenate(terms[2 * r : 2 * r + 2], axis=0).astype(jnp.bfloat16) for r in range(TERMS // 16)
    ]
    gained = jnp.dot(sym[...], jnp.concatenate(packed, axis=0), preferred_element_type=F32)
    return q + gained[0:BINS]


def emit(l, count, value, out, up, down):
    out[l] = value

    @pl.when(l < RUN)
    def _():
        down[l] = value

    @pl.when(l >= count - RUN)
    def _():
        up[l - (count - RUN)] = value


def upper_kernel(scal, table, spectra, courant, low, high, sym, q1, cs, side, out, up, down, q0, fy, fz, q2):
    count = scal[MID1] - scal[MID0]

    def gather(l, _):
        fetch(scal[MID0] + l, scal, spectra, courant, low, high, BINS, q0, cs, l)
        return 0

    lax.fori_loop(0, count, gather, 0)

    def first(l, _):
        position = lax.rem(l, RUN)
        back, y, z = upwind_of(table, position)
        uy, uz = y + (l - position), z + (l - position)
        ux = jnp.where(back, l - RUN, l + RUN)
        here = ((ux >= 0) & (ux < count)).astype(F32)
        ux = jnp.clip(ux, 0, count - 1)
        q_prev, cx_prev = q0[ux, :, span(3)], cs[ux, 0:1, span(3)] * here
        for v in range(4):
            s = span(v)
            q, c = q0[l, :, s], cs[l, :, s]
            new = donor(q, c, q_prev, cx_prev, q0[uy, :, s], cs[uy, :, s], q0[uz, :, s], cs[uz, :, s])
            q1[l, :, s] = new
            q_prev, cx_prev = q, c[0:1]
        other = swap(new)
        side[l] = jnp.where(upper(), limited(new, c[0:1], other), other)
        return 0

    lax.fori_loop(0, count, first, 0)
    cross_flux(count, table, q1, cs, fy, fz, 2)

    def second(l, _):
        q_prev = q1[l, :, span(1)]
        f_prev = limited(q_prev, cs[l, 0:1, span(1)], swap(q_prev))
        for v in (2, 3):
            q = q1[l, :, span(v)]
            f = limited(q, cs[l, 0:1, span(v)], swap(jnp.where(upper(), q_prev, q)))
            q2[l, :, span(v - 2)] = q - f + swap(jnp.where(upper(), f_prev, f)) + cross(table, l, fy, fz, v - 2)
            q_prev, f_prev = q, f
        return 0

    lax.fori_loop(0, count, second, 0)

    def third(l, _):
        emit(l, count, coalesce(q2[l], sym), out, up, down)
        return 0

    lax.fori_loop(0, count, third, 0)


def cross_flux(count, table, q1, cs, fy, fz, v0):
    def body(l, _):
        position = lax.rem(l, RUN)
        _, y, z = upwind_of(table, position)
        uy, uz = y + (l - position), z + (l - position)
        for w in range(2):
            s = span(v0 + w)
            q, c = q1[l, :, s], cs[l, :, s]
            before_y = step_y(jnp.where(last_y(), q1[uy, :, s], q))
            before_z = step_z(jnp.where(last_z(), q1[uz, :, s], q))
            fy[l, :, span(w)] = limited(q, c[1:2], before_y)
            fz[l, :, span(w)] = limited(q, c[2:3], before_z)
        return 0

    lax.fori_loop(0, count, body, 0)


def cross(table, l, fy, fz, w):
    position = lax.rem(l, RUN)
    _, y, z = upwind_of(table, position)
    uy, uz = y + (l - position), z + (l - position)
    s = span(w)
    y_own, z_own = fy[l, :, s], fz[l, :, s]
    y_in = step_y(jnp.where(last_y(), fy[uy, :, s], y_own))
    z_in = step_z(jnp.where(last_z(), fz[uz, :, s], z_own))
    return (y_in - y_own) + (z_in - z_own)


def upper_half(scal, table, spectra, courant, low, high, sym):
    capacity = spectra.shape[0]
    return pl.pallas_call(
        upper_kernel,
        in_specs=[SMEM, SMEM] + [VMEM] * 5,
        out_specs=[VMEM] * 6,
        out_shape=[
            jax.ShapeDtypeStruct((capacity, BINS, CELLS), F32),
            jax.ShapeDtypeStruct((capacity, 3, CELLS), F32),
            jax.ShapeDtypeStruct((capacity, BINS, LANES), F32),
            jax.ShapeDtypeStruct((capacity, BINS, HALF), F32),
            jax.ShapeDtypeStruct((RUN, BINS, HALF), F32),
            jax.ShapeDtypeStruct((RUN, BINS, HALF), F32),
        ],
        scratch_shapes=[
            pltpu.VMEM((capacity, BINS, CELLS), F32),
            pltpu.VMEM((capacity, BINS, HALF), F32),
            pltpu.VMEM((capacity, BINS, HALF), F32),
            pltpu.VMEM((capacity, BINS, HALF), F32),
        ],
        compiler_params=params(48),
        cost_estimate=pl.CostEstimate(flops=8 * 10**9, bytes_accessed=20 * 10**6, transcendentals=0),
    )(scal, table, spectra, courant, low, high, sym)


def lower_kernel(scal, table, q1_in, cs, side, below, above, sym, out, up, down, q1, fy, fz, fx, q2):
    count = scal[MID1] - scal[MID0]

    def fix(l, _):
        position = lax.rem(l, RUN)
        back, _, _ = upwind_of(table, position)
        ux = jnp.where(back, l - RUN, l + RUN)
        q1[l] = q1_in[l]

        def remote(face):
            fx[l] = face[position, 0:BINS]
            flux = face[RUN + position // 2, 0:BINS]
            flux = jnp.where(lax.rem(position, 2) == 0, flux, swap(flux))
            q1[l, :, span(0)] += jnp.where(upper(), 0.0, flux)

        @pl.when(ux < 0)
        def _():
            remote(below)

        @pl.when(ux >= count)
        def _():
            remote(above)

        @pl.when((ux >= 0) & (ux < count))
        def _():
            fx[l] = side[ux]

        return 0

    lax.fori_loop(0, count, fix, 0)
    cross_flux(count, table, q1, cs, fy, fz, 0)

    def second(l, _):
        face = fx[l]
        q = q1[l, :, span(0)]
        f = limited(q, cs[l, 0:1, span(0)], jnp.where(upper(), swap(q), face))
        q2[l, :, span(0)] = q - f + swap(jnp.where(upper(), face, f)) + cross(table, l, fy, fz, 0)
        q_prev, f_prev = q, f
        q = q1[l, :, span(1)]
        f = limited(q, cs[l, 0:1, span(1)], swap(jnp.where(upper(), q_prev, q)))
        q2[l, :, span(1)] = q - f + swap(jnp.where(upper(), f_prev, f)) + cross(table, l, fy, fz, 1)
        return 0

    lax.fori_loop(0, count, second, 0)

    def third(l, _):
        emit(l, count, coalesce(q2[l], sym), out, up, down)
        return 0

    lax.fori_loop(0, count, third, 0)


def lower_half(scal, table, q1, cs, side, below, above, sym):
    capacity = q1.shape[0]
    halved = jax.ShapeDtypeStruct((capacity, BINS, HALF), F32)
    sent = jax.ShapeDtypeStruct((RUN, BINS, HALF), F32)

    def at_zero(*dims):
        return pl.BlockSpec(dims, lambda i: (0,) * len(dims))

    return pl.pallas_call(
        lower_kernel,
        grid=(1,),
        in_specs=[
            SMEM,
            SMEM,
            at_zero(capacity, BINS, HALF),
            at_zero(capacity, 3, HALF),
            at_zero(capacity, BINS, LANES),
            VMEM,
            VMEM,
            VMEM,
        ],
        out_specs=[VMEM] * 3,
        out_shape=[halved, sent, sent],
        scratch_shapes=[pltpu.VMEM((capacity, BINS, HALF), F32)] * 3
        + [pltpu.VMEM((capacity, BINS, LANES), F32), pltpu.VMEM((capacity, BINS, HALF), F32)],
        compiler_params=params(48),
        cost_estimate=pl.CostEstimate(flops=8 * 10**9, bytes_accessed=20 * 10**6, transcendentals=0),
    )(scal, table, q1, cs, side, below, above, sym)


def place_kernel(scal, own_u, low_u, high_u, own_l, low_l, high_l, out):
    start, end = scal[MID0], scal[MID1]
    count = scal[NEW1] - scal[NEW0]

    def body(s, _):
        block = scal[NEW0] + s
        live = s < count

        def put(lower, upper_, i):
            out[s, :, 0:HALF] = lower[i]
            out[s, :, HALF:CELLS] = upper_[i]

        @pl.when(live & (block >= start) & (block < end))
        def _():
            put(own_l, own_u, block - start)

        @pl.when(live & (block < start))
        def _():
            put(low_l, low_u, block - start + RUN)

        @pl.when(live & (block >= end))
        def _():
            put(high_l, high_u, block - end)

        @pl.when(jnp.logical_not(live))
        def _():
            out[s] = jnp.zeros((BINS, CELLS), F32)

        return 0

    lax.fori_loop(0, out.shape[0], body, 0)


def place(scal, *pieces):
    capacity = pieces[0].shape[0]
    return pl.pallas_call(
        place_kernel,
        in_specs=[SMEM] + [VMEM] * 6,
        out_specs=VMEM,
        out_shape=jax.ShapeDtypeStruct((capacity, BINS, CELLS), F32),
        compiler_params=params(32),
    )(scal, *pieces)


def bounds(device, devices, old_count, new_count):
    ids = jnp.arange(devices, dtype=jnp.int32)
    counts = jnp.stack([old_count, new_count])

    def start(p):
        old, new = jnp.sum(jnp.where(ids < p, counts, 0), axis=1)
        least = (jnp.maximum(old, new) - RUN + RUN - 1 + RUN) // RUN * RUN - RUN
        most = (jnp.minimum(old, new) + RUN) // RUN * RUN
        return old, jnp.clip(2 * RUN * p, least, most), new

    old0, mid0, new0 = start(device)
    old1, mid1, new1 = start(device + 1)
    return jnp.stack([old0, old1, mid0, mid1, new0, new1]).astype(jnp.int32)


def on_device(devices, spectra, courant, kernel, old_count, new_count, upwind):
    device = lax.axis_index("blocks").astype(jnp.int32)
    rise = [(i, i + 1) for i in range(devices - 1)]
    fall = [(i + 1, i) for i in range(devices - 1)]
    around = [(i, (i + 1) % devices) for i in range(devices)]
    reverse = [(j, i) for i, j in around]

    def move(block, route):
        return lax.ppermute(block, "blocks", route)

    tail_start = lax.dynamic_slice(old_count, (device,), (1,)) - RUN
    tail, head = pack(spectra, courant, tail_start)
    low, high = move(tail, rise), move(head, fall)
    scal = bounds(device, devices, old_count, new_count)
    table = upwind[RUN : 2 * RUN].reshape(-1)
    sym = symmetric_kernel(kernel)
    up, down = faces(scal, table, spectra, courant, low, high)
    below, above = move(up, around), move(down, reverse)
    q1, cs, side, own_u, up_u, down_u = upper_half(scal, table, spectra, courant, low, high, sym)
    low_u, high_u = move(up_u, rise), move(down_u, fall)
    own_l, up_l, down_l = lower_half(scal, table, q1, cs, side, below, above, sym)
    low_l, high_l = move(up_l, rise), move(down_l, fall)
    return place(scal, own_u, low_u, high_u, own_l, low_l, high_l)


def solution(mesh):
    in_specs = (P("blocks", None, None), P("blocks", None, None), P(), P(), P(), P())
    out_specs = P("blocks", None, None)
    return jax.shard_map(
        functools.partial(on_device, mesh.shape["blocks"]),
        mesh=mesh,
        in_specs=in_specs,
        out_specs=out_specs,
        check_vma=False,
    )
```

```python
import functools

import jax
import jax.numpy as jnp
import numpy as np
from jax import lax
from jax.experimental import pallas as pl
from jax.experimental.pallas import tpu as pltpu
from jax.sharding import PartitionSpec as P

RUN = 12
BINS = 66
CELLS = 512
HALF = 256
LANES = 128
PACKED = 72
FULL = 64
TERMS = 2304
GROUPS = 9
FACES = 18
F32 = jnp.float32
VMEM = pl.BlockSpec(memory_space=pltpu.VMEM)
SMEM = pl.BlockSpec(memory_space=pltpu.SMEM)
OLD0, OLD1, MID0, MID1, NEW0, NEW1 = range(6)


def params(mib):
    return pltpu.CompilerParams(vmem_limit_bytes=mib * 2**20)


def lanes():
    return lax.broadcasted_iota(jnp.int32, (8, LANES), 1)


def span(v):
    return slice(v * LANES, (v + 1) * LANES)


def upper():
    return lanes() >= 64


def last_y():
    return lanes() // 8 % 8 == 7


def last_z():
    return lanes() % 8 == 7


def view(x):
    return x.reshape(GROUPS, 8, LANES)


def flat(x):
    return x.reshape(PACKED, LANES)


def swap(x):
    return pltpu.roll(flat(x), 64, 1).reshape(x.shape)


def permuted(x, source):
    return view(jnp.take_along_axis(flat(x), source, axis=1))


def wide_lanes():
    return lax.broadcasted_iota(jnp.int32, (PACKED, LANES), 1)


def step_y(x):
    at = wide_lanes()
    return permuted(x, jnp.where(at // 8 % 8 == 0, at + 56, at - 8))


def step_z(x):
    at = wide_lanes()
    return permuted(x, jnp.where(at % 8 == 0, at + 7, at - 1))


def minmod(a, e):
    return jnp.maximum(jnp.minimum(a, e), 0.0) + jnp.minimum(jnp.maximum(a, e), 0.0)


def limited(q, c, before):
    return c * (q + (0.5 * (1.0 - c)) * minmod(q - before, q))


def upwind_of(table, position):
    back = table[3 * position] < RUN + position
    return back, table[3 * position + 1] - RUN, table[3 * position + 2] - RUN


def read(ref, l, v):
    return view(ref[l, :, span(v)])


def speed(ref, l, d, v):
    return ref[l, 8 * d : 8 * d + 8, span(v)]


def donor(q0, cs, l, v, q_prev, cx_prev, uy, uz):
    q, cx, cy, cz = read(q0, l, v), speed(cs, l, 0, v), speed(cs, l, 1, v), speed(cs, l, 2, v)
    up, ly, lz = upper(), last_y(), last_z()
    in_x = swap(jnp.where(up, cx_prev, cx) * jnp.where(up, q_prev, q))
    in_y = step_y(jnp.where(ly, speed(cs, uy, 1, v), cy) * jnp.where(ly, read(q0, uy, v), q))
    in_z = step_z(jnp.where(lz, speed(cs, uz, 2, v), cz) * jnp.where(lz, read(q0, uz, v), q))
    return (1.0 - (cx + cy + cz)) * q + in_x + in_y + in_z


def fetch(block, scal, spectra, courant, low, high, q_dst, c_dst, at):
    own0, own1 = scal[OLD0], scal[OLD1]

    def spread(ref, i, row):
        for d in range(3):
            c_dst[at, 8 * d : 8 * d + 8] = jnp.broadcast_to(
                ref[i, row + d : row + d + 1], (8,) + ref.shape[2:]
            )

    @pl.when((block >= own0) & (block < own1))
    def _():
        q_dst[at, 0:BINS] = spectra[block - own0]
        spread(courant, block - own0, 0)

    def received(ref, i):
        q_dst[at] = ref[i]
        spread(ref, i, BINS)

    @pl.when(block < own0)
    def _():
        received(low, block - own0 + RUN)

    @pl.when(block >= own1)
    def _():
        received(high, block - own1)


def pack_kernel(scal, tail_q, tail_c, head_q, head_c, up, down):
    pad = jnp.zeros((1, PACKED - BINS - 3, CELLS), F32)
    up[...] = jnp.concatenate([tail_q[...], tail_c[...], pad], axis=1)
    down[...] = jnp.concatenate([head_q[...], head_c[...], pad], axis=1)


def pack(spectra, courant, tail_start):
    def tail(i, scal):
        return (scal[0] + i, 0, 0)

    def head(i, scal):
        return (i, 0, 0)

    return pl.pallas_call(
        pack_kernel,
        grid_spec=pltpu.PrefetchScalarGridSpec(
            num_scalar_prefetch=1,
            grid=(RUN,),
            in_specs=[
                pl.BlockSpec((1, BINS, CELLS), tail),
                pl.BlockSpec((1, 3, CELLS), tail),
                pl.BlockSpec((1, BINS, CELLS), head),
                pl.BlockSpec((1, 3, CELLS), head),
            ],
            out_specs=[pl.BlockSpec((1, PACKED, CELLS), head)] * 2,
        ),
        out_shape=[jax.ShapeDtypeStruct((RUN, PACKED, CELLS), F32)] * 2,
        compiler_params=params(24),
    )(tail_start, spectra, courant, spectra, courant)


def face_kernel(scal, table, spectra, courant, low, high, up, down, q0, cs):
    count = scal[MID1] - scal[MID0]

    def gather(j, _):
        first = scal[MID0] + jnp.where(j < RUN, j, count - 2 * RUN + j)
        fetch(first, scal, spectra, courant, low, high, q0, cs, j)
        return 0

    lax.fori_loop(0, 2 * RUN, gather, 0)

    def face(j, position):
        _, y, z = upwind_of(table, position)
        uy, uz = y + (j - position), z + (j - position)
        q1 = donor(q0, cs, j, 1, read(q0, j, 0), speed(cs, j, 0, 0), uy, uz)
        other = swap(q1)
        c = speed(cs, j, 0, 1)
        return jnp.where(upper(), limited(q1, c, other), other), c * read(q0, j, 1)

    for base, out in ((0, down), (RUN, up)):

        def pair(i, _, base=base, out=out):
            a0, b0 = face(base + 2 * i, 2 * i)
            a1, b1 = face(base + 2 * i + 1, 2 * i + 1)
            out[2 * i] = flat(a0)
            out[2 * i + 1] = flat(a1)
            out[RUN + i] = flat(jnp.where(upper(), b1, swap(b0)))
            return 0

        lax.fori_loop(0, RUN // 2, pair, 0)


def faces(scal, table, spectra, courant, low, high):
    capacity = spectra.shape[0]

    def half(*dims):
        return pl.BlockSpec(dims + (HALF,), lambda i: (0, 0, 1))

    return pl.pallas_call(
        face_kernel,
        grid=(1,),
        in_specs=[
            SMEM,
            SMEM,
            half(capacity, BINS),
            half(capacity, 3),
            half(RUN, PACKED),
            half(RUN, PACKED),
        ],
        out_specs=[VMEM] * 2,
        out_shape=[jax.ShapeDtypeStruct((FACES, PACKED, LANES), F32)] * 2,
        scratch_shapes=[pltpu.VMEM((2 * RUN, PACKED, HALF), F32), pltpu.VMEM((2 * RUN, 24, HALF), F32)],
        compiler_params=params(24),
    )(scal, table, spectra, courant, low, high)


def pair_terms(q):
    wide = q.shape[1]
    group = [q[8 * g : 8 * g + 8, :] for g in range(8)]
    row = [jnp.broadcast_to(q[i : i + 1, :], (8, wide)) for i in range(BINS)]
    out = [row[i] * group[g] for i in range(56) for g in range(i // 8 + 1, 8)]
    out += [row[i] * group[g] for i in (64, 65) for g in range(8)]
    for s in range(5):
        out += [x * (pltpu.roll(x, s, 0) if s else x) for x in group]
    at = lax.broadcasted_iota(jnp.int32, (8, wide), 0)
    rest = jnp.where(at < 2, row[64], row[65]) * jnp.where(at < 1, row[64], row[65])
    out.append(jnp.where(at < 3, rest, 0.0))
    return out + [jnp.zeros((8, wide), F32)] * (TERMS // 8 - len(out))


def pair_columns():
    pairs = [(i, j) for i in range(56) for j in range(i // 8 * 8 + 8, FULL)]
    pairs += [(i, j) for i in (64, 65) for j in range(FULL)]
    for s in range(5):
        for g in range(0, FULL, 8):
            pairs += [(g + r, g + (r - s) % 8) if s < 4 or r < 4 else None for r in range(8)]
    pairs += [(64, 64), (64, 65), (65, 65)]
    pairs += [None] * (TERMS - len(pairs))
    one = [p[0] * BINS + p[1] if p else -1 for p in pairs]
    two = [p[1] * BINS + p[0] if p and p[0] != p[1] else -1 for p in pairs]
    return np.array([one, two], np.int32)


def symmetric_kernel_body(columns, kernel, out):
    width = out.shape[1]
    one, two = columns[0:1], columns[1:2]

    def chunk(i, total):
        base = pl.multiple_of(i * 256, 256)
        row = lax.broadcasted_iota(jnp.int32, (256, width), 0) + base
        pick = jnp.where((row == one) | (row == two), 1.0, 0.0).astype(jnp.bfloat16)
        return total + jnp.dot(kernel[:, pl.ds(base, 256)], pick, preferred_element_type=F32)

    total = lax.fori_loop(0, kernel.shape[1] // 256, chunk, jnp.zeros((80, width), F32))
    out[...] = total.astype(jnp.bfloat16)


def symmetric_kernel(kernel):
    wide = -(-kernel.shape[1] // 256) * 256
    padded = jnp.pad(kernel, ((0, 80 - BINS), (0, wide - kernel.shape[1])))
    return pl.pallas_call(
        symmetric_kernel_body,
        grid=(TERMS // 256,),
        in_specs=[
            pl.BlockSpec((2, 256), lambda i: (0, i)),
            pl.BlockSpec((80, wide), lambda i: (0, 0)),
        ],
        out_specs=pl.BlockSpec((80, 256), lambda i: (0, i)),
        out_shape=jax.ShapeDtypeStruct((80, TERMS), jnp.bfloat16),
        compiler_params=params(16),
        cost_estimate=pl.CostEstimate(flops=2 * 10**9, bytes_accessed=10**6, transcendentals=0),
    )(jnp.asarray(pair_columns()), padded)


def coalesce(q, sym):
    terms = pair_terms(q)
    packed = [
        jnp.concatenate(terms[2 * r : 2 * r + 2], axis=0).astype(jnp.bfloat16) for r in range(TERMS // 16)
    ]
    gained = jnp.dot(sym[...], jnp.concatenate(packed, axis=0), preferred_element_type=F32)
    return q + gained[0:PACKED]


def neighbours(table, l):
    position = lax.rem(l, RUN)
    back, y, z = upwind_of(table, position)
    return jnp.where(back, l - RUN, l + RUN), y + (l - position), z + (l - position)


def cross_flux(count, table, q1, cs, fy, fz, v0, vf):
    def cross_body(l, _):
        _, uy, uz = neighbours(table, l)
        for w in range(2):
            q = read(q1, l, v0 + w)
            before_y = step_y(jnp.where(last_y(), read(q1, uy, v0 + w), q))
            before_z = step_z(jnp.where(last_z(), read(q1, uz, v0 + w), q))
            fy[l, :, span(w)] = flat(limited(q, speed(cs, l, 1, vf + w), before_y))
            fz[l, :, span(w)] = flat(limited(q, speed(cs, l, 2, vf + w), before_z))
        return 0

    lax.fori_loop(0, count, cross_body, 0)


def cross(table, l, fy, fz, w):
    _, uy, uz = neighbours(table, l)
    y_own, z_own = read(fy, l, w), read(fz, l, w)
    y_in = step_y(jnp.where(last_y(), read(fy, uy, w), y_own))
    z_in = step_z(jnp.where(last_z(), read(fz, uz, w), z_own))
    return (y_in - y_own) + (z_in - z_own)


def finish(count, second, q2, sym, out, up, down):
    second(0)

    def third(l, _):
        out[l] = coalesce(q2[l], sym)[0:BINS]
        second(jnp.minimum(l + 1, count - 1))
        return 0

    lax.fori_loop(0, count, third, 0)

    def hand_on(k, _):
        down[k] = out[k]
        up[k] = out[count - RUN + k]
        return 0

    lax.fori_loop(0, RUN, hand_on, 0)


def upper_kernel(scal, table, spectra, courant, low, high, sym, low_q1, low_c, side, out, up, down, q0, cs, q1, fy, fz, q2):
    count = scal[MID1] - scal[MID0]

    def gather(l, _):
        fetch(scal[MID0] + l, scal, spectra, courant, low, high, q0, cs, l)
        low_c[l] = cs[l, :, 0:HALF]
        return 0

    lax.fori_loop(0, count, gather, 0)

    def first(l, _):
        ux, uy, uz = neighbours(table, l)
        here = ((ux >= 0) & (ux < count)).astype(F32)
        ux = jnp.clip(ux, 0, count - 1)
        q_prev, cx_prev = read(q0, ux, 3), speed(cs, ux, 0, 3) * here
        for v in range(4):
            new = donor(q0, cs, l, v, q_prev, cx_prev, uy, uz)
            q_prev, cx_prev = read(q0, l, v), speed(cs, l, 0, v)
            if v < 2:
                low_q1[l, :, span(v)] = flat(new)
            else:
                q1[l, :, span(v - 2)] = flat(new)
        other = swap(new)
        side[l] = flat(jnp.where(upper(), limited(new, cx_prev, other), other))
        return 0

    lax.fori_loop(0, count, first, 0)
    cross_flux(count, table, q1, cs, fy, fz, 0, 2)

    def second(l):
        q_prev = read(low_q1, l, 1)
        f_prev = limited(q_prev, speed(cs, l, 0, 1), swap(q_prev))
        for w in range(2):
            q = read(q1, l, w)
            f = limited(q, speed(cs, l, 0, w + 2), swap(jnp.where(upper(), q_prev, q)))
            new = q - f + swap(jnp.where(upper(), f_prev, f)) + cross(table, l, fy, fz, w)
            q2[l, :, span(w)] = flat(new)
            q_prev, f_prev = q, f

    finish(count, second, q2, sym, out, up, down)


def upper_half(scal, table, spectra, courant, low, high, sym):
    capacity = spectra.shape[0]
    held = pltpu.VMEM((capacity, PACKED, HALF), F32)
    return pl.pallas_call(
        upper_kernel,
        in_specs=[SMEM, SMEM] + [VMEM] * 5,
        out_specs=[VMEM] * 6,
        out_shape=[
            jax.ShapeDtypeStruct((capacity, PACKED, HALF), F32),
            jax.ShapeDtypeStruct((capacity, 24, HALF), F32),
            jax.ShapeDtypeStruct((capacity, PACKED, LANES), F32),
            jax.ShapeDtypeStruct((capacity, BINS, HALF), F32),
            jax.ShapeDtypeStruct((RUN, BINS, HALF), F32),
            jax.ShapeDtypeStruct((RUN, BINS, HALF), F32),
        ],
        scratch_shapes=[
            pltpu.VMEM((capacity, PACKED, CELLS), F32),
            pltpu.VMEM((capacity, 24, CELLS), F32),
            held,
            held,
            held,
            held,
        ],
        compiler_params=params(48),
        cost_estimate=pl.CostEstimate(flops=8 * 10**9, bytes_accessed=20 * 10**6, transcendentals=0),
    )(scal, table, spectra, courant, low, high, sym)


def lower_kernel(scal, table, q1_in, cs, side, below, above, sym, out, up, down, q1, fy, fz, fx, q2):
    count = scal[MID1] - scal[MID0]

    def fix(l, _):
        position = lax.rem(l, RUN)
        ux, _, _ = neighbours(table, l)
        q1[l] = q1_in[l]

        def remote(face):
            fx[l] = face[position]
            flux = view(face[RUN + position // 2])
            flux = jnp.where(upper(), 0.0, jnp.where(lax.rem(position, 2) == 0, flux, swap(flux)))
            q1[l, :, span(0)] += flat(flux)

        @pl.when(ux < 0)
        def _():
            remote(below)

        @pl.when(ux >= count)
        def _():
            remote(above)

        @pl.when((ux >= 0) & (ux < count))
        def _():
            fx[l] = side[ux]

        return 0

    lax.fori_loop(0, count, fix, 0)
    cross_flux(count, table, q1, cs, fy, fz, 0, 0)

    def second(l):
        face = view(fx[l])
        q = read(q1, l, 0)
        f = limited(q, speed(cs, l, 0, 0), jnp.where(upper(), swap(q), face))
        q2[l, :, span(0)] = flat(q - f + swap(jnp.where(upper(), face, f)) + cross(table, l, fy, fz, 0))
        q_prev, f_prev = q, f
        q = read(q1, l, 1)
        f = limited(q, speed(cs, l, 0, 1), swap(jnp.where(upper(), q_prev, q)))
        q2[l, :, span(1)] = flat(q - f + swap(jnp.where(upper(), f_prev, f)) + cross(table, l, fy, fz, 1))

    finish(count, second, q2, sym, out, up, down)


def lower_half(scal, table, q1, cs, side, below, above, sym):
    capacity = q1.shape[0]
    sent = jax.ShapeDtypeStruct((RUN, BINS, HALF), F32)
    held = pltpu.VMEM((capacity, PACKED, HALF), F32)
    return pl.pallas_call(
        lower_kernel,
        in_specs=[SMEM, SMEM] + [VMEM] * 6,
        out_specs=[VMEM] * 3,
        out_shape=[jax.ShapeDtypeStruct((capacity, BINS, HALF), F32), sent, sent],
        scratch_shapes=[held, held, held, pltpu.VMEM((capacity, PACKED, LANES), F32), held],
        compiler_params=params(48),
        cost_estimate=pl.CostEstimate(flops=8 * 10**9, bytes_accessed=20 * 10**6, transcendentals=0),
    )(scal, table, q1, cs, side, below, above, sym)


def place_kernel(scal, own_u, low_u, high_u, own_l, low_l, high_l, out):
    start, end = scal[MID0], scal[MID1]
    count = scal[NEW1] - scal[NEW0]

    def body(s, _):
        block = scal[NEW0] + s
        live = s < count

        def put(lower, upper_, i):
            out[s, :, 0:HALF] = lower[i]
            out[s, :, HALF:CELLS] = upper_[i]

        @pl.when(live & (block >= start) & (block < end))
        def _():
            put(own_l, own_u, block - start)

        @pl.when(live & (block < start))
        def _():
            put(low_l, low_u, block - start + RUN)

        @pl.when(live & (block >= end))
        def _():
            put(high_l, high_u, block - end)

        @pl.when(jnp.logical_not(live))
        def _():
            out[s] = jnp.zeros((BINS, CELLS), F32)

        return 0

    lax.fori_loop(0, out.shape[0], body, 0)


def place(scal, *pieces):
    capacity = pieces[0].shape[0]
    return pl.pallas_call(
        place_kernel,
        in_specs=[SMEM] + [VMEM] * 6,
        out_specs=VMEM,
        out_shape=jax.ShapeDtypeStruct((capacity, BINS, CELLS), F32),
        compiler_params=params(32),
    )(scal, *pieces)


def bounds(device, devices, old_count, new_count):
    ids = jnp.arange(devices, dtype=jnp.int32)
    counts = jnp.stack([old_count, new_count])

    def start(p):
        old, new = jnp.sum(jnp.where(ids < p, counts, 0), axis=1)
        least = (jnp.maximum(old, new) - RUN + RUN - 1 + RUN) // RUN * RUN - RUN
        most = (jnp.minimum(old, new) + RUN) // RUN * RUN
        return old, jnp.clip(2 * RUN * p, least, most), new

    old0, mid0, new0 = start(device)
    old1, mid1, new1 = start(device + 1)
    return jnp.stack([old0, old1, mid0, mid1, new0, new1]).astype(jnp.int32)


def on_device(devices, spectra, courant, kernel, old_count, new_count, upwind):
    device = lax.axis_index("blocks").astype(jnp.int32)
    rise = [(i, i + 1) for i in range(devices - 1)]
    fall = [(i + 1, i) for i in range(devices - 1)]
    around = [(i, (i + 1) % devices) for i in range(devices)]
    reverse = [(j, i) for i, j in around]

    def move(block, route):
        return lax.ppermute(block, "blocks", route)

    tail_start = lax.dynamic_slice(old_count, (device,), (1,)) - RUN
    tail, head = pack(spectra, courant, tail_start)
    low, high = move(tail, rise), move(head, fall)
    scal = bounds(device, devices, old_count, new_count)
    table = upwind[RUN : 2 * RUN].reshape(-1)
    sym = symmetric_kernel(kernel)
    up, down = faces(scal, table, spectra, courant, low, high)
    below, above = move(up, around), move(down, reverse)
    q1, cs, side, own_u, up_u, down_u = upper_half(scal, table, spectra, courant, low, high, sym)
    low_u, high_u = move(up_u, rise), move(down_u, fall)
    own_l, up_l, down_l = lower_half(scal, table, q1, cs, side, below, above, sym)
    low_l, high_l = move(up_l, rise), move(down_l, fall)
    return place(scal, own_u, low_u, high_u, own_l, low_l, high_l)


def solution(mesh):
    in_specs = (P("blocks", None, None), P("blocks", None, None), P(), P(), P(), P())
    out_specs = P("blocks", None, None)
    return jax.shard_map(
        functools.partial(on_device, mesh.shape["blocks"]),
        mesh=mesh,
        in_specs=in_specs,
        out_specs=out_specs,
        check_vma=False,
    )
```

```python
import functools

import jax
import jax.numpy as jnp
import numpy as np
from jax import lax
from jax.experimental import pallas as pl
from jax.experimental.pallas import tpu as pltpu
from jax.sharding import PartitionSpec as P

RUN = 12
BINS = 66
CELLS = 512
HALF = 256
LANES = 128
PACKED = 72
FULL = 64
TERMS = 2304
GROUPS = 9
FACES = 18
F32 = jnp.float32
VMEM = pl.BlockSpec(memory_space=pltpu.VMEM)
SMEM = pl.BlockSpec(memory_space=pltpu.SMEM)
OLD0, OLD1, MID0, MID1, NEW0, NEW1, HERE0, HERE1 = range(8)
ANY = pl.BlockSpec(memory_space=pl.ANY)


def params(mib):
    return pltpu.CompilerParams(vmem_limit_bytes=mib * 2**20)


def lanes():
    return lax.broadcasted_iota(jnp.int32, (8, LANES), 1)


def span(v):
    return slice(v * LANES, (v + 1) * LANES)


def upper():
    return lanes() >= 64


def last_y():
    return lanes() // 8 % 8 == 7


def last_z():
    return lanes() % 8 == 7


def view(x):
    return x.reshape(GROUPS, 8, LANES)


def flat(x):
    return x.reshape(PACKED, LANES)


def swap(x):
    return pltpu.roll(flat(x), 64, 1).reshape(x.shape)


def permuted(x, source):
    return view(jnp.take_along_axis(flat(x), source, axis=1))


def wide_lanes():
    return lax.broadcasted_iota(jnp.int32, (PACKED, LANES), 1)


def step_y(x):
    at = wide_lanes()
    return permuted(x, jnp.where(at // 8 % 8 == 0, at + 56, at - 8))


def step_z(x):
    at = wide_lanes()
    return permuted(x, jnp.where(at % 8 == 0, at + 7, at - 1))


def minmod(a, e):
    return jnp.maximum(jnp.minimum(a, e), 0.0) + jnp.minimum(jnp.maximum(a, e), 0.0)


def limited(q, c, before):
    return c * (q + (0.5 * (1.0 - c)) * minmod(q - before, q))


def upwind_of(table, position):
    back = table[3 * position] < RUN + position
    return back, table[3 * position + 1] - RUN, table[3 * position + 2] - RUN


def read(ref, l, v):
    return view(ref[l, :, span(v)])


def speed(ref, l, d, v):
    return ref[l, 8 * d : 8 * d + 8, span(v)]


def donor(q0, cs, l, v, q_prev, cx_prev, uy, uz):
    q, cx, cy, cz = read(q0, l, v), speed(cs, l, 0, v), speed(cs, l, 1, v), speed(cs, l, 2, v)
    up, ly, lz = upper(), last_y(), last_z()
    in_x = swap(jnp.where(up, 0.0 if q_prev is None else cx_prev * q_prev, cx * q))
    in_y = step_y(jnp.where(ly, speed(cs, uy, 1, v), cy) * jnp.where(ly, read(q0, uy, v), q))
    in_z = step_z(jnp.where(lz, speed(cs, uz, 2, v), cz) * jnp.where(lz, read(q0, uz, v), q))
    return (1.0 - (cx + cy + cz)) * q + in_x + in_y + in_z


def fetch(block, scal, spectra, courant, low, high, q_dst, c_dst, at):
    own0, own1 = scal[OLD0], scal[OLD1]

    def spread(ref, i, row):
        for d in range(3):
            c_dst[at, 8 * d : 8 * d + 8] = jnp.broadcast_to(
                ref[i, row + d : row + d + 1], (8,) + ref.shape[2:]
            )

    def owned():
        q_dst[at, 0:BINS] = spectra[block - own0]
        spread(courant, block - own0, 0)

    if low is None:
        owned()
        return
    pl.when((block >= own0) & (block < own1))(owned)

    def received(ref, i):
        q_dst[at] = ref[i]
        spread(ref, i, BINS)

    @pl.when(block < own0)
    def _():
        received(low, block - own0 + RUN)

    @pl.when(block >= own1)
    def _():
        received(high, block - own1)


def pack_kernel(old_count, device, spectra, courant, up, down, raw, speeds, joined, in_sems, out_sems):
    tail = old_count[device[0]] - RUN
    copies = []
    for side, start in ((0, tail), (1, 0)):
        copies.append(pltpu.make_async_copy(courant.at[pl.ds(start, RUN)], speeds.at[side], in_sems.at[side, RUN]))
        copies[-1].start()
    waits, sends = [], []
    for k in range(0, RUN, 2):
        for side, start, out in ((0, tail, up), (1, 0, down)):
            here = pl.ds(k, 2)
            copy = pltpu.make_async_copy(spectra.at[pl.ds(start + k, 2)], raw.at[side, here], in_sems.at[side, k])
            copy.start()
            waits.append((side, k, copy))
            sends.append(pltpu.make_async_copy(joined.at[side, here], out.at[here], out_sems.at[side, k]))
    for copy in copies:
        copy.wait()
    for (side, k, copy), send in zip(waits, sends):
        copy.wait()
        for i in (k, k + 1):
            joined[side, i, 0:BINS] = raw[side, i]
            joined[side, i, BINS : BINS + 3] = speeds[side, i]
        send.start()
    for send in sends:
        send.wait()


def pack(old_count, device, spectra, courant):
    sent = jax.ShapeDtypeStruct((RUN, PACKED, CELLS), F32)
    return pl.pallas_call(
        pack_kernel,
        in_specs=[SMEM, SMEM, ANY, ANY],
        out_specs=[ANY, ANY],
        out_shape=[sent, sent],
        scratch_shapes=[
            pltpu.VMEM((2, RUN, BINS, CELLS), F32),
            pltpu.VMEM((2, RUN, 3, CELLS), F32),
            pltpu.VMEM((2, RUN, PACKED, CELLS), F32),
            pltpu.SemaphoreType.DMA((2, RUN + 1)),
            pltpu.SemaphoreType.DMA((2, RUN)),
        ],
        compiler_params=params(56),
    )(old_count, device, spectra, courant)


def face_kernel(scal, table, spectra, courant, low, high, up, down, q0, cs):
    count = scal[MID1] - scal[MID0]

    def gather(j, _):
        first = scal[MID0] + jnp.where(j < RUN, j, count - 2 * RUN + j)
        fetch(first, scal, spectra, courant, low, high, q0, cs, j)
        return 0

    lax.fori_loop(0, 2 * RUN, gather, 0)

    def face(j, position):
        _, y, z = upwind_of(table, position)
        uy, uz = y + (j - position), z + (j - position)
        q1 = donor(q0, cs, j, 1, read(q0, j, 0), speed(cs, j, 0, 0), uy, uz)
        other = swap(q1)
        c = speed(cs, j, 0, 1)
        return jnp.where(upper(), limited(q1, c, other), other), c * read(q0, j, 1)

    for base, out in ((0, down), (RUN, up)):

        def pair(i, _, base=base, out=out):
            a0, b0 = face(base + 2 * i, 2 * i)
            a1, b1 = face(base + 2 * i + 1, 2 * i + 1)
            out[2 * i] = flat(a0)
            out[2 * i + 1] = flat(a1)
            out[RUN + i] = flat(jnp.where(upper(), b1, swap(b0)))
            return 0

        lax.fori_loop(0, RUN // 2, pair, 0)


def faces(scal, table, spectra, courant, low, high):
    capacity = spectra.shape[0]

    def half(*dims):
        return pl.BlockSpec(dims + (HALF,), lambda i: (0, 0, 1))

    return pl.pallas_call(
        face_kernel,
        grid=(1,),
        in_specs=[
            SMEM,
            SMEM,
            half(capacity, BINS),
            half(capacity, 3),
            half(RUN, PACKED),
            half(RUN, PACKED),
        ],
        out_specs=[VMEM] * 2,
        out_shape=[jax.ShapeDtypeStruct((FACES, PACKED, LANES), F32)] * 2,
        scratch_shapes=[pltpu.VMEM((2 * RUN, PACKED, HALF), F32), pltpu.VMEM((2 * RUN, 24, HALF), F32)],
        compiler_params=params(24),
    )(scal, table, spectra, courant, low, high)


def pair_terms(q):
    wide = q.shape[1]
    group = [q[8 * g : 8 * g + 8, :] for g in range(8)]
    row = [jnp.broadcast_to(q[i : i + 1, :], (8, wide)) for i in range(BINS)]
    out = [row[i] * group[g] for i in range(56) for g in range(i // 8 + 1, 8)]
    out += [row[i] * group[g] for i in (64, 65) for g in range(8)]
    for s in range(5):
        out += [x * (pltpu.roll(x, s, 0) if s else x) for x in group]
    at = lax.broadcasted_iota(jnp.int32, (8, wide), 0)
    rest = jnp.where(at < 2, row[64], row[65]) * jnp.where(at < 1, row[64], row[65])
    out.append(jnp.where(at < 3, rest, 0.0))
    return out + [jnp.zeros((8, wide), F32)] * (TERMS // 8 - len(out))


def pair_columns():
    pairs = [(i, j) for i in range(56) for j in range(i // 8 * 8 + 8, FULL)]
    pairs += [(i, j) for i in (64, 65) for j in range(FULL)]
    for s in range(5):
        for g in range(0, FULL, 8):
            pairs += [(g + r, g + (r - s) % 8) if s < 4 or r < 4 else None for r in range(8)]
    pairs += [(64, 64), (64, 65), (65, 65)]
    pairs += [None] * (TERMS - len(pairs))
    one = [p[0] * BINS + p[1] if p else -1 for p in pairs]
    two = [p[1] * BINS + p[0] if p and p[0] != p[1] else -1 for p in pairs]
    return np.array([one, two], np.int32)


def symmetric_kernel_body(columns, kernel, out):
    width = out.shape[1]
    one, two = columns[0:1], columns[1:2]
    picks = []
    for base in range(0, kernel.shape[1], 256):
        row = lax.broadcasted_iota(jnp.int32, (256, width), 0) + base
        picks.append(jnp.where((row == one) | (row == two), 1.0, 0.0).astype(jnp.bfloat16))
    total = jnp.dot(kernel[...], jnp.concatenate(picks, axis=0), preferred_element_type=F32)
    out[...] = total.astype(jnp.bfloat16)


def symmetric_kernel(kernel):
    wide = -(-kernel.shape[1] // 256) * 256
    padded = jnp.pad(kernel, ((0, 80 - BINS), (0, wide - kernel.shape[1])))
    return pl.pallas_call(
        symmetric_kernel_body,
        grid=(TERMS // 256,),
        in_specs=[
            pl.BlockSpec((2, 256), lambda i: (0, i)),
            pl.BlockSpec((80, wide), lambda i: (0, 0)),
        ],
        out_specs=pl.BlockSpec((80, 256), lambda i: (0, i)),
        out_shape=jax.ShapeDtypeStruct((80, TERMS), jnp.bfloat16),
        compiler_params=params(16),
        cost_estimate=pl.CostEstimate(flops=2 * 10**9, bytes_accessed=10**6, transcendentals=0),
    )(jnp.asarray(pair_columns()), padded)


def coalesce(q, sym):
    terms = pair_terms(q)
    packed = [
        jnp.concatenate(terms[2 * r : 2 * r + 2], axis=0).astype(jnp.bfloat16) for r in range(TERMS // 16)
    ]
    gained = jnp.dot(sym[...], jnp.concatenate(packed, axis=0), preferred_element_type=F32)
    return q + gained[0:PACKED]


def neighbours(table, l):
    position = lax.rem(l, RUN)
    back, y, z = upwind_of(table, position)
    return jnp.where(back, l - RUN, l + RUN), y + (l - position), z + (l - position)


def cross_flux(count, block_at, table, q1, cs, fy, fz, v0, vf):
    def cross_body(i, _):
        l = block_at(i)
        _, uy, uz = neighbours(table, l)
        for w in range(2):
            q = read(q1, l, v0 + w)
            before_y = step_y(jnp.where(last_y(), read(q1, uy, v0 + w), q))
            before_z = step_z(jnp.where(last_z(), read(q1, uz, v0 + w), q))
            fy[l, :, span(w)] = flat(limited(q, speed(cs, l, 1, vf + w), before_y))
            fz[l, :, span(w)] = flat(limited(q, speed(cs, l, 2, vf + w), before_z))
        return 0

    lax.fori_loop(0, count, cross_body, 0)


def cross(table, l, fy, fz, w):
    _, uy, uz = neighbours(table, l)
    y_own, z_own = read(fy, l, w), read(fz, l, w)
    y_in = step_y(jnp.where(last_y(), read(fy, uy, w), y_own))
    z_in = step_z(jnp.where(last_z(), read(fz, uz, w), z_own))
    return (y_in - y_own) + (z_in - z_own)


def coalesce_all(count, block_at, second, q2, sym, out):
    def third(i, _):
        l = block_at(i)
        out[l, :, 0:HALF] = coalesce(q2[l], sym)[0:BINS]
        second(block_at(jnp.minimum(i + 1, count - 1)))
        return 0

    @pl.when(count > 0)
    def _():
        second(block_at(0))

    lax.fori_loop(0, count, third, 0)


def upper_kernel(received, scal, table, spectra, courant, sym, *rest):
    low, high = rest[:2] if received else (None, None)
    low_q1, low_c, face, out, q0, cs, q1, fy, fz, q2 = rest[2 if received else 0 :]
    here0, here = scal[HERE0], scal[HERE1] - scal[HERE0]
    count = scal[MID1] - scal[MID0] - here if received else here

    def block_at(i):
        return i + jnp.where(i >= here0, here, 0) if received else i + here0

    def gather(i, _):
        l = block_at(i)
        fetch(scal[MID0] + l, scal, spectra, courant, low, high, q0, cs, l)
        low_c[l] = cs[l, :, 0:HALF]
        return 0

    lax.fori_loop(0, count, gather, 0)

    def first(i, _):
        l = block_at(i)
        _, uy, uz = neighbours(table, l)
        q_prev = cx_prev = None
        for v in range(4):
            new = donor(q0, cs, l, v, q_prev, cx_prev, uy, uz)
            q_prev, cx_prev = read(q0, l, v), speed(cs, l, 0, v)
            if v < 2:
                low_q1[l, :, span(v)] = flat(new)
            else:
                q1[l, :, span(v - 2)] = flat(new)
        other = swap(new)
        face[l, 0:PACKED] = flat(jnp.where(upper(), limited(new, cx_prev, other), other))
        face[l, PACKED : 2 * PACKED] = flat(cx_prev * q_prev)
        return 0

    lax.fori_loop(0, count, first, 0)
    cross_flux(count, block_at, table, q1, cs, fy, fz, 0, 2)

    def second(l):
        q_prev = read(low_q1, l, 1)
        f_prev = limited(q_prev, speed(cs, l, 0, 1), swap(q_prev))
        for w in range(2):
            q = read(q1, l, w)
            f = limited(q, speed(cs, l, 0, w + 2), swap(jnp.where(upper(), q_prev, q)))
            new = q - f + swap(jnp.where(upper(), f_prev, f)) + cross(table, l, fy, fz, w)
            q2[l, :, span(w)] = flat(new)
            q_prev, f_prev = q, f

    coalesce_all(count, block_at, second, q2, sym, out)


def upper_half(scal, table, spectra, courant, sym, *moved):
    capacity = spectra.shape[0]
    held = pltpu.VMEM((capacity, PACKED, HALF), F32)
    return pl.pallas_call(
        functools.partial(upper_kernel, bool(moved)),
        in_specs=[SMEM, SMEM] + [VMEM] * (3 + len(moved)),
        out_specs=[VMEM] * 4,
        out_shape=[
            jax.ShapeDtypeStruct((capacity, PACKED, HALF), F32),
            jax.ShapeDtypeStruct((capacity, 24, HALF), F32),
            jax.ShapeDtypeStruct((capacity, 2 * PACKED, LANES), F32),
            jax.ShapeDtypeStruct((capacity, BINS, HALF), F32),
        ],
        scratch_shapes=[
            pltpu.VMEM((capacity, PACKED, CELLS), F32),
            pltpu.VMEM((capacity, 24, CELLS), F32),
            held,
            held,
            held,
            held,
        ],
        compiler_params=params(48),
        cost_estimate=pl.CostEstimate(flops=4 * 10**9, bytes_accessed=20 * 10**6, transcendentals=0),
    )(scal, table, spectra, courant, sym, *moved)


def lower_kernel(scal, table, *rest):
    early, late = rest[0:4], rest[4:8]
    below, above, sym, own, up, down, q1, cs, fy, fz, fx, q2 = rest[8:]
    count = scal[MID1] - scal[MID0]

    def choose(l, take):
        was_here = (l >= scal[HERE0]) & (l < scal[HERE1])
        pl.when(was_here)(functools.partial(take, *early))
        pl.when(jnp.logical_not(was_here))(functools.partial(take, *late))

    def fix(l, _):
        position = lax.rem(l, RUN)
        ux, _, _ = neighbours(table, l)

        def take(low_q1, low_c, face, out):
            q1[l] = low_q1[l]
            cs[l] = low_c[l]
            own[l, :, HALF:CELLS] = out[l]

        choose(l, take)

        def add_flux(flux):
            q1[l, :, span(0)] += flat(jnp.where(upper(), 0.0, flux))

        def remote(face):
            fx[l] = face[position]
            flux = view(face[RUN + position // 2])
            add_flux(jnp.where(lax.rem(position, 2) == 0, flux, swap(flux)))

        @pl.when(ux < 0)
        def _():
            remote(below)

        @pl.when(ux >= count)
        def _():
            remote(above)

        @pl.when((ux >= 0) & (ux < count))
        def _():
            def take_face(low_q1, low_c, face, out):
                fx[l] = face[ux, 0:PACKED]
                add_flux(swap(view(face[ux, PACKED : 2 * PACKED])))

            choose(ux, take_face)

        return 0

    lax.fori_loop(0, count, fix, 0)
    cross_flux(count, lambda i: i, table, q1, cs, fy, fz, 0, 0)

    def second(l):
        face = view(fx[l])
        q = read(q1, l, 0)
        f = limited(q, speed(cs, l, 0, 0), jnp.where(upper(), swap(q), face))
        q2[l, :, span(0)] = flat(q - f + swap(jnp.where(upper(), face, f)) + cross(table, l, fy, fz, 0))
        q_prev, f_prev = q, f
        q = read(q1, l, 1)
        f = limited(q, speed(cs, l, 0, 1), swap(jnp.where(upper(), q_prev, q)))
        q2[l, :, span(1)] = flat(q - f + swap(jnp.where(upper(), f_prev, f)) + cross(table, l, fy, fz, 1))

    coalesce_all(count, lambda i: i, second, q2, sym, own)

    def hand_on(k, _):
        down[k] = own[k]
        up[k] = own[count - RUN + k]
        return 0

    lax.fori_loop(0, RUN, hand_on, 0)


def lower_half(scal, table, early, late, below, above, sym):
    capacity = early[0].shape[0]
    sent = jax.ShapeDtypeStruct((RUN, BINS, CELLS), F32)
    held = pltpu.VMEM((capacity, PACKED, HALF), F32)
    return pl.pallas_call(
        lower_kernel,
        in_specs=[SMEM, SMEM] + [VMEM] * 11,
        out_specs=[VMEM] * 3,
        out_shape=[jax.ShapeDtypeStruct((capacity, BINS, CELLS), F32), sent, sent],
        scratch_shapes=[
            held,
            pltpu.VMEM((capacity, 24, HALF), F32),
            held,
            held,
            pltpu.VMEM((capacity, PACKED, LANES), F32),
            held,
        ],
        compiler_params=params(52),
        cost_estimate=pl.CostEstimate(flops=8 * 10**9, bytes_accessed=20 * 10**6, transcendentals=0),
    )(scal, table, *early, *late, below, above, sym)


def place_own_kernel(scal, own, out):
    start, end = scal[MID0], scal[MID1]
    count = scal[NEW1] - scal[NEW0]

    def body(s, _):
        block = scal[NEW0] + s
        mine = (s < count) & (block >= start) & (block < end)

        @pl.when(mine)
        def _():
            out[s] = own[block - start]

        @pl.when(jnp.logical_not(mine))
        def _():
            out[s] = jnp.zeros((BINS, CELLS), F32)

        return 0

    lax.fori_loop(0, out.shape[0], body, 0)


def place_own(scal, own):
    return pl.pallas_call(
        place_own_kernel,
        in_specs=[SMEM, VMEM],
        out_specs=VMEM,
        out_shape=own,
        compiler_params=params(24),
        cost_estimate=pl.CostEstimate(flops=10**6, bytes_accessed=11 * 10**6, transcendentals=0),
    )(scal, own)


def place_moved_kernel(scal, low, high, _, out, sems):
    first, end = scal[NEW0], scal[NEW1]

    def copies(act):
        for k in range(RUN):
            block = scal[MID0] - RUN + k

            @pl.when((block >= first) & (block < end))
            def _(k=k, block=block):
                act(pltpu.make_async_copy(low.at[k], out.at[block - first], sems.at[0, k]))

            above = scal[MID1] + k

            @pl.when((above >= first) & (above < end))
            def _(k=k, above=above):
                act(pltpu.make_async_copy(high.at[k], out.at[above - first], sems.at[1, k]))

    copies(lambda copy: copy.start())
    copies(lambda copy: copy.wait())


def place_moved(scal, low, high, out):
    return pl.pallas_call(
        place_moved_kernel,
        in_specs=[SMEM, ANY, ANY, ANY],
        out_specs=ANY,
        out_shape=jax.ShapeDtypeStruct(out.shape, F32),
        scratch_shapes=[pltpu.SemaphoreType.DMA((2, RUN))],
        input_output_aliases={3: 0},
        compiler_params=params(56),
    )(scal, low, high, out)


def bounds_kernel(device, old_count, new_count, out):
    ids = lax.broadcasted_iota(jnp.int32, old_count.shape, 1)

    def total(counts, p):
        return jnp.sum(jnp.where(ids < p, counts[...], 0).astype(F32)).astype(jnp.int32)

    def start(p):
        old, new = total(old_count, p), total(new_count, p)
        least = lax.div(jnp.maximum(old, new) + RUN - 1, RUN) * RUN - RUN
        most = lax.div(jnp.minimum(old, new), RUN) * RUN + RUN
        return old, jnp.clip(2 * RUN * p, least, most), new

    old0, mid0, new0 = start(device[0])
    old1, mid1, new1 = start(device[0] + 1)
    out[OLD0], out[OLD1], out[MID0], out[MID1], out[NEW0], out[NEW1] = old0, old1, mid0, mid1, new0, new1
    here0 = lax.div(jnp.maximum(old0 - mid0, 0) + RUN - 1, RUN) * RUN
    here1 = lax.div(jnp.minimum(old1, mid1) - mid0, RUN) * RUN
    out[HERE0], out[HERE1] = here0, jnp.maximum(here0, here1)


def bounds(device, old_count, new_count):
    return pl.pallas_call(
        bounds_kernel,
        in_specs=[SMEM, VMEM, VMEM],
        out_specs=SMEM,
        out_shape=jax.ShapeDtypeStruct((8,), jnp.int32),
    )(device, old_count.reshape(1, -1), new_count.reshape(1, -1))


def on_device(devices, spectra, courant, kernel, old_count, new_count, upwind):
    device = lax.axis_index("blocks").astype(jnp.int32).reshape(1)
    rise = [(i, i + 1) for i in range(devices - 1)]
    fall = [(i + 1, i) for i in range(devices - 1)]
    around = [(i, (i + 1) % devices) for i in range(devices)]
    reverse = [(j, i) for i, j in around]

    def move(block, route):
        return lax.ppermute(block, "blocks", route)

    tail, head = pack(old_count, device, spectra, courant)
    low, high = move(tail, rise), move(head, fall)
    scal = bounds(device, old_count, new_count)
    table = upwind[RUN : 2 * RUN].reshape(-1)
    sym = symmetric_kernel(kernel)
    early = upper_half(scal, table, spectra, courant, sym)
    up, down = faces(scal, table, spectra, courant, low, high)
    below, above = move(up, around), move(down, reverse)
    late = upper_half(scal, table, spectra, courant, sym, low, high)
    own, up, down = lower_half(scal, table, early, late, below, above, sym)
    low, high = move(up, rise), move(down, fall)
    return place_moved(scal, low, high, place_own(scal, own))


def solution(mesh):
    in_specs = (P("blocks", None, None), P("blocks", None, None), P(), P(), P(), P())
    out_specs = P("blocks", None, None)
    return jax.shard_map(
        functools.partial(on_device, mesh.shape["blocks"]),
        mesh=mesh,
        in_specs=in_specs,
        out_specs=out_specs,
        check_vma=False,
    )
```

```python
import functools

import jax
import jax.numpy as jnp
import numpy as np
from jax import lax
from jax.experimental import pallas as pl
from jax.experimental.pallas import tpu as pltpu
from jax.sharding import PartitionSpec as P

RUN = 12
BINS = 66
CELLS = 512
HALF = 256
LANES = 128
PACKED = 72
FULL = 64
TERMS = 2304
GROUPS = 9
FACES = 18
F32 = jnp.float32
VMEM = pl.BlockSpec(memory_space=pltpu.VMEM)
SMEM = pl.BlockSpec(memory_space=pltpu.SMEM)
OLD0, OLD1, MID0, MID1, NEW0, NEW1, HERE0, HERE1 = range(8)
ANY = pl.BlockSpec(memory_space=pl.ANY)


def params(mib):
    return pltpu.CompilerParams(vmem_limit_bytes=mib * 2**20)


def lanes():
    return lax.broadcasted_iota(jnp.int32, (8, LANES), 1)


def span(v):
    return slice(v * LANES, (v + 1) * LANES)


def upper():
    return lanes() >= 64


def last_y():
    return lanes() // 8 % 8 == 7


def last_z():
    return lanes() % 8 == 7


def view(x):
    return x.reshape(GROUPS, 8, LANES)


def flat(x):
    return x.reshape(PACKED, LANES)


def swap(x):
    return pltpu.roll(flat(x), 64, 1).reshape(x.shape)


def permuted(x, source):
    return view(jnp.take_along_axis(flat(x), source, axis=1))


def wide_lanes():
    return lax.broadcasted_iota(jnp.int32, (PACKED, LANES), 1)


def step_y(x):
    at = wide_lanes()
    return permuted(x, jnp.where(at // 8 % 8 == 0, at + 56, at - 8))


def step_z(x):
    at = wide_lanes()
    return permuted(x, jnp.where(at % 8 == 0, at + 7, at - 1))


def minmod(a, e):
    return jnp.maximum(jnp.minimum(a, e), 0.0) + jnp.minimum(jnp.maximum(a, e), 0.0)


def limited(q, c, before):
    return c * (q + (0.5 * (1.0 - c)) * minmod(q - before, q))


def upwind_of(table, position):
    back = table[3 * position] < RUN + position
    return back, table[3 * position + 1] - RUN, table[3 * position + 2] - RUN


def read(ref, l, v):
    return view(ref[l, :, span(v)])


def speed(ref, l, d, v):
    return ref[l, 8 * d : 8 * d + 8, span(v)]


def donor(q0, cs, l, v, q_prev, cx_prev, uy, uz):
    q, cx, cy, cz = read(q0, l, v), speed(cs, l, 0, v), speed(cs, l, 1, v), speed(cs, l, 2, v)
    up, ly, lz = upper(), last_y(), last_z()
    in_x = swap(jnp.where(up, 0.0 if q_prev is None else cx_prev * q_prev, cx * q))
    in_y = step_y(jnp.where(ly, speed(cs, uy, 1, v), cy) * jnp.where(ly, read(q0, uy, v), q))
    in_z = step_z(jnp.where(lz, speed(cs, uz, 2, v), cz) * jnp.where(lz, read(q0, uz, v), q))
    return (1.0 - (cx + cy + cz)) * q + in_x + in_y + in_z


def fetch(block, scal, spectra, courant, low, high, q_dst, c_dst, at):
    own0, own1 = scal[OLD0], scal[OLD1]

    def spread(ref, i, row):
        for d in range(3):
            c_dst[at, 8 * d : 8 * d + 8] = jnp.broadcast_to(
                ref[i, row + d : row + d + 1], (8,) + ref.shape[2:]
            )

    def owned():
        q_dst[at, 0:BINS] = spectra[block - own0]
        spread(courant, block - own0, 0)

    if low is None:
        owned()
        return
    pl.when((block >= own0) & (block < own1))(owned)

    def received(ref, i):
        q_dst[at] = ref[i]
        spread(ref, i, BINS)

    @pl.when(block < own0)
    def _():
        received(low, block - own0 + RUN)

    @pl.when(block >= own1)
    def _():
        received(high, block - own1)


def pack_kernel(old_count, device, spectra, courant, up, down, raw, speeds, joined, in_sems, out_sems):
    tail = old_count[device[0]] - RUN
    copies = []
    for side, start in ((0, tail), (1, 0)):
        copies.append(pltpu.make_async_copy(courant.at[pl.ds(start, RUN)], speeds.at[side], in_sems.at[side, RUN]))
        copies[-1].start()
    waits, sends = [], []
    for k in range(0, RUN, 2):
        for side, start, out in ((0, tail, up), (1, 0, down)):
            here = pl.ds(k, 2)
            copy = pltpu.make_async_copy(spectra.at[pl.ds(start + k, 2)], raw.at[side, here], in_sems.at[side, k])
            copy.start()
            waits.append((side, k, copy))
            sends.append(pltpu.make_async_copy(joined.at[side, here], out.at[here], out_sems.at[side, k]))
    for copy in copies:
        copy.wait()
    for (side, k, copy), send in zip(waits, sends):
        copy.wait()
        for i in (k, k + 1):
            joined[side, i, 0:BINS] = raw[side, i]
            joined[side, i, BINS : BINS + 3] = speeds[side, i]
        send.start()
    for send in sends:
        send.wait()


def pack(old_count, device, spectra, courant):
    sent = jax.ShapeDtypeStruct((RUN, PACKED, CELLS), F32)
    return pl.pallas_call(
        pack_kernel,
        in_specs=[SMEM, SMEM, ANY, ANY],
        out_specs=[ANY, ANY],
        out_shape=[sent, sent],
        scratch_shapes=[
            pltpu.VMEM((2, RUN, BINS, CELLS), F32),
            pltpu.VMEM((2, RUN, 3, CELLS), F32),
            pltpu.VMEM((2, RUN, PACKED, CELLS), F32),
            pltpu.SemaphoreType.DMA((2, RUN + 1)),
            pltpu.SemaphoreType.DMA((2, RUN)),
        ],
        compiler_params=params(56),
    )(old_count, device, spectra, courant)


def face_kernel(scal, table, spectra, courant, low, high, up, down, q0, cs):
    count = scal[MID1] - scal[MID0]

    def gather(j, _):
        first = scal[MID0] + jnp.where(j < RUN, j, count - 2 * RUN + j)
        fetch(first, scal, spectra, courant, low, high, q0, cs, j)
        return 0

    lax.fori_loop(0, 2 * RUN, gather, 0)

    def face(j, position):
        _, y, z = upwind_of(table, position)
        uy, uz = y + (j - position), z + (j - position)
        q1 = donor(q0, cs, j, 1, read(q0, j, 0), speed(cs, j, 0, 0), uy, uz)
        other = swap(q1)
        c = speed(cs, j, 0, 1)
        return jnp.where(upper(), limited(q1, c, other), other), c * read(q0, j, 1)

    for base, out in ((0, down), (RUN, up)):

        def pair(i, _, base=base, out=out):
            a0, b0 = face(base + 2 * i, 2 * i)
            a1, b1 = face(base + 2 * i + 1, 2 * i + 1)
            out[2 * i] = flat(a0)
            out[2 * i + 1] = flat(a1)
            out[RUN + i] = flat(jnp.where(upper(), b1, swap(b0)))
            return 0

        lax.fori_loop(0, RUN // 2, pair, 0)


def faces(scal, table, spectra, courant, low, high):
    capacity = spectra.shape[0]

    def half(*dims):
        return pl.BlockSpec(dims + (HALF,), lambda i: (0, 0, 1))

    return pl.pallas_call(
        face_kernel,
        grid=(1,),
        in_specs=[
            SMEM,
            SMEM,
            half(capacity, BINS),
            half(capacity, 3),
            half(RUN, PACKED),
            half(RUN, PACKED),
        ],
        out_specs=[VMEM] * 2,
        out_shape=[jax.ShapeDtypeStruct((FACES, PACKED, LANES), F32)] * 2,
        scratch_shapes=[pltpu.VMEM((2 * RUN, PACKED, HALF), F32), pltpu.VMEM((2 * RUN, 24, HALF), F32)],
        compiler_params=params(24),
    )(scal, table, spectra, courant, low, high)


def pair_terms(q):
    wide = q.shape[1]
    group = [q[8 * g : 8 * g + 8, :] for g in range(8)]
    row = [jnp.broadcast_to(q[i : i + 1, :], (8, wide)) for i in range(BINS)]
    out = [row[i] * group[g] for i in range(56) for g in range(i // 8 + 1, 8)]
    out += [row[i] * group[g] for i in (64, 65) for g in range(8)]
    for s in range(5):
        out += [x * (pltpu.roll(x, s, 0) if s else x) for x in group]
    at = lax.broadcasted_iota(jnp.int32, (8, wide), 0)
    rest = jnp.where(at < 2, row[64], row[65]) * jnp.where(at < 1, row[64], row[65])
    out.append(jnp.where(at < 3, rest, 0.0))
    return out + [jnp.zeros((8, wide), F32)] * (TERMS // 8 - len(out))


def pair_columns():
    pairs = [(i, j) for i in range(56) for j in range(i // 8 * 8 + 8, FULL)]
    pairs += [(i, j) for i in (64, 65) for j in range(FULL)]
    for s in range(5):
        for g in range(0, FULL, 8):
            pairs += [(g + r, g + (r - s) % 8) if s < 4 or r < 4 else None for r in range(8)]
    pairs += [(64, 64), (64, 65), (65, 65)]
    pairs += [None] * (TERMS - len(pairs))
    one = [p[0] * BINS + p[1] if p else -1 for p in pairs]
    two = [p[1] * BINS + p[0] if p and p[0] != p[1] else -1 for p in pairs]
    return np.array([one, two], np.int32)


def symmetric_kernel_body(columns, kernel, out):
    width = out.shape[1]
    row = lax.broadcasted_iota(jnp.int32, (256, width), 0).astype(F32).astype(jnp.bfloat16)
    picks = []
    for base in range(0, kernel.shape[1], 256):
        near = jnp.clip(columns[...] - base, -1, 256).astype(F32).astype(jnp.bfloat16)
        hit = (row == near[0:1]) | (row == near[1:2])
        picks.append(jnp.where(hit, jnp.bfloat16(1), jnp.bfloat16(0)))
    total = jnp.dot(kernel[...], jnp.concatenate(picks, axis=0), preferred_element_type=F32)
    out[...] = total.astype(jnp.bfloat16)


def symmetric_kernel(kernel):
    wide = -(-kernel.shape[1] // 256) * 256
    padded = jnp.pad(kernel, ((0, 80 - BINS), (0, wide - kernel.shape[1])))
    return pl.pallas_call(
        symmetric_kernel_body,
        grid=(TERMS // 256,),
        in_specs=[
            pl.BlockSpec((2, 256), lambda i: (0, i)),
            pl.BlockSpec((80, wide), lambda i: (0, 0)),
        ],
        out_specs=pl.BlockSpec((80, 256), lambda i: (0, i)),
        out_shape=jax.ShapeDtypeStruct((80, TERMS), jnp.bfloat16),
        compiler_params=params(16),
        cost_estimate=pl.CostEstimate(flops=2 * 10**9, bytes_accessed=10**6, transcendentals=0),
    )(jnp.asarray(pair_columns()), padded)


def coalesce(q, sym):
    terms = pair_terms(q)
    packed = [
        jnp.concatenate(terms[2 * r : 2 * r + 2], axis=0).astype(jnp.bfloat16) for r in range(TERMS // 16)
    ]
    gained = jnp.dot(sym[...], jnp.concatenate(packed, axis=0), preferred_element_type=F32)
    return q + gained[0:PACKED]


def neighbours(table, l):
    position = lax.rem(l, RUN)
    back, y, z = upwind_of(table, position)
    return jnp.where(back, l - RUN, l + RUN), y + (l - position), z + (l - position)


def cross_flux(count, block_at, table, q1, cs, fy, fz, v0, vf):
    def cross_body(i, _):
        l = block_at(i)
        _, uy, uz = neighbours(table, l)
        for w in range(2):
            q = read(q1, l, v0 + w)
            before_y = step_y(jnp.where(last_y(), read(q1, uy, v0 + w), q))
            before_z = step_z(jnp.where(last_z(), read(q1, uz, v0 + w), q))
            fy[l, :, span(w)] = flat(limited(q, speed(cs, l, 1, vf + w), before_y))
            fz[l, :, span(w)] = flat(limited(q, speed(cs, l, 2, vf + w), before_z))
        return 0

    lax.fori_loop(0, count, cross_body, 0)


def cross(table, l, fy, fz, w):
    _, uy, uz = neighbours(table, l)
    y_own, z_own = read(fy, l, w), read(fz, l, w)
    y_in = step_y(jnp.where(last_y(), read(fy, uy, w), y_own))
    z_in = step_z(jnp.where(last_z(), read(fz, uz, w), z_own))
    return (y_in - y_own) + (z_in - z_own)


def upper_kernel(moved, scal, table, spectra, courant, sym, *rest):
    low, high = rest[:2] if moved else (None, None)
    to_q1, to_c, to_face, to_out, scal_out, low_q1, low_c, face, out, q0, cs, q1, fy, fz, q2, sems = rest[6 if moved else 0 :]
    for k in range(8):
        scal_out[k] = scal[k]
    here0, here = scal[HERE0], scal[HERE1] - scal[HERE0]
    count = scal[MID1] - scal[MID0] - here if moved else here

    def block_at(i):
        return i + jnp.where(i >= here0, here, 0) if moved else i + here0

    def copy(k, l):
        source, target = ((low_q1, to_q1), (low_c, to_c), (face, to_face), (out, to_out))[k]
        return pltpu.make_async_copy(source.at[l], target.at[l], sems.at[k, l])

    def gather(i, _):
        l = block_at(i)
        fetch(scal[MID0] + l, scal, spectra, courant, low, high, q0, cs, l)
        low_c[l] = cs[l, :, 0:HALF]
        copy(1, l).start()
        return 0

    lax.fori_loop(0, count, gather, 0)

    def first(i, _):
        l = block_at(i)
        _, uy, uz = neighbours(table, l)
        q_prev = cx_prev = None
        for v in range(4):
            new = donor(q0, cs, l, v, q_prev, cx_prev, uy, uz)
            q_prev, cx_prev = read(q0, l, v), speed(cs, l, 0, v)
            if v < 2:
                low_q1[l, :, span(v)] = flat(new)
            else:
                q1[l, :, span(v - 2)] = flat(new)
        other = swap(new)
        face[l, 0:PACKED] = flat(jnp.where(upper(), limited(new, cx_prev, other), other))
        face[l, PACKED : 2 * PACKED] = flat(cx_prev * q_prev)
        copy(0, l).start()
        copy(2, l).start()
        return 0

    lax.fori_loop(0, count, first, 0)
    cross_flux(count, block_at, table, q1, cs, fy, fz, 0, 2)

    def second(l):
        q_prev = read(low_q1, l, 1)
        f_prev = limited(q_prev, speed(cs, l, 0, 1), swap(q_prev))
        for w in range(2):
            q = read(q1, l, w)
            f = limited(q, speed(cs, l, 0, w + 2), swap(jnp.where(upper(), q_prev, q)))
            new = q - f + swap(jnp.where(upper(), f_prev, f)) + cross(table, l, fy, fz, w)
            q2[l, :, span(w)] = flat(new)
            q_prev, f_prev = q, f

    @pl.when(count > 0)
    def _():
        second(block_at(0))

    def third(i, _):
        l = block_at(i)
        out[l] = coalesce(q2[l], sym)[0:BINS]
        second(block_at(jnp.minimum(i + 1, count - 1)))
        copy(3, l).start()
        return 0

    lax.fori_loop(0, count, third, 0)

    def drain(i, _):
        for k in range(4):
            copy(k, block_at(i)).wait()
        return 0

    lax.fori_loop(0, count, drain, 0)


def upper_half(scal, table, spectra, courant, sym, *moved):
    capacity = spectra.shape[0]
    held = (capacity, PACKED, HALF)
    shapes = [held, (capacity, 24, HALF), (capacity, 2 * PACKED, LANES), (capacity, BINS, HALF)]
    return pl.pallas_call(
        functools.partial(upper_kernel, bool(moved)),
        in_specs=[SMEM, SMEM] + [VMEM] * 3 + ([VMEM] * 2 + [ANY] * 4 if moved else []),
        out_specs=[ANY] * 4 + [SMEM],
        out_shape=[jax.ShapeDtypeStruct(shape, F32) for shape in shapes] + [jax.ShapeDtypeStruct((8,), jnp.int32)],
        scratch_shapes=[pltpu.VMEM(shape, F32) for shape in shapes]
        + [pltpu.VMEM((capacity, PACKED, CELLS), F32), pltpu.VMEM((capacity, 24, CELLS), F32)]
        + [pltpu.VMEM(held, F32)] * 4
        + [pltpu.SemaphoreType.DMA((4, capacity))],
        input_output_aliases={7: 0, 8: 1, 9: 2, 10: 3} if moved else {},
        compiler_params=params(40),
        cost_estimate=pl.CostEstimate(flops=4 * 10**9, bytes_accessed=20 * 10**6, transcendentals=0),
    )(scal, table, spectra, courant, sym, *moved)


def lower_kernel(scal, table, from_q1, from_c, from_face, from_out, below, above, sym, result, up, down, q1, cs, face, own, fy, fz, fx, q2, blank, sems, out_sems, blank_sems):
    count = scal[MID1] - scal[MID0]
    slots = scal[NEW1] - scal[NEW0]

    def copy(k, l):
        source, target = ((from_q1, q1), (from_c, cs), (from_face, face))[k]
        return pltpu.make_async_copy(source.at[l], target.at[l], sems.at[k, l])

    def copy_out(l):
        return pltpu.make_async_copy(from_out.at[l], own.at[l, :, HALF:CELLS], sems.at[3, l])

    def begin(l, _):
        for k in range(3):
            copy(k, l).start()
        copy_out(l).start()
        return 0

    lax.fori_loop(0, count, begin, 0)

    def clear(s):
        return pltpu.make_async_copy(blank, result.at[s], blank_sems.at[s])

    blank[...] = jnp.zeros(blank.shape, F32)

    def clear_start(s, _):
        clear(s).start()
        return 0

    lax.fori_loop(slots, result.shape[0], clear_start, 0)

    def arrive(l, _):
        for k in range(3):
            copy(k, l).wait()
        copy_out(l).wait()
        return 0

    lax.fori_loop(0, count, arrive, 0)

    def fix(l, _):
        position = lax.rem(l, RUN)
        ux, _, _ = neighbours(table, l)

        def add_flux(flux):
            q1[l, :, span(0)] += flat(jnp.where(upper(), 0.0, flux))

        def remote(side):
            fx[l] = side[position]
            flux = view(side[RUN + position // 2])
            add_flux(jnp.where(lax.rem(position, 2) == 0, flux, swap(flux)))

        @pl.when(ux < 0)
        def _():
            remote(below)

        @pl.when(ux >= count)
        def _():
            remote(above)

        @pl.when((ux >= 0) & (ux < count))
        def _():
            fx[l] = face[ux, 0:PACKED]
            add_flux(swap(view(face[ux, PACKED : 2 * PACKED])))

        return 0

    lax.fori_loop(0, count, fix, 0)
    cross_flux(count, lambda i: i, table, q1, cs, fy, fz, 0, 0)

    def second(l):
        side = view(fx[l])
        q = read(q1, l, 0)
        f = limited(q, speed(cs, l, 0, 0), jnp.where(upper(), swap(q), side))
        q2[l, :, span(0)] = flat(q - f + swap(jnp.where(upper(), side, f)) + cross(table, l, fy, fz, 0))
        q_prev, f_prev = q, f
        q = read(q1, l, 1)
        f = limited(q, speed(cs, l, 0, 1), swap(jnp.where(upper(), q_prev, q)))
        q2[l, :, span(1)] = flat(q - f + swap(jnp.where(upper(), f_prev, f)) + cross(table, l, fy, fz, 1))

    second(0)

    def third(l, _):
        own[l, :, 0:HALF] = coalesce(q2[l], sym)[0:BINS]
        second(jnp.minimum(l + 1, count - 1))
        return 0

    def leave(act):
        def body(l, _):
            s = scal[MID0] + l - scal[NEW0]

            @pl.when(l < RUN)
            def _():
                act(pltpu.make_async_copy(own.at[l], down.at[l], out_sems.at[0, l]))

            @pl.when(l >= count - RUN)
            def _():
                act(pltpu.make_async_copy(own.at[l], up.at[l - (count - RUN)], out_sems.at[1, l]))

            @pl.when((s >= 0) & (s < slots))
            def _():
                act(pltpu.make_async_copy(own.at[l], result.at[s], out_sems.at[2, l]))

            return 0

        return body

    def one_run(r, _):
        lax.fori_loop(r * RUN, r * RUN + RUN, third, 0)
        lax.fori_loop(r * RUN, r * RUN + RUN, leave(lambda copy: copy.start()), 0)
        return 0

    lax.fori_loop(0, lax.div(count, RUN), one_run, 0)
    lax.fori_loop(0, count, leave(lambda copy: copy.wait()), 0)

    def clear_wait(s, _):
        clear(s).wait()
        return 0

    lax.fori_loop(slots, result.shape[0], clear_wait, 0)


def lower_half(scal, table, arrays, below, above, sym):
    capacity = arrays[0].shape[0]
    whole = jax.ShapeDtypeStruct((capacity, BINS, CELLS), F32)
    sent = jax.ShapeDtypeStruct((RUN, BINS, CELLS), F32)
    held = pltpu.VMEM((capacity, PACKED, HALF), F32)
    return pl.pallas_call(
        lower_kernel,
        in_specs=[SMEM, SMEM] + [ANY] * 4 + [VMEM] * 3,
        out_specs=[ANY] * 3,
        out_shape=[whole, sent, sent],
        scratch_shapes=[
            held,
            pltpu.VMEM((capacity, 24, HALF), F32),
            pltpu.VMEM((capacity, 2 * PACKED, LANES), F32),
            pltpu.VMEM((capacity, BINS, CELLS), F32),
            held,
            held,
            pltpu.VMEM((capacity, PACKED, LANES), F32),
            held,
            pltpu.VMEM((BINS, CELLS), F32),
            pltpu.SemaphoreType.DMA((4, capacity)),
            pltpu.SemaphoreType.DMA((3, capacity)),
            pltpu.SemaphoreType.DMA((capacity,)),
        ],
        compiler_params=params(32),
        cost_estimate=pl.CostEstimate(flops=8 * 10**9, bytes_accessed=20 * 10**6, transcendentals=0),
    )(scal, table, *arrays, below, above, sym)


def place_moved_kernel(scal, low, high, _, out, sems):
    first, end = scal[NEW0], scal[NEW1]

    def copies(act):
        for k in range(RUN):
            block = scal[MID0] - RUN + k

            @pl.when((block >= first) & (block < end))
            def _(k=k, block=block):
                act(pltpu.make_async_copy(low.at[k], out.at[block - first], sems.at[0, k]))

            above = scal[MID1] + k

            @pl.when((above >= first) & (above < end))
            def _(k=k, above=above):
                act(pltpu.make_async_copy(high.at[k], out.at[above - first], sems.at[1, k]))

    copies(lambda copy: copy.start())
    copies(lambda copy: copy.wait())


def place_moved(scal, low, high, out):
    return pl.pallas_call(
        place_moved_kernel,
        in_specs=[SMEM, VMEM, VMEM, ANY],
        out_specs=ANY,
        out_shape=jax.ShapeDtypeStruct(out.shape, F32),
        scratch_shapes=[pltpu.SemaphoreType.DMA((2, RUN))],
        input_output_aliases={3: 0},
        compiler_params=params(8),
    )(scal, low, high, out)


def bounds_kernel(device, old_count, new_count, out):
    ids = lax.broadcasted_iota(jnp.int32, old_count.shape, 1)

    def total(counts, p):
        return jnp.sum(jnp.where(ids < p, counts[...], 0).astype(F32)).astype(jnp.int32)

    def start(p):
        old, new = total(old_count, p), total(new_count, p)
        least = lax.div(jnp.maximum(old, new) + RUN - 1, RUN) * RUN - RUN
        most = lax.div(jnp.minimum(old, new), RUN) * RUN + RUN
        return old, jnp.clip(2 * RUN * p, least, most), new

    old0, mid0, new0 = start(device[0])
    old1, mid1, new1 = start(device[0] + 1)
    out[OLD0], out[OLD1], out[MID0], out[MID1], out[NEW0], out[NEW1] = old0, old1, mid0, mid1, new0, new1
    here0 = lax.div(jnp.maximum(old0 - mid0, 0) + RUN - 1, RUN) * RUN
    here1 = lax.div(jnp.minimum(old1, mid1) - mid0, RUN) * RUN
    out[HERE0], out[HERE1] = here0, jnp.maximum(here0, here1)


def bounds(device, old_count, new_count):
    return pl.pallas_call(
        bounds_kernel,
        in_specs=[SMEM, VMEM, VMEM],
        out_specs=SMEM,
        out_shape=jax.ShapeDtypeStruct((8,), jnp.int32),
    )(device, old_count.reshape(1, -1), new_count.reshape(1, -1))


def on_device(devices, spectra, courant, kernel, old_count, new_count, upwind):
    device = lax.axis_index("blocks").astype(jnp.int32).reshape(1)
    rise = [(i, i + 1) for i in range(devices - 1)]
    fall = [(i + 1, i) for i in range(devices - 1)]
    around = [(i, (i + 1) % devices) for i in range(devices)]
    reverse = [(j, i) for i, j in around]

    def move(block, route):
        return lax.ppermute(block, "blocks", route)

    tail, head = pack(old_count, device, spectra, courant)
    low, high = move(tail, rise), move(head, fall)
    scal = bounds(device, old_count, new_count)
    table = upwind[RUN : 2 * RUN].reshape(-1)
    sym = symmetric_kernel(kernel)
    *early, scal = upper_half(scal, table, spectra, courant, sym)
    up, down = faces(scal, table, spectra, courant, low, high)
    below, above = move(up, around), move(down, reverse)
    *arrays, scal = upper_half(scal, table, spectra, courant, sym, low, high, *early)
    result, up, down = lower_half(scal, table, arrays, below, above, sym)
    low, high = move(up, rise), move(down, fall)
    return place_moved(scal, low, high, result)


def solution(mesh):
    in_specs = (P("blocks", None, None), P("blocks", None, None), P(), P(), P(), P())
    out_specs = P("blocks", None, None)
    return jax.shard_map(
        functools.partial(on_device, mesh.shape["blocks"]),
        mesh=mesh,
        in_specs=in_specs,
        out_specs=out_specs,
        check_vma=False,
    )
```

```python
import functools

import jax
import jax.numpy as jnp
import numpy as np
from jax import lax
from jax.experimental import pallas as pl
from jax.experimental.pallas import tpu as pltpu
from jax.sharding import PartitionSpec as P

RUN = 12
BINS = 66
CELLS = 512
HALF = 256
LANES = 128
PACKED = 72
FULL = 64
TERMS = 2304
GROUPS = 9
FACES = 18
F32 = jnp.float32
VMEM = pl.BlockSpec(memory_space=pltpu.VMEM)
SMEM = pl.BlockSpec(memory_space=pltpu.SMEM)
OLD0, OLD1, MID0, MID1, NEW0, NEW1, HERE0, HERE1 = range(8)
ANY = pl.BlockSpec(memory_space=pl.ANY)


def params(mib):
    return pltpu.CompilerParams(vmem_limit_bytes=mib * 2**20)


def lanes():
    return lax.broadcasted_iota(jnp.int32, (8, LANES), 1)


def span(v):
    return slice(v * LANES, (v + 1) * LANES)


def upper():
    return lanes() >= 64


def last_y():
    return lanes() // 8 % 8 == 7


def last_z():
    return lanes() % 8 == 7


def view(x):
    return x.reshape(GROUPS, 8, LANES)


def flat(x):
    return x.reshape(PACKED, LANES)


def swap(x):
    return pltpu.roll(flat(x), 64, 1).reshape(x.shape)


def permuted(x, source):
    return view(jnp.take_along_axis(flat(x), source, axis=1, mode="promise_in_bounds"))


def wide_lanes():
    return lax.broadcasted_iota(jnp.int32, (PACKED, LANES), 1)


def step_y(x):
    at = wide_lanes()
    return permuted(x, jnp.where(at // 8 % 8 == 0, at + 56, at - 8))


def step_z(x):
    at = wide_lanes()
    return permuted(x, jnp.where(at % 8 == 0, at + 7, at - 1))


def minmod(a, e):
    return jnp.maximum(jnp.minimum(a, e), 0.0) + jnp.minimum(jnp.maximum(a, e), 0.0)


def limited(q, c, before):
    return c * (q + (0.5 * (1.0 - c)) * minmod(q - before, q))


def upwind_of(table, position):
    back = table[3 * position] < RUN + position
    return back, table[3 * position + 1] - RUN, table[3 * position + 2] - RUN


def read(ref, l, v):
    return view(ref[l, :, span(v)])


def speed(ref, l, d, v):
    return ref[l, 8 * d : 8 * d + 8, span(v)]


def donor(q0, cs, l, v, q_prev, cx_prev, uy, uz):
    q, cx, cy, cz = read(q0, l, v), speed(cs, l, 0, v), speed(cs, l, 1, v), speed(cs, l, 2, v)
    up, ly, lz = upper(), last_y(), last_z()
    in_x = swap(jnp.where(up, 0.0 if q_prev is None else cx_prev * q_prev, cx * q))
    in_y = step_y(jnp.where(ly, speed(cs, uy, 1, v), cy) * jnp.where(ly, read(q0, uy, v), q))
    in_z = step_z(jnp.where(lz, speed(cs, uz, 2, v), cz) * jnp.where(lz, read(q0, uz, v), q))
    return (1.0 - (cx + cy + cz)) * q + in_x + in_y + in_z


def fetch(block, scal, spectra, courant, low, high, q_dst, c_dst, at):
    own0, own1 = scal[OLD0], scal[OLD1]

    def spread(ref, i, row):
        for d in range(3):
            c_dst[at, 8 * d : 8 * d + 8] = jnp.broadcast_to(
                ref[i, row + d : row + d + 1], (8,) + ref.shape[2:]
            )

    def owned():
        q_dst[at, 0:BINS] = spectra[block - own0]
        spread(courant, block - own0, 0)

    if low is None:
        owned()
        return
    pl.when((block >= own0) & (block < own1))(owned)

    def received(ref, i):
        q_dst[at] = ref[i]
        spread(ref, i, BINS)

    @pl.when(block < own0)
    def _():
        received(low, block - own0 + RUN)

    @pl.when(block >= own1)
    def _():
        received(high, block - own1)


def pack_kernel(old_count, device, spectra, courant, up, down, raw, speeds, joined, in_sems, out_sems):
    tail = old_count[device[0]] - RUN
    copies = []
    for side, start in ((0, tail), (1, 0)):
        copies.append(pltpu.make_async_copy(courant.at[pl.ds(start, RUN)], speeds.at[side], in_sems.at[side, RUN]))
        copies[-1].start()
    waits, sends = [], []
    for k in range(0, RUN, 2):
        for side, start, out in ((0, tail, up), (1, 0, down)):
            here = pl.ds(k, 2)
            copy = pltpu.make_async_copy(spectra.at[pl.ds(start + k, 2)], raw.at[side, here], in_sems.at[side, k])
            copy.start()
            waits.append((side, k, copy))
            sends.append(pltpu.make_async_copy(joined.at[side, here], out.at[here], out_sems.at[side, k]))
    for copy in copies:
        copy.wait()
    for (side, k, copy), send in zip(waits, sends):
        copy.wait()
        for i in (k, k + 1):
            joined[side, i, 0:BINS] = raw[side, i]
            joined[side, i, BINS : BINS + 3] = speeds[side, i]
        send.start()
    for send in sends:
        send.wait()


def pack(old_count, device, spectra, courant):
    sent = jax.ShapeDtypeStruct((RUN, PACKED, CELLS), F32)
    return pl.pallas_call(
        pack_kernel,
        in_specs=[SMEM, SMEM, ANY, ANY],
        out_specs=[ANY, ANY],
        out_shape=[sent, sent],
        scratch_shapes=[
            pltpu.VMEM((2, RUN, BINS, CELLS), F32),
            pltpu.VMEM((2, RUN, 3, CELLS), F32),
            pltpu.VMEM((2, RUN, PACKED, CELLS), F32),
            pltpu.SemaphoreType.DMA((2, RUN + 1)),
            pltpu.SemaphoreType.DMA((2, RUN)),
        ],
        compiler_params=params(56),
    )(old_count, device, spectra, courant)


def face_kernel(scal, table, spectra, courant, low, high, up, down, q0, cs):
    count = scal[MID1] - scal[MID0]

    def gather(j, _):
        first = scal[MID0] + jnp.where(j < RUN, j, count - 2 * RUN + j)
        fetch(first, scal, spectra, courant, low, high, q0, cs, j)
        return 0

    lax.fori_loop(0, 2 * RUN, gather, 0)

    def face(j, position):
        _, y, z = upwind_of(table, position)
        uy, uz = y + (j - position), z + (j - position)
        q1 = donor(q0, cs, j, 1, read(q0, j, 0), speed(cs, j, 0, 0), uy, uz)
        other = swap(q1)
        c = speed(cs, j, 0, 1)
        return jnp.where(upper(), limited(q1, c, other), other), c * read(q0, j, 1)

    for base, out in ((0, down), (RUN, up)):

        def pair(i, _, base=base, out=out):
            a0, b0 = face(base + 2 * i, 2 * i)
            a1, b1 = face(base + 2 * i + 1, 2 * i + 1)
            out[2 * i] = flat(a0)
            out[2 * i + 1] = flat(a1)
            out[RUN + i] = flat(jnp.where(upper(), b1, swap(b0)))
            return 0

        lax.fori_loop(0, RUN // 2, pair, 0)


def faces(scal, table, spectra, courant, low, high):
    capacity = spectra.shape[0]

    def half(*dims):
        return pl.BlockSpec(dims + (HALF,), lambda i: (0, 0, 1))

    return pl.pallas_call(
        face_kernel,
        grid=(1,),
        in_specs=[
            SMEM,
            SMEM,
            half(capacity, BINS),
            half(capacity, 3),
            half(RUN, PACKED),
            half(RUN, PACKED),
        ],
        out_specs=[VMEM] * 2,
        out_shape=[jax.ShapeDtypeStruct((FACES, PACKED, LANES), F32)] * 2,
        scratch_shapes=[pltpu.VMEM((2 * RUN, PACKED, HALF), F32), pltpu.VMEM((2 * RUN, 24, HALF), F32)],
        compiler_params=params(24),
    )(scal, table, spectra, courant, low, high)


def pair_terms(q):
    wide = q.shape[1]
    group = [q[8 * g : 8 * g + 8, :] for g in range(8)]
    row = [jnp.broadcast_to(q[i : i + 1, :], (8, wide)) for i in range(BINS)]
    out = [row[i] * group[g] for i in range(56) for g in range(i // 8 + 1, 8)]
    out += [row[i] * group[g] for i in (64, 65) for g in range(8)]
    for s in range(5):
        out += [x * (pltpu.roll(x, s, 0) if s else x) for x in group]
    at = lax.broadcasted_iota(jnp.int32, (8, wide), 0)
    rest = jnp.where(at < 2, row[64], row[65]) * jnp.where(at < 1, row[64], row[65])
    out.append(jnp.where(at < 3, rest, 0.0))
    return out + [jnp.zeros((8, wide), F32)] * (TERMS // 8 - len(out))


def pair_columns():
    pairs = [(i, j) for i in range(56) for j in range(i // 8 * 8 + 8, FULL)]
    pairs += [(i, j) for i in (64, 65) for j in range(FULL)]
    for s in range(5):
        for g in range(0, FULL, 8):
            pairs += [(g + r, g + (r - s) % 8) if s < 4 or r < 4 else None for r in range(8)]
    pairs += [(64, 64), (64, 65), (65, 65)]
    pairs += [None] * (TERMS - len(pairs))
    one = [p[0] * BINS + p[1] if p else -1 for p in pairs]
    two = [p[1] * BINS + p[0] if p and p[0] != p[1] else -1 for p in pairs]
    return np.array([one, two], np.int32)


def symmetric_kernel_body(columns, kernel, out):
    width = out.shape[1]
    row = lax.broadcasted_iota(jnp.int32, (256, width), 0).astype(F32).astype(jnp.bfloat16)
    picks = []
    for base in range(0, kernel.shape[1], 256):
        near = jnp.clip(columns[...] - base, -1, 256).astype(F32).astype(jnp.bfloat16)
        hit = (row == near[0:1]) | (row == near[1:2])
        picks.append(jnp.where(hit, jnp.bfloat16(1), jnp.bfloat16(0)))
    total = jnp.dot(kernel[...], jnp.concatenate(picks, axis=0), preferred_element_type=F32)
    out[...] = total.astype(jnp.bfloat16)


def symmetric_kernel(kernel):
    wide = -(-kernel.shape[1] // 256) * 256
    padded = jnp.pad(kernel, ((0, 80 - BINS), (0, wide - kernel.shape[1])))
    return pl.pallas_call(
        symmetric_kernel_body,
        grid=(TERMS // 256,),
        in_specs=[
            pl.BlockSpec((2, 256), lambda i: (0, i)),
            pl.BlockSpec((80, wide), lambda i: (0, 0)),
        ],
        out_specs=pl.BlockSpec((80, 256), lambda i: (0, i)),
        out_shape=jax.ShapeDtypeStruct((80, TERMS), jnp.bfloat16),
        compiler_params=params(16),
        cost_estimate=pl.CostEstimate(flops=2 * 10**9, bytes_accessed=10**6, transcendentals=0),
    )(jnp.asarray(pair_columns()), padded)


def coalesce(q, sym):
    terms = pair_terms(q)
    packed = [
        jnp.concatenate(terms[2 * r : 2 * r + 2], axis=0).astype(jnp.bfloat16) for r in range(TERMS // 16)
    ]
    gained = jnp.dot(sym[...], jnp.concatenate(packed, axis=0), preferred_element_type=F32)
    return q + gained[0:PACKED]


def neighbours(table, l):
    position = lax.rem(l, RUN)
    back, y, z = upwind_of(table, position)
    return jnp.where(back, l - RUN, l + RUN), y + (l - position), z + (l - position)


def cross_flux(count, block_at, table, q1, cs, fy, fz, v0, vf):
    def cross_body(i, _):
        l = block_at(i)
        _, uy, uz = neighbours(table, l)
        for w in range(2):
            q = read(q1, l, v0 + w)
            before_y = step_y(jnp.where(last_y(), read(q1, uy, v0 + w), q))
            before_z = step_z(jnp.where(last_z(), read(q1, uz, v0 + w), q))
            fy[l, :, span(w)] = flat(limited(q, speed(cs, l, 1, vf + w), before_y))
            fz[l, :, span(w)] = flat(limited(q, speed(cs, l, 2, vf + w), before_z))
        return 0

    lax.fori_loop(0, count, cross_body, 0)


def cross(table, l, fy, fz, w):
    _, uy, uz = neighbours(table, l)
    y_own, z_own = read(fy, l, w), read(fz, l, w)
    y_in = step_y(jnp.where(last_y(), read(fy, uy, w), y_own))
    z_in = step_z(jnp.where(last_z(), read(fz, uz, w), z_own))
    return (y_in - y_own) + (z_in - z_own)


def upper_kernel(moved, scal, table, spectra, courant, sym, *rest):
    low, high = rest[:2] if moved else (None, None)
    low_q1, low_c, face, out, scal_out, q0, cs, q1, fy, fz, q2 = rest[6 if moved else 0 :]
    for k in range(8):
        scal_out[k] = scal[k]
    here0, here = scal[HERE0], scal[HERE1] - scal[HERE0]
    count = scal[MID1] - scal[MID0] - here if moved else here

    def block_at(i):
        return i + jnp.where(i >= here0, here, 0) if moved else i + here0

    def gather(i, _):
        l = block_at(i)
        fetch(scal[MID0] + l, scal, spectra, courant, low, high, q0, cs, l)
        low_c[l] = cs[l, :, 0:HALF]
        return 0

    lax.fori_loop(0, count, gather, 0)

    def first(i, _):
        l = block_at(i)
        _, uy, uz = neighbours(table, l)
        q_prev = cx_prev = None
        for v in range(4):
            new = donor(q0, cs, l, v, q_prev, cx_prev, uy, uz)
            q_prev, cx_prev = read(q0, l, v), speed(cs, l, 0, v)
            if v < 2:
                low_q1[l, :, span(v)] = flat(new)
            else:
                q1[l, :, span(v - 2)] = flat(new)
        other = swap(new)
        face[l, 0:PACKED] = flat(jnp.where(upper(), limited(new, cx_prev, other), other))
        face[l, PACKED : 2 * PACKED] = flat(cx_prev * q_prev)
        return 0

    lax.fori_loop(0, count, first, 0)
    cross_flux(count, block_at, table, q1, cs, fy, fz, 0, 2)

    def second(l):
        q_prev = read(low_q1, l, 1)
        f_prev = limited(q_prev, speed(cs, l, 0, 1), swap(q_prev))
        for w in range(2):
            q = read(q1, l, w)
            f = limited(q, speed(cs, l, 0, w + 2), swap(jnp.where(upper(), q_prev, q)))
            new = q - f + swap(jnp.where(upper(), f_prev, f)) + cross(table, l, fy, fz, w)
            q2[l, :, span(w)] = flat(new)
            q_prev, f_prev = q, f

    @pl.when(count > 0)
    def _():
        second(block_at(0))

    def third(i, _):
        l = block_at(i)
        out[l] = coalesce(q2[l], sym)[0:BINS]
        second(block_at(jnp.minimum(i + 1, count - 1)))
        return 0

    lax.fori_loop(0, count, third, 0)


def upper_half(scal, table, spectra, courant, sym, *moved):
    capacity = spectra.shape[0]
    held = (capacity, PACKED, HALF)
    shapes = [held, (capacity, 24, HALF), (capacity, 2 * PACKED, LANES), (capacity, BINS, HALF)]
    return pl.pallas_call(
        functools.partial(upper_kernel, bool(moved)),
        in_specs=[SMEM, SMEM] + [VMEM] * 3 + ([VMEM] * 6 if moved else []),
        out_specs=[VMEM] * 4 + [SMEM],
        out_shape=[jax.ShapeDtypeStruct(shape, F32) for shape in shapes] + [jax.ShapeDtypeStruct((8,), jnp.int32)],
        scratch_shapes=[pltpu.VMEM((capacity, PACKED, CELLS), F32), pltpu.VMEM((capacity, 24, CELLS), F32)]
        + [pltpu.VMEM(held, F32)] * 4,
        input_output_aliases={7: 0, 8: 1, 9: 2, 10: 3} if moved else {},
        compiler_params=params(32),
        cost_estimate=pl.CostEstimate(flops=4 * 10**9, bytes_accessed=20 * 10**6, transcendentals=0),
    )(scal, table, spectra, courant, sym, *moved)


def lower_kernel(scal, table, q1_in, cs, face, high_cells, below, above, sym, result, up, down, q1, low_cells, fy, fz, fx, q2, blank, sems, blank_sems):
    count = scal[MID1] - scal[MID0]
    runs = lax.div(count, RUN)
    shift, slots = scal[MID0] - scal[NEW0], scal[NEW1] - scal[NEW0]

    def leave(half, act):
        source = (low_cells, high_cells)[half]
        cells = pl.ds(half * HALF, HALF)

        def body(r, _):
            first = r * RUN
            block = source.at[pl.ds(first, RUN)]

            @pl.when(r == 0)
            def _():
                act(pltpu.make_async_copy(block, down.at[:, :, cells], sems.at[half, 0]))

            @pl.when(r == runs - 1)
            def _():
                act(pltpu.make_async_copy(block, up.at[:, :, cells], sems.at[half, 1]))

            slot = first + shift
            fits = (slot >= 0) & (slot + RUN <= slots)

            @pl.when(fits)
            def _():
                act(pltpu.make_async_copy(block, result.at[pl.ds(slot, RUN), :, cells], sems.at[half, 2 + first]))

            def one(l, _):
                @pl.when((l + shift >= 0) & (l + shift < slots))
                def _():
                    act(pltpu.make_async_copy(source.at[l], result.at[l + shift, :, cells], sems.at[half, 2 + l]))

                return 0

            @pl.when(jnp.logical_not(fits))
            def _():
                lax.fori_loop(first, first + RUN, one, 0)

            return 0

        return body

    def start(copy):
        copy.start()

    def wait(copy):
        copy.wait()

    def clear(act):
        many = blank.shape[0]
        dead = result.shape[0] - slots
        whole = lax.div(dead, many)

        def chunk(k, _):
            at = slots + k * many
            act(pltpu.make_async_copy(blank, result.at[pl.ds(at, many)], blank_sems.at[k]))
            return 0

        lax.fori_loop(0, whole, chunk, 0)

        def one(s, _):
            act(pltpu.make_async_copy(blank.at[0], result.at[s], blank_sems.at[s]))
            return 0

        lax.fori_loop(slots + whole * many, result.shape[0], one, 0)

    lax.fori_loop(0, runs, leave(1, start), 0)
    blank[...] = jnp.zeros(blank.shape, F32)
    clear(start)

    def fix(l, _):
        position = lax.rem(l, RUN)
        ux, _, _ = neighbours(table, l)
        q1[l] = q1_in[l]

        def add_flux(flux):
            q1[l, :, span(0)] += flat(jnp.where(upper(), 0.0, flux))

        def remote(side):
            fx[l] = side[position]
            flux = view(side[RUN + position // 2])
            add_flux(jnp.where(lax.rem(position, 2) == 0, flux, swap(flux)))

        @pl.when(ux < 0)
        def _():
            remote(below)

        @pl.when(ux >= count)
        def _():
            remote(above)

        @pl.when((ux >= 0) & (ux < count))
        def _():
            fx[l] = face[ux, 0:PACKED]
            add_flux(swap(view(face[ux, PACKED : 2 * PACKED])))

        return 0

    lax.fori_loop(0, count, fix, 0)
    cross_flux(count, lambda i: i, table, q1, cs, fy, fz, 0, 0)

    def second(l):
        side = view(fx[l])
        q = read(q1, l, 0)
        f = limited(q, speed(cs, l, 0, 0), jnp.where(upper(), swap(q), side))
        q2[l, :, span(0)] = flat(q - f + swap(jnp.where(upper(), side, f)) + cross(table, l, fy, fz, 0))
        q_prev, f_prev = q, f
        q = read(q1, l, 1)
        f = limited(q, speed(cs, l, 0, 1), swap(jnp.where(upper(), q_prev, q)))
        q2[l, :, span(1)] = flat(q - f + swap(jnp.where(upper(), f_prev, f)) + cross(table, l, fy, fz, 1))

    second(0)

    def third(l, _):
        low_cells[l] = coalesce(q2[l], sym)[0:BINS]
        second(jnp.minimum(l + 1, count - 1))
        return 0

    def one_run(r, _):
        lax.fori_loop(r * RUN, r * RUN + RUN, third, 0)
        leave(0, start)(r, 0)
        return 0

    lax.fori_loop(0, runs, one_run, 0)
    lax.fori_loop(0, runs, leave(0, wait), 0)
    lax.fori_loop(0, runs, leave(1, wait), 0)
    clear(wait)


def lower_half(scal, table, arrays, below, above, sym):
    capacity = arrays[0].shape[0]
    whole = jax.ShapeDtypeStruct((capacity, BINS, CELLS), F32)
    sent = jax.ShapeDtypeStruct((RUN, BINS, CELLS), F32)
    held = pltpu.VMEM((capacity, PACKED, HALF), F32)
    return pl.pallas_call(
        lower_kernel,
        in_specs=[SMEM, SMEM] + [VMEM] * 7,
        out_specs=[ANY] * 3,
        out_shape=[whole, sent, sent],
        scratch_shapes=[
            held,
            pltpu.VMEM((capacity, BINS, HALF), F32),
            held,
            held,
            pltpu.VMEM((capacity, PACKED, LANES), F32),
            held,
            pltpu.VMEM((4, BINS, CELLS), F32),
            pltpu.SemaphoreType.DMA((2, capacity + 2)),
            pltpu.SemaphoreType.DMA((capacity,)),
        ],
        compiler_params=params(30),
        cost_estimate=pl.CostEstimate(flops=8 * 10**9, bytes_accessed=20 * 10**6, transcendentals=0),
    )(scal, table, *arrays, below, above, sym)


def place_moved_kernel(scal, low, high, _, out, sems):
    first, end = scal[NEW0], scal[NEW1]

    def copies(act):
        for k in range(RUN):
            block = scal[MID0] - RUN + k

            @pl.when((block >= first) & (block < end))
            def _(k=k, block=block):
                act(pltpu.make_async_copy(low.at[k], out.at[block - first], sems.at[0, k]))

            above = scal[MID1] + k

            @pl.when((above >= first) & (above < end))
            def _(k=k, above=above):
                act(pltpu.make_async_copy(high.at[k], out.at[above - first], sems.at[1, k]))

    copies(lambda copy: copy.start())
    copies(lambda copy: copy.wait())


def place_moved(scal, low, high, out):
    return pl.pallas_call(
        place_moved_kernel,
        in_specs=[SMEM, VMEM, VMEM, ANY],
        out_specs=ANY,
        out_shape=jax.ShapeDtypeStruct(out.shape, F32),
        scratch_shapes=[pltpu.SemaphoreType.DMA((2, RUN))],
        input_output_aliases={3: 0},
        compiler_params=params(8),
    )(scal, low, high, out)


def bounds_kernel(device, old_count, new_count, out):
    ids = lax.broadcasted_iota(jnp.int32, old_count.shape, 1)

    def total(counts, p):
        return jnp.sum(jnp.where(ids < p, counts[...], 0).astype(F32)).astype(jnp.int32)

    def start(p):
        old, new = total(old_count, p), total(new_count, p)
        least = lax.div(jnp.maximum(old, new) + RUN - 1, RUN) * RUN - RUN
        most = lax.div(jnp.minimum(old, new), RUN) * RUN + RUN
        return old, jnp.clip(2 * RUN * p, least, most), new

    old0, mid0, new0 = start(device[0])
    old1, mid1, new1 = start(device[0] + 1)
    out[OLD0], out[OLD1], out[MID0], out[MID1], out[NEW0], out[NEW1] = old0, old1, mid0, mid1, new0, new1
    here0 = lax.div(jnp.maximum(old0 - mid0, 0) + RUN - 1, RUN) * RUN
    here1 = lax.div(jnp.minimum(old1, mid1) - mid0, RUN) * RUN
    out[HERE0], out[HERE1] = here0, jnp.clip(here1, here0, here0 + RUN)


def bounds(device, old_count, new_count):
    return pl.pallas_call(
        bounds_kernel,
        in_specs=[SMEM, VMEM, VMEM],
        out_specs=SMEM,
        out_shape=jax.ShapeDtypeStruct((8,), jnp.int32),
    )(device, old_count.reshape(1, -1), new_count.reshape(1, -1))


def on_device(devices, spectra, courant, kernel, old_count, new_count, upwind):
    device = lax.axis_index("blocks").astype(jnp.int32).reshape(1)
    rise = [(i, i + 1) for i in range(devices - 1)]
    fall = [(i + 1, i) for i in range(devices - 1)]
    around = [(i, (i + 1) % devices) for i in range(devices)]
    reverse = [(j, i) for i, j in around]

    def move(block, route):
        return lax.ppermute(block, "blocks", route)

    tail, head = pack(old_count, device, spectra, courant)
    low, high = move(tail, rise), move(head, fall)
    scal = bounds(device, old_count, new_count)
    table = upwind[RUN : 2 * RUN].reshape(-1)
    sym = symmetric_kernel(kernel)
    *early, scal = upper_half(scal, table, spectra, courant, sym)
    up, down = faces(scal, table, spectra, courant, low, high)
    below, above = move(up, around), move(down, reverse)
    *arrays, scal = upper_half(scal, table, spectra, courant, sym, low, high, *early)
    result, up, down = lower_half(scal, table, arrays, below, above, sym)
    low, high = move(up, rise), move(down, fall)
    return place_moved(scal, low, high, result)


def solution(mesh):
    in_specs = (P("blocks", None, None), P("blocks", None, None), P(), P(), P(), P())
    out_specs = P("blocks", None, None)
    return jax.shard_map(
        functools.partial(on_device, mesh.shape["blocks"]),
        mesh=mesh,
        in_specs=in_specs,
        out_specs=out_specs,
        check_vma=False,
    )
```

```python
import functools

import jax
import jax.numpy as jnp
import numpy as np
from jax import lax
from jax.experimental import pallas as pl
from jax.experimental.pallas import tpu as pltpu
from jax.sharding import PartitionSpec as P

RUN = 12
BINS = 66
CELLS = 512
HALF = 256
LANES = 128
PACKED = 72
FULL = 64
TERMS = 2304
GROUPS = 9
FACES = 18
F32 = jnp.float32
VMEM = pl.BlockSpec(memory_space=pltpu.VMEM)
SMEM = pl.BlockSpec(memory_space=pltpu.SMEM)
OLD0, OLD1, MID0, MID1, NEW0, NEW1, HERE0, HERE1, ODD = range(9)
SCALARS = 9
ANY = pl.BlockSpec(memory_space=pl.ANY)


def params(mib):
    return pltpu.CompilerParams(vmem_limit_bytes=mib * 2**20)


def lanes():
    return lax.broadcasted_iota(jnp.int32, (8, LANES), 1)


def span(v):
    return slice(v * LANES, (v + 1) * LANES)


def upper():
    return lanes() >= 64


def last_y():
    return lanes() // 8 % 8 == 7


def last_z():
    return lanes() % 8 == 7


def view(x):
    return x.reshape(GROUPS, 8, LANES)


def flat(x):
    return x.reshape(PACKED, LANES)


def swap(x):
    return pltpu.roll(flat(x), 64, 1).reshape(x.shape)


def permuted(x, source):
    return view(jnp.take_along_axis(flat(x), source, axis=1, mode="promise_in_bounds"))


def wide_lanes():
    return lax.broadcasted_iota(jnp.int32, (PACKED, LANES), 1)


def step_y(x):
    at = wide_lanes()
    return permuted(x, jnp.where(at // 8 % 8 == 0, at + 56, at - 8))


def step_z(x):
    at = wide_lanes()
    return permuted(x, jnp.where(at % 8 == 0, at + 7, at - 1))


def minmod(a, e):
    return jnp.maximum(jnp.minimum(a, e), 0.0)


def limited(q, c, before):
    return c * (q + (0.5 * (1.0 - c)) * minmod(q - before, q))


def upwind_of(table, position):
    back = table[3 * position] < RUN + position
    return back, table[3 * position + 1] - RUN, table[3 * position + 2] - RUN


def by_side(scal, pair, other, act_low, act_high, is_low, is_high):
    odd = scal[ODD] == 1
    for mine, low, high in ((odd, pair, other), (jnp.logical_not(odd), other, pair)):
        pl.when(mine & is_low)(functools.partial(act_low, low))
        pl.when(mine & is_high)(functools.partial(act_high, high))


def read(ref, l, v):
    return view(ref[l, :, span(v)])


def speed(ref, l, d, v):
    return ref[l, 8 * d : 8 * d + 8, span(v)]


def donor(q0, cs, l, v, q_prev, cx_prev, uy, uz):
    q, cx, cy, cz = read(q0, l, v), speed(cs, l, 0, v), speed(cs, l, 1, v), speed(cs, l, 2, v)
    up, ly, lz = upper(), last_y(), last_z()
    in_x = swap(jnp.where(up, 0.0 if q_prev is None else cx_prev * q_prev, cx * q))
    in_y = step_y(jnp.where(ly, speed(cs, uy, 1, v), cy) * jnp.where(ly, read(q0, uy, v), q))
    in_z = step_z(jnp.where(lz, speed(cs, uz, 2, v), cz) * jnp.where(lz, read(q0, uz, v), q))
    return (1.0 - (cx + cy + cz)) * q + in_x + in_y + in_z


def fetch(block, scal, spectra, courant, moved, cells, q_dst, c_dst, at):
    own0, own1 = scal[OLD0], scal[OLD1]

    def spread(d, row):
        c_dst[at, 8 * d : 8 * d + 8] = jnp.broadcast_to(row, (8, row.shape[1]))

    def owned():
        q_dst[at, 0:BINS] = spectra[block - own0, :, cells]
        for d in range(3):
            spread(d, courant[d, pl.ds(block - own0, 1), cells])

    if not moved:
        owned()
        return
    pl.when((block >= own0) & (block < own1))(owned)

    def received(i, ref):
        q_dst[at] = ref[i, :, cells]
        for d in range(3):
            spread(d, ref[i, BINS + d : BINS + d + 1, cells])

    from_low = functools.partial(received, block - own0 + RUN)
    from_high = functools.partial(received, block - own1)
    by_side(scal, *moved, from_low, from_high, block < own0, block >= own1)


def pack_kernel(old_count, device, spectra, courant, pair, other, raw, speeds, joined, c_sem, in_sems, out_sems):
    tail = old_count[device[0]] - RUN
    odd = lax.rem(device[0], 2) == 1
    all_speeds = pltpu.make_async_copy(courant, speeds, c_sem)
    all_speeds.start()
    steps = [(k, side) for k in range(0, RUN, 2) for side in (0, 1)]
    starts = (tail, 0)

    def arrival(k, side):
        return pltpu.make_async_copy(
            spectra.at[pl.ds(starts[side] + k, 2)], raw.at[side, pl.ds(k, 2)], in_sems.at[side, k]
        )

    def leave(k, side, act):
        def to(out):
            act(pltpu.make_async_copy(joined.at[side, pl.ds(k, 2)], out.at[pl.ds(k, 2)], out_sems.at[side, k]))

        pl.when(odd)(functools.partial(to, (other, pair)[side]))
        pl.when(jnp.logical_not(odd))(functools.partial(to, (pair, other)[side]))

    for k, side in steps:
        arrival(k, side).start()
    all_speeds.wait()
    for k, side in steps:
        arrival(k, side).wait()
        for i in (k, k + 1):
            joined[side, i, 0:BINS] = raw[side, i]
            for d in range(3):
                joined[side, i, BINS + d : BINS + d + 1] = speeds[d, pl.ds(starts[side] + i, 1)]
        leave(k, side, lambda copy: copy.start())
    for k, side in steps:
        leave(k, side, lambda copy: copy.wait())


def pack(old_count, device, spectra, courant):
    sent = jax.ShapeDtypeStruct((RUN, PACKED, CELLS), F32)
    return pl.pallas_call(
        pack_kernel,
        in_specs=[SMEM, SMEM, ANY, ANY],
        out_specs=[ANY, ANY],
        out_shape=[sent, sent],
        scratch_shapes=[
            pltpu.VMEM((2, RUN, BINS, CELLS), F32),
            pltpu.VMEM(courant.shape, F32),
            pltpu.VMEM((2, RUN, PACKED, CELLS), F32),
            pltpu.SemaphoreType.DMA(()),
            pltpu.SemaphoreType.DMA((2, RUN)),
            pltpu.SemaphoreType.DMA((2, RUN)),
        ],
        compiler_params=params(56),
    )(old_count, device, spectra, courant)


def face_kernel(scal, table, spectra, courant, in_pair, in_other, early, pair, other, scal_out, q0, cs, up, down):
    count = scal[MID1] - scal[MID0]
    for k in range(SCALARS):
        scal_out[k] = scal[k]

    def face(j):
        _, y, z = upwind_of(table, j)
        q1 = donor(q0, cs, j, 1, read(q0, j, 0), speed(cs, j, 0, 0), y, z)
        side = swap(q1)
        c = speed(cs, j, 0, 1)
        return jnp.where(upper(), limited(q1, c, side), side), c * read(q0, j, 1)

    def one_run(start, out):
        was_early = (start >= scal[HERE0]) & (start < scal[HERE1])

        def put(i, a0, b0, a1, b1):
            out[2 * i] = flat(a0)
            out[2 * i + 1] = flat(a1)
            out[RUN + i] = flat(jnp.where(upper(), b1, swap(b0)))

        def take(i, _):
            at = start + 2 * i
            parts = [view(early[l, k : k + PACKED]) for l in (at, at + 1) for k in (0, PACKED)]
            put(i, *parts)
            return 0

        def gather(j, _):
            block = scal[MID0] + start + j
            fetch(block, scal, spectra, courant, (in_pair, in_other), slice(HALF, CELLS), q0, cs, j)
            return 0

        def make(i, _):
            put(i, *face(2 * i), *face(2 * i + 1))
            return 0

        @pl.when(was_early)
        def _():
            lax.fori_loop(0, RUN // 2, take, 0)

        @pl.when(jnp.logical_not(was_early))
        def _():
            lax.fori_loop(0, RUN, gather, 0)
            lax.fori_loop(0, RUN // 2, make, 0)

    one_run(0, down)
    one_run(count - RUN, up)
    odd = scal[ODD] == 1

    @pl.when(odd)
    def _():
        pair[...] = down[...]
        other[...] = up[...]

    @pl.when(jnp.logical_not(odd))
    def _():
        pair[...] = up[...]
        other[...] = down[...]


def faces(scal, table, spectra, courant, in_pair, in_other, early):
    sent = jax.ShapeDtypeStruct((FACES, PACKED, LANES), F32)
    return pl.pallas_call(
        face_kernel,
        in_specs=[SMEM, SMEM] + [VMEM] * 5,
        out_specs=[VMEM, VMEM, SMEM],
        out_shape=[sent, sent, jax.ShapeDtypeStruct((SCALARS,), jnp.int32)],
        scratch_shapes=[
            pltpu.VMEM((RUN, PACKED, HALF), F32),
            pltpu.VMEM((RUN, 24, HALF), F32),
            pltpu.VMEM(sent.shape, F32),
            pltpu.VMEM(sent.shape, F32),
        ],
        compiler_params=params(10),
    )(scal, table, spectra, courant, in_pair, in_other, early)


def pair_terms(q):
    wide = q.shape[1]
    group = [q[8 * g : 8 * g + 8, :] for g in range(8)]
    row = [jnp.broadcast_to(q[i : i + 1, :], (8, wide)) for i in range(BINS)]
    out = [row[i] * group[g] for i in range(56) for g in range(i // 8 + 1, 8)]
    out += [row[i] * group[g] for i in (64, 65) for g in range(8)]
    for s in range(5):
        out += [x * (pltpu.roll(x, s, 0) if s else x) for x in group]
    at = lax.broadcasted_iota(jnp.int32, (8, wide), 0)
    rest = jnp.where(at < 2, row[64], row[65]) * jnp.where(at < 1, row[64], row[65])
    out.append(jnp.where(at < 3, rest, 0.0))
    return out + [jnp.zeros((8, wide), F32)] * (TERMS // 8 - len(out))


def pair_columns():
    pairs = [(i, j) for i in range(56) for j in range(i // 8 * 8 + 8, FULL)]
    pairs += [(i, j) for i in (64, 65) for j in range(FULL)]
    for s in range(5):
        for g in range(0, FULL, 8):
            pairs += [(g + r, g + (r - s) % 8) if s < 4 or r < 4 else None for r in range(8)]
    pairs += [(64, 64), (64, 65), (65, 65)]
    pairs += [None] * (TERMS - len(pairs))
    one = [p[0] * BINS + p[1] if p else -1 for p in pairs]
    two = [p[1] * BINS + p[0] if p and p[0] != p[1] else -1 for p in pairs]
    return np.array([one, two], np.int32)


def symmetric_kernel_body(columns, kernel, out):
    width = out.shape[1]
    row = lax.broadcasted_iota(jnp.int32, (256, width), 0).astype(F32).astype(jnp.bfloat16)
    picks = []
    for base in range(0, kernel.shape[1], 256):
        near = jnp.clip(columns[...] - base, -1, 256).astype(F32).astype(jnp.bfloat16)
        hit = (row == near[0:1]) | (row == near[1:2])
        picks.append(jnp.where(hit, jnp.bfloat16(1), jnp.bfloat16(0)))
    total = jnp.dot(kernel[...], jnp.concatenate(picks, axis=0), preferred_element_type=F32)
    out[...] = total.astype(jnp.bfloat16)


def symmetric_kernel(kernel):
    wide = -(-kernel.shape[1] // 256) * 256
    padded = jnp.pad(kernel, ((0, 80 - BINS), (0, wide - kernel.shape[1])))
    return pl.pallas_call(
        symmetric_kernel_body,
        grid=(TERMS // 256,),
        in_specs=[
            pl.BlockSpec((2, 256), lambda i: (0, i)),
            pl.BlockSpec((80, wide), lambda i: (0, 0)),
        ],
        out_specs=pl.BlockSpec((80, 256), lambda i: (0, i)),
        out_shape=jax.ShapeDtypeStruct((80, TERMS), jnp.bfloat16),
        compiler_params=params(16),
        cost_estimate=pl.CostEstimate(flops=2 * 10**9, bytes_accessed=10**6, transcendentals=0),
    )(jnp.asarray(pair_columns()), padded)


def coalesce(q, sym):
    terms = pair_terms(q)
    packed = [
        jnp.concatenate(terms[2 * r : 2 * r + 2], axis=0).astype(jnp.bfloat16) for r in range(TERMS // 16)
    ]
    gained = jnp.dot(sym[...], jnp.concatenate(packed, axis=0), preferred_element_type=F32)
    return q + gained[0:PACKED]


def neighbours(table, l):
    position = lax.rem(l, RUN)
    back, y, z = upwind_of(table, position)
    return jnp.where(back, l - RUN, l + RUN), y + (l - position), z + (l - position)


def cross_flux(count, block_at, table, q1, cs, fy, fz, v0, vf):
    def cross_body(i, _):
        l = block_at(i)
        _, uy, uz = neighbours(table, l)
        for w in range(2):
            q = read(q1, l, v0 + w)
            before_y = step_y(jnp.where(last_y(), read(q1, uy, v0 + w), q))
            before_z = step_z(jnp.where(last_z(), read(q1, uz, v0 + w), q))
            fy[l, :, span(w)] = flat(limited(q, speed(cs, l, 1, vf + w), before_y))
            fz[l, :, span(w)] = flat(limited(q, speed(cs, l, 2, vf + w), before_z))
        return 0

    lax.fori_loop(0, count, cross_body, 0)


def cross(table, l, fy, fz, w):
    _, uy, uz = neighbours(table, l)
    y_own, z_own = read(fy, l, w), read(fz, l, w)
    y_in = step_y(jnp.where(last_y(), read(fy, uy, w), y_own))
    z_in = step_z(jnp.where(last_z(), read(fz, uz, w), z_own))
    return (y_in - y_own) + (z_in - z_own)


def upper_kernel(moved, scal, table, spectra, courant, sym, *rest):
    low_q1, low_c, face, out, scal_out, q0, cs, q1, fy, fz, q2 = rest[6 if moved else 0 :]
    for k in range(SCALARS):
        scal_out[k] = scal[k]
    here0, here = scal[HERE0], scal[HERE1] - scal[HERE0]
    count = scal[MID1] - scal[MID0] - here if moved else here

    def block_at(i):
        return i + jnp.where(i >= here0, here, 0) if moved else i + here0

    def gather(i, _):
        l = block_at(i)
        fetch(scal[MID0] + l, scal, spectra, courant, rest[:2] if moved else (), slice(0, CELLS), q0, cs, l)
        low_c[l] = cs[l, :, 0:HALF]
        return 0

    lax.fori_loop(0, count, gather, 0)

    def first(i, _):
        l = block_at(i)
        _, uy, uz = neighbours(table, l)
        q_prev = cx_prev = None
        for v in range(4):
            new = donor(q0, cs, l, v, q_prev, cx_prev, uy, uz)
            q_prev, cx_prev = read(q0, l, v), speed(cs, l, 0, v)
            if v < 2:
                low_q1[l, :, span(v)] = flat(new)
            else:
                q1[l, :, span(v - 2)] = flat(new)
        other = swap(new)
        face[l, 0:PACKED] = flat(jnp.where(upper(), limited(new, cx_prev, other), other))
        face[l, PACKED : 2 * PACKED] = flat(cx_prev * q_prev)
        return 0

    lax.fori_loop(0, count, first, 0)
    cross_flux(count, block_at, table, q1, cs, fy, fz, 0, 2)

    def second(l):
        q_prev = read(low_q1, l, 1)
        f_prev = limited(q_prev, speed(cs, l, 0, 1), swap(q_prev))
        for w in range(2):
            q = read(q1, l, w)
            f = limited(q, speed(cs, l, 0, w + 2), swap(jnp.where(upper(), q_prev, q)))
            new = q - f + swap(jnp.where(upper(), f_prev, f)) + cross(table, l, fy, fz, w)
            q2[l, :, span(w)] = flat(new)
            q_prev, f_prev = q, f

    @pl.when(count > 0)
    def _():
        second(block_at(0))

    def third(i, _):
        l = block_at(i)
        out[l] = coalesce(q2[l], sym)[0:BINS]
        second(block_at(jnp.minimum(i + 1, count - 1)))
        return 0

    lax.fori_loop(0, count, third, 0)


def upper_half(scal, table, spectra, courant, sym, *moved):
    capacity = spectra.shape[0]
    held = (capacity, PACKED, HALF)
    shapes = [held, (capacity, 24, HALF), (capacity, 2 * PACKED, LANES), (capacity, BINS, HALF)]
    return pl.pallas_call(
        functools.partial(upper_kernel, bool(moved)),
        in_specs=[SMEM, SMEM] + [VMEM] * 3 + ([VMEM] * 6 if moved else []),
        out_specs=[VMEM] * 4 + [SMEM],
        out_shape=[jax.ShapeDtypeStruct(shape, F32) for shape in shapes] + [jax.ShapeDtypeStruct((SCALARS,), jnp.int32)],
        scratch_shapes=[pltpu.VMEM((capacity, PACKED, CELLS), F32), pltpu.VMEM((capacity, 24, CELLS), F32)]
        + [pltpu.VMEM(held, F32)] * 4,
        input_output_aliases={7: 0, 8: 1, 9: 2, 10: 3} if moved else {},
        compiler_params=params(32),
        cost_estimate=pl.CostEstimate(flops=4 * 10**9, bytes_accessed=20 * 10**6, transcendentals=0),
    )(scal, table, spectra, courant, sym, *moved)


def lower_kernel(scal, table, q1_in, cs, face, high_cells, in_pair, in_other, sym, result, pair, other, q1, low_cells, fy, fz, fx, q2, blank, sems, blank_sems):
    count = scal[MID1] - scal[MID0]
    runs = lax.div(count, RUN)
    shift, slots = scal[MID0] - scal[NEW0], scal[NEW1] - scal[NEW0]

    def leave(half, act):
        source = (low_cells, high_cells)[half]
        cells = pl.ds(half * HALF, HALF)

        def body(r, _):
            first = r * RUN
            block = source.at[pl.ds(first, RUN)]

            def down(ref):
                act(pltpu.make_async_copy(block, ref.at[:, :, cells], sems.at[half, 0]))

            def up(ref):
                act(pltpu.make_async_copy(block, ref.at[:, :, cells], sems.at[half, 1]))

            by_side(scal, pair, other, down, up, r == 0, r == runs - 1)

            slot = first + shift
            fits = (slot >= 0) & (slot + RUN <= slots)

            @pl.when(fits)
            def _():
                act(pltpu.make_async_copy(block, result.at[pl.ds(slot, RUN), :, cells], sems.at[half, 2 + first]))

            def one(l, _):
                @pl.when((l + shift >= 0) & (l + shift < slots))
                def _():
                    act(pltpu.make_async_copy(source.at[l], result.at[l + shift, :, cells], sems.at[half, 2 + l]))

                return 0

            @pl.when(jnp.logical_not(fits))
            def _():
                lax.fori_loop(first, first + RUN, one, 0)

            return 0

        return body

    def start(copy):
        copy.start()

    def wait(copy):
        copy.wait()

    def clear(act):
        many = blank.shape[0]
        dead = result.shape[0] - slots
        whole = lax.div(dead, many)

        def chunk(k, _):
            at = slots + k * many
            act(pltpu.make_async_copy(blank, result.at[pl.ds(at, many)], blank_sems.at[k]))
            return 0

        lax.fori_loop(0, whole, chunk, 0)

        def one(s, _):
            act(pltpu.make_async_copy(blank.at[0], result.at[s], blank_sems.at[s]))
            return 0

        lax.fori_loop(slots + whole * many, result.shape[0], one, 0)

    lax.fori_loop(0, runs, leave(1, start), 0)
    blank[...] = jnp.zeros(blank.shape, F32)
    clear(start)

    def fix(l, _):
        position = lax.rem(l, RUN)
        ux, _, _ = neighbours(table, l)
        q1[l] = q1_in[l]

        def add_flux(flux):
            q1[l, :, span(0)] += flat(jnp.where(upper(), 0.0, flux))

        def remote(side):
            fx[l] = side[position]
            flux = view(side[RUN + position // 2])
            add_flux(jnp.where(lax.rem(position, 2) == 0, flux, swap(flux)))

        by_side(scal, in_pair, in_other, remote, remote, ux < 0, ux >= count)

        @pl.when((ux >= 0) & (ux < count))
        def _():
            fx[l] = face[ux, 0:PACKED]
            add_flux(swap(view(face[ux, PACKED : 2 * PACKED])))

        return 0

    lax.fori_loop(0, count, fix, 0)
    cross_flux(count, lambda i: i, table, q1, cs, fy, fz, 0, 0)

    def second(l):
        side = view(fx[l])
        q = read(q1, l, 0)
        f = limited(q, speed(cs, l, 0, 0), jnp.where(upper(), swap(q), side))
        q2[l, :, span(0)] = flat(q - f + swap(jnp.where(upper(), side, f)) + cross(table, l, fy, fz, 0))
        q_prev, f_prev = q, f
        q = read(q1, l, 1)
        f = limited(q, speed(cs, l, 0, 1), swap(jnp.where(upper(), q_prev, q)))
        q2[l, :, span(1)] = flat(q - f + swap(jnp.where(upper(), f_prev, f)) + cross(table, l, fy, fz, 1))

    second(0)

    def third(l, _):
        low_cells[l] = coalesce(q2[l], sym)[0:BINS]
        second(jnp.minimum(l + 1, count - 1))
        return 0

    def one_run(r, _):
        lax.fori_loop(r * RUN, r * RUN + RUN, third, 0)
        leave(0, start)(r, 0)
        return 0

    lax.fori_loop(0, runs, one_run, 0)
    lax.fori_loop(0, runs, leave(0, wait), 0)
    lax.fori_loop(0, runs, leave(1, wait), 0)
    clear(wait)


def lower_half(scal, table, arrays, in_pair, in_other, sym):
    capacity = arrays[0].shape[0]
    whole = jax.ShapeDtypeStruct((capacity, BINS, CELLS), F32)
    sent = jax.ShapeDtypeStruct((RUN, BINS, CELLS), F32)
    held = pltpu.VMEM((capacity, PACKED, HALF), F32)
    return pl.pallas_call(
        lower_kernel,
        in_specs=[SMEM, SMEM] + [VMEM] * 7,
        out_specs=[ANY] * 3,
        out_shape=[whole, sent, sent],
        scratch_shapes=[
            held,
            pltpu.VMEM((capacity, BINS, HALF), F32),
            held,
            held,
            pltpu.VMEM((capacity, PACKED, LANES), F32),
            held,
            pltpu.VMEM((4, BINS, CELLS), F32),
            pltpu.SemaphoreType.DMA((2, capacity + 2)),
            pltpu.SemaphoreType.DMA((capacity,)),
        ],
        compiler_params=params(30),
        cost_estimate=pl.CostEstimate(flops=8 * 10**9, bytes_accessed=20 * 10**6, transcendentals=0),
    )(scal, table, *arrays, in_pair, in_other, sym)


def place_moved_kernel(scal, pair, other, _, out, sems):
    first, end = scal[NEW0], scal[NEW1]

    def copies(act):
        for k in range(RUN):
            low, high = scal[MID0] - RUN + k, scal[MID1] + k

            def from_low(ref, k=k, low=low):
                act(pltpu.make_async_copy(ref.at[k], out.at[low - first], sems.at[0, k]))

            def from_high(ref, k=k, high=high):
                act(pltpu.make_async_copy(ref.at[k], out.at[high - first], sems.at[1, k]))

            low_in = (low >= first) & (low < end)
            high_in = (high >= first) & (high < end)
            by_side(scal, pair, other, from_low, from_high, low_in, high_in)

    copies(lambda copy: copy.start())
    copies(lambda copy: copy.wait())


def place_moved(scal, pair, other, out):
    return pl.pallas_call(
        place_moved_kernel,
        in_specs=[SMEM, VMEM, VMEM, ANY],
        out_specs=ANY,
        out_shape=jax.ShapeDtypeStruct(out.shape, F32),
        scratch_shapes=[pltpu.SemaphoreType.DMA((2, RUN))],
        input_output_aliases={3: 0},
        compiler_params=params(8),
    )(scal, pair, other, out)


def bounds_kernel(device, old_count, new_count, out):
    ids = lax.broadcasted_iota(jnp.int32, old_count.shape, 1)

    def total(counts, p):
        return jnp.sum(jnp.where(ids < p, counts[...], 0).astype(F32)).astype(jnp.int32)

    def start(p):
        old, new = total(old_count, p), total(new_count, p)
        least = lax.div(jnp.maximum(old, new) + RUN - 1, RUN) * RUN - RUN
        most = lax.div(jnp.minimum(old, new), RUN) * RUN + RUN
        return old, jnp.clip(2 * RUN * p, least, most), new

    old0, mid0, new0 = start(device[0])
    old1, mid1, new1 = start(device[0] + 1)
    out[OLD0], out[OLD1], out[MID0], out[MID1], out[NEW0], out[NEW1] = old0, old1, mid0, mid1, new0, new1
    here0 = lax.div(jnp.maximum(old0 - mid0, 0) + RUN - 1, RUN) * RUN
    here1 = lax.div(jnp.minimum(old1, mid1) - mid0, RUN) * RUN
    out[ODD] = lax.rem(device[0], 2)
    out[HERE0], out[HERE1] = here0, jnp.clip(here1, here0, here0 + RUN)


def bounds(device, old_count, new_count):
    return pl.pallas_call(
        bounds_kernel,
        in_specs=[SMEM, VMEM, VMEM],
        out_specs=SMEM,
        out_shape=jax.ShapeDtypeStruct((SCALARS,), jnp.int32),
    )(device, old_count.reshape(1, -1), new_count.reshape(1, -1))


def on_device(devices, spectra, courant, kernel, old_count, new_count, upwind):
    device = lax.axis_index("blocks").astype(jnp.int32).reshape(1)
    pairs = [(i, i ^ 1) for i in range(devices)]
    others = [(i, i + 1) for i in range(1, devices - 1, 2)]
    others += [(j, i) for i, j in others]
    ends = [(devices - 1, 0), (0, devices - 1)]

    def exchange(pair, other, route):
        from_other = lax.ppermute(other, "blocks", route)
        return lax.ppermute(pair, "blocks", pairs), from_other

    courant = jnp.swapaxes(courant, 0, 1)
    moved = exchange(*pack(old_count, device, spectra, courant), others)
    scal = bounds(device, old_count, new_count)
    table = upwind[RUN : 2 * RUN].reshape(-1)
    sym = symmetric_kernel(kernel)
    *early, scal = upper_half(scal, table, spectra, courant, sym)
    *sides, scal = faces(scal, table, spectra, courant, *moved, early[2])
    sides = exchange(*sides, others + ends)
    *arrays, scal = upper_half(scal, table, spectra, courant, sym, *moved, *early)
    result, *results = lower_half(scal, table, arrays, *sides, sym)
    return place_moved(scal, *exchange(*results, others), result)


def solution(mesh):
    in_specs = (P("blocks", None, None), P("blocks", None, None), P(), P(), P(), P())
    out_specs = P("blocks", None, None)
    return jax.shard_map(
        functools.partial(on_device, mesh.shape["blocks"]),
        mesh=mesh,
        in_specs=in_specs,
        out_specs=out_specs,
        check_vma=False,
    )
```

```python
import functools

import jax
import jax.numpy as jnp
import numpy as np
from jax import lax
from jax.experimental import pallas as pl
from jax.experimental.pallas import tpu as pltpu
from jax.sharding import PartitionSpec as P

RUN = 12
BINS = 66
CELLS = 512
HALF = 256
LANES = 128
PACKED = 72
FULL = 64
TERMS = 2304
GROUPS = 9
STENCILS = 6
PRODUCTS = 2
FACES = 18
F32 = jnp.float32
VMEM = pl.BlockSpec(memory_space=pltpu.VMEM)
SMEM = pl.BlockSpec(memory_space=pltpu.SMEM)
OLD0, OLD1, MID0, MID1, NEW0, NEW1, HERE0, HERE1, ODD = range(9)
SCALARS = 9
ANY = pl.BlockSpec(memory_space=pl.ANY)


def params(mib):
    return pltpu.CompilerParams(vmem_limit_bytes=mib * 2**20)


def lanes():
    return lax.broadcasted_iota(jnp.int32, (8, LANES), 1)


def span(v):
    return slice(v * LANES, (v + 1) * LANES)


def upper():
    return lanes() >= 64


def last_y():
    return lanes() // 8 % 8 == 7


def last_z():
    return lanes() % 8 == 7


def view(x):
    return x.reshape(GROUPS, 8, LANES)


def flat(x):
    return x.reshape(PACKED, LANES)


def swap(x):
    return pltpu.roll(flat(x), 64, 1).reshape(x.shape)


def permuted(x, source):
    return view(jnp.take_along_axis(flat(x), source, axis=1, mode="promise_in_bounds"))


def wide_lanes():
    return lax.broadcasted_iota(jnp.int32, (PACKED, LANES), 1)


def step_y(x):
    at = wide_lanes()
    return permuted(x, jnp.where(at // 8 % 8 == 0, at + 56, at - 8))


def step_z(x):
    at = wide_lanes()
    return permuted(x, jnp.where(at % 8 == 0, at + 7, at - 1))


def minmod(a, e):
    return jnp.maximum(jnp.minimum(a, e), 0.0)


def limited(q, c, before):
    return c * (q + (0.5 * (1.0 - c)) * minmod(q - before, q))


def upwind_of(table, position):
    back = table[3 * position] < RUN + position
    return back, table[3 * position + 1] - RUN, table[3 * position + 2] - RUN


def by_side(scal, pair, other, act_low, act_high, is_low, is_high):
    odd = scal[ODD] == 1
    for mine, low, high in ((odd, pair, other), (jnp.logical_not(odd), other, pair)):
        pl.when(mine & is_low)(functools.partial(act_low, low))
        pl.when(mine & is_high)(functools.partial(act_high, high))


def read(ref, l, v):
    return view(ref[l, :, span(v)])


def speed(ref, l, d, v):
    return ref[l, 8 * d : 8 * d + 8, span(v)]


def donor(q0, cs, l, v, q_prev, cx_prev, uy, uz):
    q, cx, cy, cz = read(q0, l, v), speed(cs, l, 0, v), speed(cs, l, 1, v), speed(cs, l, 2, v)
    up, ly, lz = upper(), last_y(), last_z()
    in_x = swap(jnp.where(up, 0.0 if q_prev is None else cx_prev * q_prev, cx * q))
    in_y = step_y(jnp.where(ly, speed(cs, uy, 1, v), cy) * jnp.where(ly, read(q0, uy, v), q))
    in_z = step_z(jnp.where(lz, speed(cs, uz, 2, v), cz) * jnp.where(lz, read(q0, uz, v), q))
    return (1.0 - (cx + cy + cz)) * q + in_x + in_y + in_z


def fetch(block, scal, spectra, courant, moved, cells, q_dst, c_dst, at):
    own0, own1 = scal[OLD0], scal[OLD1]

    def spread(d, row):
        c_dst[at, 8 * d : 8 * d + 8] = jnp.broadcast_to(row, (8, row.shape[1]))

    def owned():
        q_dst[at, 0:BINS] = spectra[block - own0, :, cells]
        for d in range(3):
            spread(d, courant[d, pl.ds(block - own0, 1), cells])

    if not moved:
        owned()
        return
    pl.when((block >= own0) & (block < own1))(owned)

    def received(i, ref):
        q_dst[at] = ref[i, :, cells]
        for d in range(3):
            spread(d, ref[i, BINS + d : BINS + d + 1, cells])

    from_low = functools.partial(received, block - own0 + RUN)
    from_high = functools.partial(received, block - own1)
    by_side(scal, *moved, from_low, from_high, block < own0, block >= own1)


def pack_kernel(old_count, device, spectra, courant, pair, other, raw, speeds, joined, c_sem, in_sems, out_sems):
    tail = old_count[device[0]] - RUN
    odd = lax.rem(device[0], 2) == 1
    all_speeds = pltpu.make_async_copy(courant, speeds, c_sem)
    all_speeds.start()
    steps = [(k, side) for k in range(0, RUN, 2) for side in (0, 1)]
    starts = (tail, 0)

    def arrival(k, side):
        return pltpu.make_async_copy(
            spectra.at[pl.ds(starts[side] + k, 2)], raw.at[side, pl.ds(k, 2)], in_sems.at[side, k]
        )

    def leave(k, side, act):
        def to(out):
            act(pltpu.make_async_copy(joined.at[side, pl.ds(k, 2)], out.at[pl.ds(k, 2)], out_sems.at[side, k]))

        pl.when(odd)(functools.partial(to, (other, pair)[side]))
        pl.when(jnp.logical_not(odd))(functools.partial(to, (pair, other)[side]))

    for k, side in steps:
        arrival(k, side).start()
    all_speeds.wait()
    for k, side in steps:
        arrival(k, side).wait()
        for i in (k, k + 1):
            joined[side, i, 0:BINS] = raw[side, i]
            for d in range(3):
                joined[side, i, BINS + d : BINS + d + 1] = speeds[d, pl.ds(starts[side] + i, 1)]
        leave(k, side, lambda copy: copy.start())
    for k, side in steps:
        leave(k, side, lambda copy: copy.wait())


def pack(old_count, device, spectra, courant):
    sent = jax.ShapeDtypeStruct((RUN, PACKED, CELLS), F32)
    return pl.pallas_call(
        pack_kernel,
        in_specs=[SMEM, SMEM, ANY, ANY],
        out_specs=[ANY, ANY],
        out_shape=[sent, sent],
        scratch_shapes=[
            pltpu.VMEM((2, RUN, BINS, CELLS), F32),
            pltpu.VMEM(courant.shape, F32),
            pltpu.VMEM((2, RUN, PACKED, CELLS), F32),
            pltpu.SemaphoreType.DMA(()),
            pltpu.SemaphoreType.DMA((2, RUN)),
            pltpu.SemaphoreType.DMA((2, RUN)),
        ],
        compiler_params=params(56),
    )(old_count, device, spectra, courant)


def face_kernel(scal, table, spectra, courant, in_pair, in_other, early, pair, other, scal_out, q0, cs, up, down):
    count = scal[MID1] - scal[MID0]
    for k in range(SCALARS):
        scal_out[k] = scal[k]

    def face(j):
        _, y, z = upwind_of(table, j)
        q1 = donor(q0, cs, j, 1, read(q0, j, 0), speed(cs, j, 0, 0), y, z)
        side = swap(q1)
        c = speed(cs, j, 0, 1)
        return jnp.where(upper(), limited(q1, c, side), side), c * read(q0, j, 1)

    def one_run(start, out):
        was_early = (start >= scal[HERE0]) & (start < scal[HERE1])

        def put(i, a0, b0, a1, b1):
            out[2 * i] = flat(a0)
            out[2 * i + 1] = flat(a1)
            out[RUN + i] = flat(jnp.where(upper(), b1, swap(b0)))

        def take(i, _):
            at = start + 2 * i
            parts = [view(early[RUN + l, k : k + PACKED]) for l in (at, at + 1) for k in (0, PACKED)]
            put(i, *parts)
            return 0

        def gather(j, _):
            block = scal[MID0] + start + j
            fetch(block, scal, spectra, courant, (in_pair, in_other), slice(HALF, CELLS), q0, cs, j)
            return 0

        def make(i, _):
            put(i, *face(2 * i), *face(2 * i + 1))
            return 0

        @pl.when(was_early)
        def _():
            lax.fori_loop(0, RUN // 2, take, 0)

        @pl.when(jnp.logical_not(was_early))
        def _():
            lax.fori_loop(0, RUN, gather, 0)
            lax.fori_loop(0, RUN // 2, make, 0)

    one_run(0, down)
    one_run(count - RUN, up)
    odd = scal[ODD] == 1

    @pl.when(odd)
    def _():
        pair[...] = down[...]
        other[...] = up[...]

    @pl.when(jnp.logical_not(odd))
    def _():
        pair[...] = up[...]
        other[...] = down[...]


def faces(scal, table, spectra, courant, in_pair, in_other, early):
    sent = jax.ShapeDtypeStruct((FACES, PACKED, LANES), F32)
    return pl.pallas_call(
        face_kernel,
        in_specs=[SMEM, SMEM] + [VMEM] * 5,
        out_specs=[VMEM, VMEM, SMEM],
        out_shape=[sent, sent, jax.ShapeDtypeStruct((SCALARS,), jnp.int32)],
        scratch_shapes=[
            pltpu.VMEM((RUN, PACKED, HALF), F32),
            pltpu.VMEM((RUN, 24, HALF), F32),
            pltpu.VMEM(sent.shape, F32),
            pltpu.VMEM(sent.shape, F32),
        ],
        compiler_params=params(10),
    )(scal, table, spectra, courant, in_pair, in_other, early)


def pair_terms(q):
    wide = q.shape[1]
    group = [q[8 * g : 8 * g + 8, :] for g in range(8)]
    row = [jnp.broadcast_to(q[i : i + 1, :], (8, wide)) for i in range(BINS)]
    out = [row[i] * group[g] for i in range(56) for g in range(i // 8 + 1, 8)]
    out += [row[i] * group[g] for i in (64, 65) for g in range(8)]
    for s in range(5):
        out += [x * (pltpu.roll(x, s, 0) if s else x) for x in group]
    at = lax.broadcasted_iota(jnp.int32, (8, wide), 0)
    rest = jnp.where(at < 2, row[64], row[65]) * jnp.where(at < 1, row[64], row[65])
    out.append(jnp.where(at < 3, rest, 0.0))
    return out + [jnp.zeros((8, wide), F32)] * (TERMS // 8 - len(out))


def pair_columns():
    pairs = [(i, j) for i in range(56) for j in range(i // 8 * 8 + 8, FULL)]
    pairs += [(i, j) for i in (64, 65) for j in range(FULL)]
    for s in range(5):
        for g in range(0, FULL, 8):
            pairs += [(g + r, g + (r - s) % 8) if s < 4 or r < 4 else None for r in range(8)]
    pairs += [(64, 64), (64, 65), (65, 65)]
    pairs += [None] * (TERMS - len(pairs))
    one = [p[0] * BINS + p[1] if p else -1 for p in pairs]
    two = [p[1] * BINS + p[0] if p and p[0] != p[1] else -1 for p in pairs]
    return np.array([one, two], np.int32)


def symmetric_kernel_body(columns, kernel, out):
    width = out.shape[1]
    row = lax.broadcasted_iota(jnp.int32, (256, width), 0).astype(F32).astype(jnp.bfloat16)
    picks = []
    for base in range(0, kernel.shape[1], 256):
        near = jnp.clip(columns[...] - base, -1, 256).astype(F32).astype(jnp.bfloat16)
        hit = (row == near[0:1]) | (row == near[1:2])
        picks.append(jnp.where(hit, jnp.bfloat16(1), jnp.bfloat16(0)))
    total = jnp.dot(kernel[...], jnp.concatenate(picks, axis=0), preferred_element_type=F32)
    out[...] = total.astype(jnp.bfloat16)


def symmetric_kernel(kernel):
    wide = -(-kernel.shape[1] // 256) * 256
    padded = jnp.pad(kernel, ((0, 80 - BINS), (0, wide - kernel.shape[1])))
    return pl.pallas_call(
        symmetric_kernel_body,
        grid=(TERMS // 256,),
        in_specs=[
            pl.BlockSpec((2, 256), lambda i: (0, i)),
            pl.BlockSpec((80, wide), lambda i: (0, 0)),
        ],
        out_specs=pl.BlockSpec((80, 256), lambda i: (0, i)),
        out_shape=jax.ShapeDtypeStruct((80, TERMS), jnp.bfloat16),
        compiler_params=params(16),
        cost_estimate=pl.CostEstimate(flops=2 * 10**9, bytes_accessed=10**6, transcendentals=0),
    )(jnp.asarray(pair_columns()), padded)


def coalesce(q, sym):
    terms = pair_terms(q)
    packed = [
        jnp.concatenate(terms[2 * r : 2 * r + 2], axis=0).astype(jnp.bfloat16) for r in range(TERMS // 16)
    ]
    gained = jnp.dot(sym[...], jnp.concatenate(packed, axis=0), preferred_element_type=F32)
    return q + gained[0:PACKED]


def several(begin, end, body, at_once):
    def step(k, _):
        for j in range(at_once):
            body(begin + k * at_once + j)
        return 0

    lax.fori_loop(0, lax.div(end - begin, at_once), step, 0)


def neighbours(table, l):
    position = lax.rem(l, RUN)
    back, y, z = upwind_of(table, position)
    return jnp.where(back, l - RUN, l + RUN), y + (l - position), z + (l - position)


def cross_flux(count, block_at, table, q1, cs, fy, fz, v0, vf):
    def cross_body(i):
        l = block_at(i)
        _, uy, uz = neighbours(table, l)
        for w in range(2):
            q = read(q1, l, v0 + w)
            before_y = step_y(jnp.where(last_y(), read(q1, uy, v0 + w), q))
            before_z = step_z(jnp.where(last_z(), read(q1, uz, v0 + w), q))
            fy[l, :, span(w)] = flat(limited(q, speed(cs, l, 1, vf + w), before_y))
            fz[l, :, span(w)] = flat(limited(q, speed(cs, l, 2, vf + w), before_z))

    several(0, count, cross_body, STENCILS)


def cross(table, l, fy, fz, w):
    _, uy, uz = neighbours(table, l)
    y_own, z_own = read(fy, l, w), read(fz, l, w)
    y_in = step_y(jnp.where(last_y(), read(fy, uy, w), y_own))
    z_in = step_z(jnp.where(last_z(), read(fz, uz, w), z_own))
    return (y_in - y_own) + (z_in - z_own)


def coalesce_all(begin, end, count, block_at, second, q2, sym, out):
    @pl.when((begin == 0) & (end > 0))
    def _():
        for j in range(PRODUCTS):
            second(block_at(j))

    def step(k, _):
        i = begin + k * PRODUCTS
        at = [block_at(i + j) for j in range(PRODUCTS)]
        for l in at:
            out[l] = coalesce(q2[l], sym)[0:BINS]
        for j in range(PRODUCTS):
            second(block_at(jnp.minimum(i + PRODUCTS + j, count - 1)))
        return 0

    lax.fori_loop(0, lax.div(end - begin, PRODUCTS), step, 0)


def upper_kernel(moved, scal, table, spectra, courant, sym, *rest):
    low_q1, low_c, face, out, scal_out, q0, cs, q1, fy, fz, q2 = rest[6 if moved else 0 :]
    for k in range(SCALARS):
        scal_out[k] = scal[k]
    here0, here = scal[HERE0], scal[HERE1] - scal[HERE0]
    count = scal[MID1] - scal[MID0] - here if moved else here

    def block_at(i):
        return i + jnp.where(i >= here0, here, 0) if moved else i + here0

    def gather(i, _):
        l = block_at(i)
        fetch(scal[MID0] + l, scal, spectra, courant, rest[:2] if moved else (), slice(0, CELLS), q0, cs, l)
        low_c[l] = cs[l, :, 0:HALF]
        return 0

    lax.fori_loop(0, count, gather, 0)

    def first(i):
        l = block_at(i)
        _, uy, uz = neighbours(table, l)
        q_prev = cx_prev = None
        for v in range(4):
            new = donor(q0, cs, l, v, q_prev, cx_prev, uy, uz)
            q_prev, cx_prev = read(q0, l, v), speed(cs, l, 0, v)
            if v < 2:
                low_q1[l, :, span(v)] = flat(new)
            else:
                q1[l, :, span(v - 2)] = flat(new)
        other = swap(new)
        face[RUN + l, 0:PACKED] = flat(jnp.where(upper(), limited(new, cx_prev, other), other))
        face[RUN + l, PACKED : 2 * PACKED] = flat(cx_prev * q_prev)

    several(0, count, first, STENCILS)
    cross_flux(count, block_at, table, q1, cs, fy, fz, 0, 2)

    def second(l):
        q_prev = read(low_q1, l, 1)
        f_prev = limited(q_prev, speed(cs, l, 0, 1), swap(q_prev))
        for w in range(2):
            q = read(q1, l, w)
            f = limited(q, speed(cs, l, 0, w + 2), swap(jnp.where(upper(), q_prev, q)))
            new = q - f + swap(jnp.where(upper(), f_prev, f)) + cross(table, l, fy, fz, w)
            q2[l, :, span(w)] = flat(new)
            q_prev, f_prev = q, f

    coalesce_all(0, count, count, block_at, second, q2, sym, out)


def upper_half(scal, table, spectra, courant, sym, *moved):
    capacity = spectra.shape[0]
    held = (capacity, PACKED, HALF)
    shapes = [held, (capacity, 24, HALF), (capacity + 2 * RUN, 2 * PACKED, LANES), (capacity, BINS, HALF)]
    return pl.pallas_call(
        functools.partial(upper_kernel, bool(moved)),
        in_specs=[SMEM, SMEM] + [VMEM] * 3 + ([VMEM] * 6 if moved else []),
        out_specs=[VMEM] * 4 + [SMEM],
        out_shape=[jax.ShapeDtypeStruct(shape, F32) for shape in shapes] + [jax.ShapeDtypeStruct((SCALARS,), jnp.int32)],
        scratch_shapes=[pltpu.VMEM((capacity, PACKED, CELLS), F32), pltpu.VMEM((capacity, 24, CELLS), F32)]
        + [pltpu.VMEM(held, F32)] * 4,
        input_output_aliases={7: 0, 8: 1, 9: 2, 10: 3} if moved else {},
        compiler_params=params(32),
        cost_estimate=pl.CostEstimate(flops=4 * 10**9, bytes_accessed=20 * 10**6, transcendentals=0),
    )(scal, table, spectra, courant, sym, *moved)


def lower_kernel(scal, table, _, cs, __, high_cells, in_pair, in_other, sym, result, pair, other, q1, face, low_cells, fy, fz, q2, blank, sems, blank_sems):
    count = scal[MID1] - scal[MID0]
    runs = lax.div(count, RUN)
    shift, slots = scal[MID0] - scal[NEW0], scal[NEW1] - scal[NEW0]

    def leave(half, act):
        source = (low_cells, high_cells)[half]
        cells = pl.ds(half * HALF, HALF)

        def body(r, _):
            first = r * RUN
            block = source.at[pl.ds(first, RUN)]

            def down(ref):
                act(pltpu.make_async_copy(block, ref.at[:, :, cells], sems.at[half, 0]))

            def up(ref):
                act(pltpu.make_async_copy(block, ref.at[:, :, cells], sems.at[half, 1]))

            by_side(scal, pair, other, down, up, r == 0, r == runs - 1)

            slot = first + shift
            fits = (slot >= 0) & (slot + RUN <= slots)

            @pl.when(fits)
            def _():
                act(pltpu.make_async_copy(block, result.at[pl.ds(slot, RUN), :, cells], sems.at[half, 2 + first]))

            def one(l, _):
                @pl.when((l + shift >= 0) & (l + shift < slots))
                def _():
                    act(pltpu.make_async_copy(source.at[l], result.at[l + shift, :, cells], sems.at[half, 2 + l]))

                return 0

            @pl.when(jnp.logical_not(fits))
            def _():
                lax.fori_loop(first, first + RUN, one, 0)

            return 0

        return body

    def start(copy):
        copy.start()

    def wait(copy):
        copy.wait()

    def clear(act):
        many = blank.shape[0]
        dead = result.shape[0] - slots
        whole = lax.div(dead, many)

        def chunk(k, _):
            at = slots + k * many
            act(pltpu.make_async_copy(blank, result.at[pl.ds(at, many)], blank_sems.at[k]))
            return 0

        lax.fori_loop(0, whole, chunk, 0)

        def one(s, _):
            act(pltpu.make_async_copy(blank.at[0], result.at[s], blank_sems.at[s]))
            return 0

        lax.fori_loop(slots + whole * many, result.shape[0], one, 0)

    lax.fori_loop(0, runs, leave(1, start), 0)
    blank[...] = jnp.zeros(blank.shape, F32)
    clear(start)

    def expand(base, ref):
        for i in range(RUN // 2):
            flux = ref[RUN + i]
            for k in (2 * i, 2 * i + 1):
                face[base + k, 0:PACKED] = ref[k]
            face[base + 2 * i, PACKED : 2 * PACKED] = pltpu.roll(flux, 64, 1)
            face[base + 2 * i + 1, PACKED : 2 * PACKED] = flux

    always = count > 0
    at_high = functools.partial(expand, count + RUN)
    by_side(scal, in_pair, in_other, functools.partial(expand, 0), at_high, always, always)

    def fix(l):
        ux, _, _ = neighbours(table, l)
        flux = swap(view(face[RUN + ux, PACKED : 2 * PACKED]))
        q1[l, :, span(0)] += flat(jnp.where(upper(), 0.0, flux))

    several(0, count, fix, STENCILS)
    cross_flux(count, lambda i: i, table, q1, cs, fy, fz, 0, 0)

    def second(l):
        side = view(face[RUN + neighbours(table, l)[0], 0:PACKED])
        q = read(q1, l, 0)
        f = limited(q, speed(cs, l, 0, 0), jnp.where(upper(), swap(q), side))
        q2[l, :, span(0)] = flat(q - f + swap(jnp.where(upper(), side, f)) + cross(table, l, fy, fz, 0))
        q_prev, f_prev = q, f
        q = read(q1, l, 1)
        f = limited(q, speed(cs, l, 0, 1), swap(jnp.where(upper(), q_prev, q)))
        q2[l, :, span(1)] = flat(q - f + swap(jnp.where(upper(), f_prev, f)) + cross(table, l, fy, fz, 1))

    def one_run(r, _):
        coalesce_all(r * RUN, r * RUN + RUN, count, lambda i: i, second, q2, sym, low_cells)
        leave(0, start)(r, 0)
        return 0

    lax.fori_loop(0, runs, one_run, 0)
    lax.fori_loop(0, runs, leave(0, wait), 0)
    lax.fori_loop(0, runs, leave(1, wait), 0)
    clear(wait)


def lower_half(scal, table, arrays, in_pair, in_other, sym):
    capacity = arrays[0].shape[0]
    whole = jax.ShapeDtypeStruct((capacity, BINS, CELLS), F32)
    sent = jax.ShapeDtypeStruct((RUN, BINS, CELLS), F32)
    held = pltpu.VMEM((capacity, PACKED, HALF), F32)
    return pl.pallas_call(
        lower_kernel,
        in_specs=[SMEM, SMEM] + [VMEM] * 7,
        out_specs=[ANY] * 3 + [VMEM] * 2,
        out_shape=[whole, sent, sent] + [jax.ShapeDtypeStruct(x.shape, F32) for x in (arrays[0], arrays[2])],
        input_output_aliases={2: 3, 4: 4},
        scratch_shapes=[
            pltpu.VMEM((capacity, BINS, HALF), F32),
            held,
            held,
            held,
            pltpu.VMEM((4, BINS, CELLS), F32),
            pltpu.SemaphoreType.DMA((2, capacity + 2)),
            pltpu.SemaphoreType.DMA((capacity,)),
        ],
        compiler_params=params(30),
        cost_estimate=pl.CostEstimate(flops=8 * 10**9, bytes_accessed=20 * 10**6, transcendentals=0),
    )(scal, table, *arrays, in_pair, in_other, sym)[:3]


def place_moved_kernel(scal, pair, other, _, out, sems):
    first, end = scal[NEW0], scal[NEW1]

    def copies(act):
        for k in range(RUN):
            low, high = scal[MID0] - RUN + k, scal[MID1] + k

            def from_low(ref, k=k, low=low):
                act(pltpu.make_async_copy(ref.at[k], out.at[low - first], sems.at[0, k]))

            def from_high(ref, k=k, high=high):
                act(pltpu.make_async_copy(ref.at[k], out.at[high - first], sems.at[1, k]))

            low_in = (low >= first) & (low < end)
            high_in = (high >= first) & (high < end)
            by_side(scal, pair, other, from_low, from_high, low_in, high_in)

    copies(lambda copy: copy.start())
    copies(lambda copy: copy.wait())


def place_moved(scal, pair, other, out):
    return pl.pallas_call(
        place_moved_kernel,
        in_specs=[SMEM, VMEM, VMEM, ANY],
        out_specs=ANY,
        out_shape=jax.ShapeDtypeStruct(out.shape, F32),
        scratch_shapes=[pltpu.SemaphoreType.DMA((2, RUN))],
        input_output_aliases={3: 0},
        compiler_params=params(8),
    )(scal, pair, other, out)


def bounds_kernel(device, old_count, new_count, out):
    ids = lax.broadcasted_iota(jnp.int32, old_count.shape, 1)

    def total(counts, p):
        return jnp.sum(jnp.where(ids < p, counts[...], 0).astype(F32)).astype(jnp.int32)

    def start(p):
        old, new = total(old_count, p), total(new_count, p)
        least = lax.div(jnp.maximum(old, new) + RUN - 1, RUN) * RUN - RUN
        most = lax.div(jnp.minimum(old, new), RUN) * RUN + RUN
        return old, jnp.clip(2 * RUN * p, least, most), new

    old0, mid0, new0 = start(device[0])
    old1, mid1, new1 = start(device[0] + 1)
    out[OLD0], out[OLD1], out[MID0], out[MID1], out[NEW0], out[NEW1] = old0, old1, mid0, mid1, new0, new1
    here0 = lax.div(jnp.maximum(old0 - mid0, 0) + RUN - 1, RUN) * RUN
    here1 = lax.div(jnp.minimum(old1, mid1) - mid0, RUN) * RUN
    out[ODD] = lax.rem(device[0], 2)
    out[HERE0], out[HERE1] = here0, jnp.clip(here1, here0, here0 + RUN)


def bounds(device, old_count, new_count):
    return pl.pallas_call(
        bounds_kernel,
        in_specs=[SMEM, VMEM, VMEM],
        out_specs=SMEM,
        out_shape=jax.ShapeDtypeStruct((SCALARS,), jnp.int32),
    )(device, old_count.reshape(1, -1), new_count.reshape(1, -1))


def on_device(devices, spectra, courant, kernel, old_count, new_count, upwind):
    device = lax.axis_index("blocks").astype(jnp.int32).reshape(1)
    pairs = [(i, i ^ 1) for i in range(devices)]
    others = [(i, i + 1) for i in range(1, devices - 1, 2)]
    others += [(j, i) for i, j in others]
    ends = [(devices - 1, 0), (0, devices - 1)]

    def exchange(pair, other, route):
        from_other = lax.ppermute(other, "blocks", route)
        return lax.ppermute(pair, "blocks", pairs), from_other

    courant = jnp.swapaxes(courant, 0, 1)
    moved = exchange(*pack(old_count, device, spectra, courant), others)
    scal = bounds(device, old_count, new_count)
    table = upwind[RUN : 2 * RUN].reshape(-1)
    sym = symmetric_kernel(kernel)
    *early, scal = upper_half(scal, table, spectra, courant, sym)
    *sides, scal = faces(scal, table, spectra, courant, *moved, early[2])
    sides = exchange(*sides, others + ends)
    *arrays, scal = upper_half(scal, table, spectra, courant, sym, *moved, *early)
    result, *results = lower_half(scal, table, arrays, *sides, sym)
    return place_moved(scal, *exchange(*results, others), result)


def solution(mesh):
    in_specs = (P("blocks", None, None), P("blocks", None, None), P(), P(), P(), P())
    out_specs = P("blocks", None, None)
    return jax.shard_map(
        functools.partial(on_device, mesh.shape["blocks"]),
        mesh=mesh,
        in_specs=in_specs,
        out_specs=out_specs,
        check_vma=False,
    )
```

```python
import functools

import jax
import jax.numpy as jnp
import numpy as np
from jax import lax
from jax.experimental import pallas as pl
from jax.experimental.pallas import tpu as pltpu
from jax.sharding import PartitionSpec as P

RUN = 12
BINS = 66
CELLS = 512
HALF = 256
LANES = 128
PACKED = 72
FULL = 64
TERMS = 2304
GROUPS = 9
STENCILS = 6
PRODUCTS = 2
FACES = 18
F32 = jnp.float32
VMEM = pl.BlockSpec(memory_space=pltpu.VMEM)
SMEM = pl.BlockSpec(memory_space=pltpu.SMEM)
OLD0, OLD1, MID0, MID1, NEW0, NEW1, HERE0, HERE1, ODD = range(9)
SCALARS = 9
ANY = pl.BlockSpec(memory_space=pl.ANY)


def params(mib):
    return pltpu.CompilerParams(vmem_limit_bytes=mib * 2**20)


def lanes():
    return lax.broadcasted_iota(jnp.int32, (8, LANES), 1)


def span(v):
    return slice(v * LANES, (v + 1) * LANES)


def upper():
    return lanes() >= 64


def last_y():
    return lanes() // 8 % 8 == 7


def last_z():
    return lanes() % 8 == 7


def view(x):
    return x.reshape(GROUPS, 8, LANES)


def flat(x):
    return x.reshape(PACKED, LANES)


def swap(x):
    return pltpu.roll(flat(x), 64, 1).reshape(x.shape)


def permuted(x, source):
    return view(jnp.take_along_axis(flat(x), source, axis=1, mode="promise_in_bounds"))


def wide_lanes():
    return lax.broadcasted_iota(jnp.int32, (PACKED, LANES), 1)


def step_y(x):
    at = wide_lanes()
    return permuted(x, jnp.where(at // 8 % 8 == 0, at + 56, at - 8))


def step_z(x):
    at = wide_lanes()
    return permuted(x, jnp.where(at % 8 == 0, at + 7, at - 1))


def minmod(a, e):
    return jnp.maximum(jnp.minimum(a, e), 0.0)


def limited(q, c, before):
    return c * (q + (0.5 * (1.0 - c)) * minmod(q - before, q))


def upwind_of(table, position):
    back = table[3 * position] < RUN + position
    return back, table[3 * position + 1] - RUN, table[3 * position + 2] - RUN


def by_side(scal, pair, other, act_low, act_high, is_low, is_high):
    odd = scal[ODD] == 1
    for mine, low, high in ((odd, pair, other), (jnp.logical_not(odd), other, pair)):
        pl.when(mine & is_low)(functools.partial(act_low, low))
        pl.when(mine & is_high)(functools.partial(act_high, high))


def read(ref, l, v):
    return view(ref[l, :, span(v)])


def speed(ref, l, d, v):
    return ref[l, 8 * d : 8 * d + 8, span(v)]


def donor(q0, cs, l, v, q_prev, cx_prev, uy, uz):
    q, cx, cy, cz = read(q0, l, v), speed(cs, l, 0, v), speed(cs, l, 1, v), speed(cs, l, 2, v)
    up, ly, lz = upper(), last_y(), last_z()
    in_x = swap(jnp.where(up, 0.0 if q_prev is None else cx_prev * q_prev, cx * q))
    in_y = step_y(jnp.where(ly, speed(cs, uy, 1, v), cy) * jnp.where(ly, read(q0, uy, v), q))
    in_z = step_z(jnp.where(lz, speed(cs, uz, 2, v), cz) * jnp.where(lz, read(q0, uz, v), q))
    return (1.0 - (cx + cy + cz)) * q + in_x + in_y + in_z


def fetch(block, scal, spectra, courant, moved, cells, q_dst, c_dst, at):
    own0, own1 = scal[OLD0], scal[OLD1]

    def spread(d, row):
        c_dst[at, 8 * d : 8 * d + 8] = jnp.broadcast_to(row, (8, row.shape[1]))

    def owned():
        q_dst[at, 0:BINS] = spectra[block - own0, :, cells]
        for d in range(3):
            spread(d, courant[d, pl.ds(block - own0, 1), cells])

    if not moved:
        owned()
        return
    pl.when((block >= own0) & (block < own1))(owned)

    def received(i, ref):
        q_dst[at] = ref[i, :, cells]
        for d in range(3):
            spread(d, ref[i, BINS + d : BINS + d + 1, cells])

    from_low = functools.partial(received, block - own0 + RUN)
    from_high = functools.partial(received, block - own1)
    by_side(scal, *moved, from_low, from_high, block < own0, block >= own1)


def pack_kernel(old_count, device, spectra, courant, pair, other, raw, speeds, joined, c_sem, in_sems, out_sems):
    tail = old_count[device[0]] - RUN
    odd = lax.rem(device[0], 2) == 1
    all_speeds = pltpu.make_async_copy(courant, speeds, c_sem)
    all_speeds.start()
    steps = [(k, side) for k in range(0, RUN, 2) for side in (0, 1)]
    starts = (tail, 0)

    def arrival(k, side):
        return pltpu.make_async_copy(
            spectra.at[pl.ds(starts[side] + k, 2)], raw.at[side, pl.ds(k, 2)], in_sems.at[side, k]
        )

    def leave(k, side, act):
        def to(out):
            act(pltpu.make_async_copy(joined.at[side, pl.ds(k, 2)], out.at[pl.ds(k, 2)], out_sems.at[side, k]))

        pl.when(odd)(functools.partial(to, (other, pair)[side]))
        pl.when(jnp.logical_not(odd))(functools.partial(to, (pair, other)[side]))

    for k, side in steps:
        arrival(k, side).start()
    all_speeds.wait()
    for k, side in steps:
        arrival(k, side).wait()
        for i in (k, k + 1):
            joined[side, i, 0:BINS] = raw[side, i]
            for d in range(3):
                joined[side, i, BINS + d : BINS + d + 1] = speeds[d, pl.ds(starts[side] + i, 1)]
        leave(k, side, lambda copy: copy.start())
    for k, side in steps:
        leave(k, side, lambda copy: copy.wait())


def pack(old_count, device, spectra, courant):
    sent = jax.ShapeDtypeStruct((RUN, PACKED, CELLS), F32)
    return pl.pallas_call(
        pack_kernel,
        in_specs=[SMEM, SMEM, ANY, ANY],
        out_specs=[ANY, ANY],
        out_shape=[sent, sent],
        scratch_shapes=[
            pltpu.VMEM((2, RUN, BINS, CELLS), F32),
            pltpu.VMEM(courant.shape, F32),
            pltpu.VMEM((2, RUN, PACKED, CELLS), F32),
            pltpu.SemaphoreType.DMA(()),
            pltpu.SemaphoreType.DMA((2, RUN)),
            pltpu.SemaphoreType.DMA((2, RUN)),
        ],
        compiler_params=params(56),
    )(old_count, device, spectra, courant)


def face_kernel(scal, table, spectra, courant, in_pair, in_other, early, pair, other, scal_out, q0, cs, up, down):
    count = scal[MID1] - scal[MID0]
    for k in range(SCALARS):
        scal_out[k] = scal[k]

    def face(j):
        _, y, z = upwind_of(table, j)
        q1 = donor(q0, cs, j, 1, read(q0, j, 0), speed(cs, j, 0, 0), y, z)
        side = swap(q1)
        c = speed(cs, j, 0, 1)
        return jnp.where(upper(), limited(q1, c, side), side), c * read(q0, j, 1)

    def one_run(start, out):
        was_early = (start >= scal[HERE0]) & (start < scal[HERE1])

        def put(i, a0, b0, a1, b1):
            out[2 * i] = flat(a0)
            out[2 * i + 1] = flat(a1)
            out[RUN + i] = flat(jnp.where(upper(), b1, swap(b0)))

        def take(i, _):
            at = start + 2 * i
            parts = [view(early[RUN + l, k : k + PACKED]) for l in (at, at + 1) for k in (0, PACKED)]
            put(i, *parts)
            return 0

        def gather(j, _):
            block = scal[MID0] + start + j
            fetch(block, scal, spectra, courant, (in_pair, in_other), slice(HALF, CELLS), q0, cs, j)
            return 0

        def make(i, _):
            put(i, *face(2 * i), *face(2 * i + 1))
            return 0

        @pl.when(was_early)
        def _():
            lax.fori_loop(0, RUN // 2, take, 0)

        @pl.when(jnp.logical_not(was_early))
        def _():
            lax.fori_loop(0, RUN, gather, 0)
            lax.fori_loop(0, RUN // 2, make, 0)

    one_run(0, down)
    one_run(count - RUN, up)
    odd = scal[ODD] == 1

    @pl.when(odd)
    def _():
        pair[...] = down[...]
        other[...] = up[...]

    @pl.when(jnp.logical_not(odd))
    def _():
        pair[...] = up[...]
        other[...] = down[...]


def faces(scal, table, spectra, courant, in_pair, in_other, early):
    sent = jax.ShapeDtypeStruct((FACES, PACKED, LANES), F32)
    return pl.pallas_call(
        face_kernel,
        in_specs=[SMEM, SMEM] + [VMEM] * 5,
        out_specs=[VMEM, VMEM, SMEM],
        out_shape=[sent, sent, jax.ShapeDtypeStruct((SCALARS,), jnp.int32)],
        scratch_shapes=[
            pltpu.VMEM((RUN, PACKED, HALF), F32),
            pltpu.VMEM((RUN, 24, HALF), F32),
            pltpu.VMEM(sent.shape, F32),
            pltpu.VMEM(sent.shape, F32),
        ],
        compiler_params=params(10),
    )(scal, table, spectra, courant, in_pair, in_other, early)


def pair_terms(q):
    wide = q.shape[1]
    group = [q[8 * g : 8 * g + 8, :] for g in range(8)]
    row = [jnp.broadcast_to(q[i : i + 1, :], (8, wide)) for i in range(BINS)]
    out = [row[i] * group[g] for i in range(56) for g in range(i // 8 + 1, 8)]
    out += [row[i] * group[g] for i in (64, 65) for g in range(8)]
    for s in range(5):
        out += [x * (pltpu.roll(x, s, 0) if s else x) for x in group]
    at = lax.broadcasted_iota(jnp.int32, (8, wide), 0)
    rest = jnp.where(at < 2, row[64], row[65]) * jnp.where(at < 1, row[64], row[65])
    out.append(jnp.where(at < 3, rest, 0.0))
    return out + [jnp.zeros((8, wide), F32)] * (TERMS // 8 - len(out))


def pair_columns():
    pairs = [(i, j) for i in range(56) for j in range(i // 8 * 8 + 8, FULL)]
    pairs += [(i, j) for i in (64, 65) for j in range(FULL)]
    for s in range(5):
        for g in range(0, FULL, 8):
            pairs += [(g + r, g + (r - s) % 8) if s < 4 or r < 4 else None for r in range(8)]
    pairs += [(64, 64), (64, 65), (65, 65)]
    pairs += [None] * (TERMS - len(pairs))
    one = [p[0] * BINS + p[1] if p else -1 for p in pairs]
    two = [p[1] * BINS + p[0] if p and p[0] != p[1] else -1 for p in pairs]
    return np.array([one, two], np.int32)


def symmetric_kernel_body(columns, kernel, out):
    width = out.shape[1]
    row = lax.broadcasted_iota(jnp.int32, (256, width), 0).astype(F32).astype(jnp.bfloat16)
    picks = []
    for base in range(0, kernel.shape[1], 256):
        near = jnp.clip(columns[...] - base, -1, 256).astype(F32).astype(jnp.bfloat16)
        hit = (row == near[0:1]) | (row == near[1:2])
        picks.append(jnp.where(hit, jnp.bfloat16(1), jnp.bfloat16(0)))
    total = jnp.dot(kernel[...], jnp.concatenate(picks, axis=0), preferred_element_type=F32)
    out[...] = total.astype(jnp.bfloat16)


def symmetric_kernel(kernel):
    wide = -(-kernel.shape[1] // 256) * 256
    padded = jnp.pad(kernel, ((0, 80 - BINS), (0, wide - kernel.shape[1])))
    return pl.pallas_call(
        symmetric_kernel_body,
        grid=(TERMS // 256,),
        in_specs=[
            pl.BlockSpec((2, 256), lambda i: (0, i)),
            pl.BlockSpec((80, wide), lambda i: (0, 0)),
        ],
        out_specs=pl.BlockSpec((80, 256), lambda i: (0, i)),
        out_shape=jax.ShapeDtypeStruct((80, TERMS), jnp.bfloat16),
        compiler_params=params(16),
        cost_estimate=pl.CostEstimate(flops=2 * 10**9, bytes_accessed=10**6, transcendentals=0),
    )(jnp.asarray(pair_columns()), padded)


def coalesce(q, sym):
    terms = pair_terms(q)
    packed = [
        jnp.concatenate(terms[2 * r : 2 * r + 2], axis=0).astype(jnp.bfloat16) for r in range(TERMS // 16)
    ]
    gained = jnp.dot(sym[...], jnp.concatenate(packed, axis=0), preferred_element_type=F32)
    return q + gained[0:PACKED]


def several(begin, end, body, at_once):
    def step(k, _):
        for j in range(at_once):
            body(begin + k * at_once + j)
        return 0

    lax.fori_loop(0, lax.div(end - begin, at_once), step, 0)


def neighbours(table, l):
    position = lax.rem(l, RUN)
    back, y, z = upwind_of(table, position)
    return jnp.where(back, l - RUN, l + RUN), y + (l - position), z + (l - position)


def cross_flux(count, block_at, table, q1, cs, fy, fz, v0, vf):
    def cross_body(i):
        l = block_at(i)
        _, uy, uz = neighbours(table, l)
        for w in range(2):
            q = read(q1, l, v0 + w)
            before_y = step_y(jnp.where(last_y(), read(q1, uy, v0 + w), q))
            before_z = step_z(jnp.where(last_z(), read(q1, uz, v0 + w), q))
            fy[l, :, span(w)] = flat(limited(q, speed(cs, l, 1, vf + w), before_y))
            fz[l, :, span(w)] = flat(limited(q, speed(cs, l, 2, vf + w), before_z))

    several(0, count, cross_body, STENCILS)


def cross(table, l, fy, fz, w):
    _, uy, uz = neighbours(table, l)
    y_own, z_own = read(fy, l, w), read(fz, l, w)
    y_in = step_y(jnp.where(last_y(), read(fy, uy, w), y_own))
    z_in = step_z(jnp.where(last_z(), read(fz, uz, w), z_own))
    return (y_in - y_own) + (z_in - z_own)


def coalesce_all(begin, end, count, block_at, second, q2, sym, out):
    @pl.when((begin == 0) & (end > 0))
    def _():
        for j in range(PRODUCTS):
            second(block_at(j))

    def step(k, _):
        i = begin + k * PRODUCTS
        at = [block_at(i + j) for j in range(PRODUCTS)]
        for l in at:
            out[l] = coalesce(q2[l], sym)[0:BINS]
        for j in range(PRODUCTS):
            second(block_at(jnp.minimum(i + PRODUCTS + j, count - 1)))
        return 0

    lax.fori_loop(0, lax.div(end - begin, PRODUCTS), step, 0)


def upper_kernel(moved, scal, table, spectra, courant, sym, *rest):
    rest_out = rest[6 if moved else 0 :]
    low_q1, low_c, face, out, scal_out = rest_out[:5]
    pair, other = rest_out[5:7] if moved else (None, None)
    q0, cs, q1, fy, fz, q2, sems = rest_out[7 if moved else 5 :]
    for k in range(SCALARS):
        scal_out[k] = scal[k]
    here0, here = scal[HERE0], scal[HERE1] - scal[HERE0]
    count = scal[MID1] - scal[MID0] - here if moved else here

    def block_at(i):
        return i + jnp.where(i >= here0, here, 0) if moved else i + here0

    def gather(i, _):
        l = block_at(i)
        fetch(scal[MID0] + l, scal, spectra, courant, rest[:2] if moved else (), slice(0, CELLS), q0, cs, l)
        low_c[l] = cs[l, :, 0:HALF]
        return 0

    lax.fori_loop(0, count, gather, 0)

    def first(i):
        l = block_at(i)
        _, uy, uz = neighbours(table, l)
        q_prev = cx_prev = None
        for v in range(4):
            new = donor(q0, cs, l, v, q_prev, cx_prev, uy, uz)
            q_prev, cx_prev = read(q0, l, v), speed(cs, l, 0, v)
            if v < 2:
                low_q1[l, :, span(v)] = flat(new)
            else:
                q1[l, :, span(v - 2)] = flat(new)
        other = swap(new)
        face[RUN + l, 0:PACKED] = flat(jnp.where(upper(), limited(new, cx_prev, other), other))
        face[RUN + l, PACKED : 2 * PACKED] = flat(cx_prev * q_prev)

    several(0, count, first, STENCILS)
    cross_flux(count, block_at, table, q1, cs, fy, fz, 0, 2)

    def second(l):
        q_prev = read(low_q1, l, 1)
        f_prev = limited(q_prev, speed(cs, l, 0, 1), swap(q_prev))
        for w in range(2):
            q = read(q1, l, w)
            f = limited(q, speed(cs, l, 0, w + 2), swap(jnp.where(upper(), q_prev, q)))
            new = q - f + swap(jnp.where(upper(), f_prev, f)) + cross(table, l, fy, fz, w)
            q2[l, :, span(w)] = flat(new)
            q_prev, f_prev = q, f

    coalesce_all(0, count, count, block_at, second, q2, sym, out)
    if not moved:
        return
    whole = scal[MID1] - scal[MID0]

    def leave(act):
        def down(ref):
            act(pltpu.make_async_copy(out.at[pl.ds(0, RUN)], ref, sems.at[0]))

        def up(ref):
            act(pltpu.make_async_copy(out.at[pl.ds(whole - RUN, RUN)], ref, sems.at[1]))

        by_side(scal, pair, other, down, up, whole > 0, whole > 0)

    leave(lambda copy: copy.start())
    leave(lambda copy: copy.wait())


def upper_half(scal, table, spectra, courant, sym, *moved):
    capacity = spectra.shape[0]
    held = (capacity, PACKED, HALF)
    shapes = [held, (capacity, 24, HALF), (capacity + 2 * RUN, 2 * PACKED, LANES), (capacity, BINS, HALF)]
    return pl.pallas_call(
        functools.partial(upper_kernel, bool(moved)),
        in_specs=[SMEM, SMEM] + [VMEM] * 3 + ([VMEM] * 6 if moved else []),
        out_specs=[VMEM] * 4 + [SMEM] + ([ANY] * 2 if moved else []),
        out_shape=[jax.ShapeDtypeStruct(shape, F32) for shape in shapes]
        + [jax.ShapeDtypeStruct((SCALARS,), jnp.int32)]
        + ([jax.ShapeDtypeStruct((RUN, BINS, HALF), F32)] * 2 if moved else []),
        scratch_shapes=[pltpu.VMEM((capacity, PACKED, CELLS), F32), pltpu.VMEM((capacity, 24, CELLS), F32)]
        + [pltpu.VMEM(held, F32)] * 4
        + [pltpu.SemaphoreType.DMA((2,))],
        input_output_aliases={7: 0, 8: 1, 9: 2, 10: 3} if moved else {},
        compiler_params=params(32),
        cost_estimate=pl.CostEstimate(flops=4 * 10**9, bytes_accessed=20 * 10**6, transcendentals=0),
    )(scal, table, spectra, courant, sym, *moved)


def lower_kernel(scal, table, _, cs, __, high_cells, in_pair, in_other, sym, result, pair, other, q1, face, low_cells, fy, fz, q2, blank, sems, blank_sems):
    count = scal[MID1] - scal[MID0]
    runs = lax.div(count, RUN)
    shift, slots = scal[MID0] - scal[NEW0], scal[NEW1] - scal[NEW0]

    def leave(half, act):
        source = (low_cells, high_cells)[half]
        cells = pl.ds(half * HALF, HALF)

        def body(r, _):
            first = r * RUN
            block = source.at[pl.ds(first, RUN)]

            def down(ref):
                act(pltpu.make_async_copy(block, ref, sems.at[half, 0]))

            def up(ref):
                act(pltpu.make_async_copy(block, ref, sems.at[half, 1]))

            if half == 0:
                by_side(scal, pair, other, down, up, r == 0, r == runs - 1)

            slot = first + shift
            fits = (slot >= 0) & (slot + RUN <= slots)

            @pl.when(fits)
            def _():
                act(pltpu.make_async_copy(block, result.at[pl.ds(slot, RUN), :, cells], sems.at[half, 2 + first]))

            def one(l, _):
                @pl.when((l + shift >= 0) & (l + shift < slots))
                def _():
                    act(pltpu.make_async_copy(source.at[l], result.at[l + shift, :, cells], sems.at[half, 2 + l]))

                return 0

            @pl.when(jnp.logical_not(fits))
            def _():
                lax.fori_loop(first, first + RUN, one, 0)

            return 0

        return body

    def start(copy):
        copy.start()

    def wait(copy):
        copy.wait()

    def clear(act):
        many = blank.shape[0]
        dead = result.shape[0] - slots
        whole = lax.div(dead, many)

        def chunk(k, _):
            at = slots + k * many
            act(pltpu.make_async_copy(blank, result.at[pl.ds(at, many)], blank_sems.at[k]))
            return 0

        lax.fori_loop(0, whole, chunk, 0)

        def one(s, _):
            act(pltpu.make_async_copy(blank.at[0], result.at[s], blank_sems.at[s]))
            return 0

        lax.fori_loop(slots + whole * many, result.shape[0], one, 0)

    lax.fori_loop(0, runs, leave(1, start), 0)
    blank[...] = jnp.zeros(blank.shape, F32)
    clear(start)

    def expand(base, ref):
        for i in range(RUN // 2):
            flux = ref[RUN + i]
            for k in (2 * i, 2 * i + 1):
                face[base + k, 0:PACKED] = ref[k]
            face[base + 2 * i, PACKED : 2 * PACKED] = pltpu.roll(flux, 64, 1)
            face[base + 2 * i + 1, PACKED : 2 * PACKED] = flux

    always = count > 0
    at_high = functools.partial(expand, count + RUN)
    by_side(scal, in_pair, in_other, functools.partial(expand, 0), at_high, always, always)

    def fix(l):
        ux, _, _ = neighbours(table, l)
        flux = swap(view(face[RUN + ux, PACKED : 2 * PACKED]))
        q1[l, :, span(0)] += flat(jnp.where(upper(), 0.0, flux))

    several(0, count, fix, STENCILS)
    cross_flux(count, lambda i: i, table, q1, cs, fy, fz, 0, 0)

    def second(l):
        side = view(face[RUN + neighbours(table, l)[0], 0:PACKED])
        q = read(q1, l, 0)
        f = limited(q, speed(cs, l, 0, 0), jnp.where(upper(), swap(q), side))
        q2[l, :, span(0)] = flat(q - f + swap(jnp.where(upper(), side, f)) + cross(table, l, fy, fz, 0))
        q_prev, f_prev = q, f
        q = read(q1, l, 1)
        f = limited(q, speed(cs, l, 0, 1), swap(jnp.where(upper(), q_prev, q)))
        q2[l, :, span(1)] = flat(q - f + swap(jnp.where(upper(), f_prev, f)) + cross(table, l, fy, fz, 1))

    def one_run(r, _):
        coalesce_all(r * RUN, r * RUN + RUN, count, lambda i: i, second, q2, sym, low_cells)
        leave(0, start)(r, 0)
        return 0

    lax.fori_loop(0, runs, one_run, 0)
    lax.fori_loop(0, runs, leave(0, wait), 0)
    lax.fori_loop(0, runs, leave(1, wait), 0)
    clear(wait)


def lower_half(scal, table, arrays, in_pair, in_other, sym):
    capacity = arrays[0].shape[0]
    whole = jax.ShapeDtypeStruct((capacity, BINS, CELLS), F32)
    sent = jax.ShapeDtypeStruct((RUN, BINS, HALF), F32)
    held = pltpu.VMEM((capacity, PACKED, HALF), F32)
    return pl.pallas_call(
        lower_kernel,
        in_specs=[SMEM, SMEM] + [VMEM] * 7,
        out_specs=[ANY] * 3 + [VMEM] * 2,
        out_shape=[whole, sent, sent] + [jax.ShapeDtypeStruct(x.shape, F32) for x in (arrays[0], arrays[2])],
        input_output_aliases={2: 3, 4: 4},
        scratch_shapes=[
            pltpu.VMEM((capacity, BINS, HALF), F32),
            held,
            held,
            held,
            pltpu.VMEM((4, BINS, CELLS), F32),
            pltpu.SemaphoreType.DMA((2, capacity + 2)),
            pltpu.SemaphoreType.DMA((capacity,)),
        ],
        compiler_params=params(30),
        cost_estimate=pl.CostEstimate(flops=8 * 10**9, bytes_accessed=20 * 10**6, transcendentals=0),
    )(scal, table, *arrays, in_pair, in_other, sym)[:3]


def place_moved_kernel(scal, *rest):
    halves, out, sems = (rest[0:2], rest[2:4]), rest[5], rest[6]
    first, end = scal[NEW0], scal[NEW1]

    def copies(act):
        for half in range(2):
            cells = pl.ds(half * HALF, HALF)
            for k in range(RUN):
                low, high = scal[MID0] - RUN + k, scal[MID1] + k

                def put(side, block, ref, k=k, half=half, cells=cells):
                    act(pltpu.make_async_copy(ref.at[k], out.at[block - first, :, cells], sems.at[half, side, k]))

                low_in = (low >= first) & (low < end)
                high_in = (high >= first) & (high < end)
                from_low, from_high = functools.partial(put, 0, low), functools.partial(put, 1, high)
                by_side(scal, *halves[half], from_low, from_high, low_in, high_in)

    copies(lambda copy: copy.start())
    copies(lambda copy: copy.wait())


def place_moved(scal, lower, upper_, out):
    return pl.pallas_call(
        place_moved_kernel,
        in_specs=[SMEM] + [VMEM] * 4 + [ANY],
        out_specs=ANY,
        out_shape=jax.ShapeDtypeStruct(out.shape, F32),
        scratch_shapes=[pltpu.SemaphoreType.DMA((2, 2, RUN))],
        input_output_aliases={5: 0},
        compiler_params=params(8),
    )(scal, *lower, *upper_, out)


def bounds_kernel(device, old_count, new_count, out):
    ids = lax.broadcasted_iota(jnp.int32, old_count.shape, 1)

    def total(counts, p):
        return jnp.sum(jnp.where(ids < p, counts[...], 0).astype(F32)).astype(jnp.int32)

    def start(p):
        old, new = total(old_count, p), total(new_count, p)
        least = lax.div(jnp.maximum(old, new) + RUN - 1, RUN) * RUN - RUN
        most = lax.div(jnp.minimum(old, new), RUN) * RUN + RUN
        return old, jnp.clip(2 * RUN * p, least, most), new

    old0, mid0, new0 = start(device[0])
    old1, mid1, new1 = start(device[0] + 1)
    out[OLD0], out[OLD1], out[MID0], out[MID1], out[NEW0], out[NEW1] = old0, old1, mid0, mid1, new0, new1
    here0 = lax.div(jnp.maximum(old0 - mid0, 0) + RUN - 1, RUN) * RUN
    here1 = lax.div(jnp.minimum(old1, mid1) - mid0, RUN) * RUN
    out[ODD] = lax.rem(device[0], 2)
    out[HERE0], out[HERE1] = here0, jnp.clip(here1, here0, here0 + RUN)


def bounds(device, old_count, new_count):
    return pl.pallas_call(
        bounds_kernel,
        in_specs=[SMEM, VMEM, VMEM],
        out_specs=SMEM,
        out_shape=jax.ShapeDtypeStruct((SCALARS,), jnp.int32),
    )(device, old_count.reshape(1, -1), new_count.reshape(1, -1))


def on_device(devices, spectra, courant, kernel, old_count, new_count, upwind):
    device = lax.axis_index("blocks").astype(jnp.int32).reshape(1)
    pairs = [(i, i ^ 1) for i in range(devices)]
    others = [(i, i + 1) for i in range(1, devices - 1, 2)]
    others += [(j, i) for i, j in others]
    ends = [(devices - 1, 0), (0, devices - 1)]

    def exchange(pair, other, route):
        from_other = lax.ppermute(other, "blocks", route)
        return lax.ppermute(pair, "blocks", pairs), from_other

    courant = jnp.swapaxes(courant, 0, 1)
    moved = exchange(*pack(old_count, device, spectra, courant), others)
    scal = bounds(device, old_count, new_count)
    table = upwind[RUN : 2 * RUN].reshape(-1)
    sym = symmetric_kernel(kernel)
    *early, scal = upper_half(scal, table, spectra, courant, sym)
    *sides, scal = faces(scal, table, spectra, courant, *moved, early[2])
    sides = exchange(*sides, others + ends)
    *arrays, scal, pair, other = upper_half(scal, table, spectra, courant, sym, *moved, *early)
    upper_results = exchange(pair, other, others)
    result, *results = lower_half(scal, table, arrays, *sides, sym)
    return place_moved(scal, exchange(*results, others), upper_results, result)


def solution(mesh):
    in_specs = (P("blocks", None, None), P("blocks", None, None), P(), P(), P(), P())
    out_specs = P("blocks", None, None)
    return jax.shard_map(
        functools.partial(on_device, mesh.shape["blocks"]),
        mesh=mesh,
        in_specs=in_specs,
        out_specs=out_specs,
        check_vma=False,
    )
```

```python
import functools

import jax
import jax.numpy as jnp
import numpy as np
from jax import lax
from jax.experimental import pallas as pl
from jax.experimental.pallas import tpu as pltpu
from jax.sharding import PartitionSpec as P

RUN = 12
BINS = 66
CELLS = 512
HALF = 256
LANES = 128
PACKED = 72
FULL = 64
TERMS = 2304
GROUPS = 9
STENCILS = 6
PRODUCTS = 2
FACES = 18
F32 = jnp.float32
VMEM = pl.BlockSpec(memory_space=pltpu.VMEM)
SMEM = pl.BlockSpec(memory_space=pltpu.SMEM)
OLD0, OLD1, MID0, MID1, NEW0, NEW1, HERE0, HERE1, ODD = range(9)
SCALARS = 9
ANY = pl.BlockSpec(memory_space=pl.ANY)


def params(mib):
    return pltpu.CompilerParams(vmem_limit_bytes=mib * 2**20)


def lanes():
    return lax.broadcasted_iota(jnp.int32, (8, LANES), 1)


def span(v):
    return slice(v * LANES, (v + 1) * LANES)


def upper():
    return lanes() >= 64


def last_y():
    return lanes() // 8 % 8 == 7


def last_z():
    return lanes() % 8 == 7


def view(x):
    return x.reshape(GROUPS, 8, LANES)


def flat(x):
    return x.reshape(PACKED, LANES)


def swap(x):
    return pltpu.roll(flat(x), 64, 1).reshape(x.shape)


def permuted(x, source):
    return view(jnp.take_along_axis(flat(x), source, axis=1, mode="promise_in_bounds"))


def wide_lanes():
    return lax.broadcasted_iota(jnp.int32, (PACKED, LANES), 1)


def step_y(x):
    at = wide_lanes()
    return permuted(x, jnp.where(at // 8 % 8 == 0, at + 56, at - 8))


def step_z(x):
    at = wide_lanes()
    return permuted(x, jnp.where(at % 8 == 0, at + 7, at - 1))


def minmod(a, e):
    return jnp.maximum(jnp.minimum(a, e), 0.0)


def limited(q, c, before):
    return c * (q + (0.5 * (1.0 - c)) * minmod(q - before, q))


def upwind_of(table, position):
    back = table[3 * position] < RUN + position
    return back, table[3 * position + 1] - RUN, table[3 * position + 2] - RUN


def by_side(scal, pair, other, act_low, act_high, is_low, is_high):
    odd = scal[ODD] == 1
    for mine, low, high in ((odd, pair, other), (jnp.logical_not(odd), other, pair)):
        pl.when(mine & is_low)(functools.partial(act_low, low))
        pl.when(mine & is_high)(functools.partial(act_high, high))


def read(ref, l, v):
    return view(ref[l, :, span(v)])


def speed(ref, l, d, v):
    return ref[l, 8 * d : 8 * d + 8, span(v)]


def donor(q0, cs, l, v, q_prev, cx_prev, uy, uz):
    q, cx, cy, cz = read(q0, l, v), speed(cs, l, 0, v), speed(cs, l, 1, v), speed(cs, l, 2, v)
    up, ly, lz = upper(), last_y(), last_z()
    in_x = swap(jnp.where(up, 0.0 if q_prev is None else cx_prev * q_prev, cx * q))
    in_y = step_y(jnp.where(ly, speed(cs, uy, 1, v), cy) * jnp.where(ly, read(q0, uy, v), q))
    in_z = step_z(jnp.where(lz, speed(cs, uz, 2, v), cz) * jnp.where(lz, read(q0, uz, v), q))
    return (1.0 - (cx + cy + cz)) * q + in_x + in_y + in_z


def fetch(block, scal, spectra, courant, moved, cells, q_dst, c_dst, at):
    own0, own1 = scal[OLD0], scal[OLD1]

    def spread(d, row):
        c_dst[at, 8 * d : 8 * d + 8] = jnp.broadcast_to(row, (8, row.shape[1]))

    def owned():
        q_dst[at, 0:BINS] = spectra[block - own0, :, cells]
        for d in range(3):
            spread(d, courant[d, pl.ds(block - own0, 1), cells])

    if not moved:
        owned()
        return
    pl.when((block >= own0) & (block < own1))(owned)

    def received(i, ref):
        q_dst[at] = ref[i, :, cells]
        for d in range(3):
            spread(d, ref[i, BINS + d : BINS + d + 1, cells])

    from_low = functools.partial(received, block - own0 + RUN)
    from_high = functools.partial(received, block - own1)
    by_side(scal, *moved, from_low, from_high, block < own0, block >= own1)


def pack_kernel(old_count, device, spectra, courant, pair, other, raw, speeds, joined, c_sem, in_sems, out_sems):
    tail = old_count[device[0]] - RUN
    odd = lax.rem(device[0], 2) == 1
    all_speeds = pltpu.make_async_copy(courant, speeds, c_sem)
    all_speeds.start()
    steps = [(k, side) for k in range(0, RUN, 2) for side in (0, 1)]
    starts = (tail, 0)

    def arrival(k, side):
        return pltpu.make_async_copy(
            spectra.at[pl.ds(starts[side] + k, 2)], raw.at[side, pl.ds(k, 2)], in_sems.at[side, k]
        )

    def leave(k, side, act):
        def to(out):
            act(pltpu.make_async_copy(joined.at[side, pl.ds(k, 2)], out.at[pl.ds(k, 2)], out_sems.at[side, k]))

        pl.when(odd)(functools.partial(to, (other, pair)[side]))
        pl.when(jnp.logical_not(odd))(functools.partial(to, (pair, other)[side]))

    for k, side in steps:
        arrival(k, side).start()
    all_speeds.wait()
    for k, side in steps:
        arrival(k, side).wait()
        for i in (k, k + 1):
            joined[side, i, 0:BINS] = raw[side, i]
            for d in range(3):
                joined[side, i, BINS + d : BINS + d + 1] = speeds[d, pl.ds(starts[side] + i, 1)]
        leave(k, side, lambda copy: copy.start())
    for k, side in steps:
        leave(k, side, lambda copy: copy.wait())


def pack(old_count, device, spectra, courant):
    sent = jax.ShapeDtypeStruct((RUN, PACKED, CELLS), F32)
    return pl.pallas_call(
        pack_kernel,
        in_specs=[SMEM, SMEM, ANY, ANY],
        out_specs=[ANY, ANY],
        out_shape=[sent, sent],
        scratch_shapes=[
            pltpu.VMEM((2, RUN, BINS, CELLS), F32),
            pltpu.VMEM(courant.shape, F32),
            pltpu.VMEM((2, RUN, PACKED, CELLS), F32),
            pltpu.SemaphoreType.DMA(()),
            pltpu.SemaphoreType.DMA((2, RUN)),
            pltpu.SemaphoreType.DMA((2, RUN)),
        ],
        compiler_params=params(56),
    )(old_count, device, spectra, courant)


def face_kernel(scal, table, spectra, courant, in_pair, in_other, early, pair, other, scal_out, q0, cs, up, down):
    count = scal[MID1] - scal[MID0]
    for k in range(SCALARS):
        scal_out[k] = scal[k]

    def face(j):
        _, y, z = upwind_of(table, j)
        q1 = donor(q0, cs, j, 1, read(q0, j, 0), speed(cs, j, 0, 0), y, z)
        side = swap(q1)
        c = speed(cs, j, 0, 1)
        return jnp.where(upper(), limited(q1, c, side), side), c * read(q0, j, 1)

    def one_run(start, out):
        was_early = (start >= scal[HERE0]) & (start < scal[HERE1])

        def put(i, a0, b0, a1, b1):
            out[2 * i] = flat(a0)
            out[2 * i + 1] = flat(a1)
            out[RUN + i] = flat(jnp.where(upper(), b1, swap(b0)))

        def take(i, _):
            at = start + 2 * i
            parts = [view(early[RUN + l, k : k + PACKED]) for l in (at, at + 1) for k in (0, PACKED)]
            put(i, *parts)
            return 0

        def gather(j, _):
            block = scal[MID0] + start + j
            fetch(block, scal, spectra, courant, (in_pair, in_other), slice(HALF, CELLS), q0, cs, j)
            return 0

        def make(i, _):
            put(i, *face(2 * i), *face(2 * i + 1))
            return 0

        @pl.when(was_early)
        def _():
            lax.fori_loop(0, RUN // 2, take, 0)

        @pl.when(jnp.logical_not(was_early))
        def _():
            lax.fori_loop(0, RUN, gather, 0)
            lax.fori_loop(0, RUN // 2, make, 0)

    one_run(0, down)
    one_run(count - RUN, up)
    odd = scal[ODD] == 1

    @pl.when(odd)
    def _():
        pair[...] = down[...]
        other[...] = up[...]

    @pl.when(jnp.logical_not(odd))
    def _():
        pair[...] = up[...]
        other[...] = down[...]


def faces(scal, table, spectra, courant, in_pair, in_other, early):
    sent = jax.ShapeDtypeStruct((FACES, PACKED, LANES), F32)
    return pl.pallas_call(
        face_kernel,
        in_specs=[SMEM, SMEM] + [VMEM] * 5,
        out_specs=[VMEM, VMEM, SMEM],
        out_shape=[sent, sent, jax.ShapeDtypeStruct((SCALARS,), jnp.int32)],
        scratch_shapes=[
            pltpu.VMEM((RUN, PACKED, HALF), F32),
            pltpu.VMEM((RUN, 24, HALF), F32),
            pltpu.VMEM(sent.shape, F32),
            pltpu.VMEM(sent.shape, F32),
        ],
        compiler_params=params(10),
    )(scal, table, spectra, courant, in_pair, in_other, early)


def pair_terms(q):
    wide = q.shape[1]
    group = [q[8 * g : 8 * g + 8, :] for g in range(8)]
    row = [jnp.broadcast_to(q[i : i + 1, :], (8, wide)) for i in range(BINS)]
    out = [row[i] * group[g] for i in range(56) for g in range(i // 8 + 1, 8)]
    out += [row[i] * group[g] for i in (64, 65) for g in range(8)]
    for s in range(5):
        out += [x * (pltpu.roll(x, s, 0) if s else x) for x in group]
    at = lax.broadcasted_iota(jnp.int32, (8, wide), 0)
    rest = jnp.where(at < 2, row[64], row[65]) * jnp.where(at < 1, row[64], row[65])
    out.append(jnp.where(at < 3, rest, 0.0))
    return out + [jnp.zeros((8, wide), F32)] * (TERMS // 8 - len(out))


def pair_columns():
    pairs = [(i, j) for i in range(56) for j in range(i // 8 * 8 + 8, FULL)]
    pairs += [(i, j) for i in (64, 65) for j in range(FULL)]
    for s in range(5):
        for g in range(0, FULL, 8):
            pairs += [(g + r, g + (r - s) % 8) if s < 4 or r < 4 else None for r in range(8)]
    pairs += [(64, 64), (64, 65), (65, 65)]
    pairs += [None] * (TERMS - len(pairs))
    one = [p[0] * BINS + p[1] if p else -1 for p in pairs]
    two = [p[1] * BINS + p[0] if p and p[0] != p[1] else -1 for p in pairs]
    return np.array([one, two], np.int32)


def symmetric_kernel_body(columns, kernel, out):
    width = out.shape[1]
    row = lax.broadcasted_iota(jnp.int32, (256, width), 0).astype(F32).astype(jnp.bfloat16)
    picks = []
    for base in range(0, kernel.shape[1], 256):
        near = jnp.clip(columns[...] - base, -1, 256).astype(F32).astype(jnp.bfloat16)
        hit = (row == near[0:1]) | (row == near[1:2])
        picks.append(jnp.where(hit, jnp.bfloat16(1), jnp.bfloat16(0)))
    total = jnp.dot(kernel[...], jnp.concatenate(picks, axis=0), preferred_element_type=F32)
    out[...] = total.astype(jnp.bfloat16)


def symmetric_kernel(kernel):
    wide = -(-kernel.shape[1] // 256) * 256
    padded = jnp.pad(kernel, ((0, 80 - BINS), (0, wide - kernel.shape[1])))
    return pl.pallas_call(
        symmetric_kernel_body,
        grid=(TERMS // 256,),
        in_specs=[
            pl.BlockSpec((2, 256), lambda i: (0, i)),
            pl.BlockSpec((80, wide), lambda i: (0, 0)),
        ],
        out_specs=pl.BlockSpec((80, 256), lambda i: (0, i)),
        out_shape=jax.ShapeDtypeStruct((80, TERMS), jnp.bfloat16),
        compiler_params=params(16),
        cost_estimate=pl.CostEstimate(flops=2 * 10**9, bytes_accessed=10**6, transcendentals=0),
    )(jnp.asarray(pair_columns()), padded)


def coalesce(q, sym):
    terms = pair_terms(q)
    packed = [
        jnp.concatenate(terms[2 * r : 2 * r + 2], axis=0).astype(jnp.bfloat16) for r in range(TERMS // 16)
    ]
    gained = jnp.dot(sym[...], jnp.concatenate(packed, axis=0), preferred_element_type=F32)
    return q + gained[0:PACKED]


def several(begin, end, body, at_once):
    def step(k, _):
        for j in range(at_once):
            body(begin + k * at_once + j)
        return 0

    lax.fori_loop(0, lax.div(end - begin, at_once), step, 0)


def neighbours(table, l):
    position = lax.rem(l, RUN)
    back, y, z = upwind_of(table, position)
    return jnp.where(back, l - RUN, l + RUN), y + (l - position), z + (l - position)


def cross_flux(count, block_at, table, q1, cs, fy, fz, v0, vf):
    def cross_body(i):
        l = block_at(i)
        _, uy, uz = neighbours(table, l)
        for w in range(2):
            q = read(q1, l, v0 + w)
            before_y = step_y(jnp.where(last_y(), read(q1, uy, v0 + w), q))
            before_z = step_z(jnp.where(last_z(), read(q1, uz, v0 + w), q))
            fy[l, :, span(w)] = flat(limited(q, speed(cs, l, 1, vf + w), before_y))
            fz[l, :, span(w)] = flat(limited(q, speed(cs, l, 2, vf + w), before_z))

    several(0, count, cross_body, STENCILS)


def cross(table, l, fy, fz, w):
    _, uy, uz = neighbours(table, l)
    y_own, z_own = read(fy, l, w), read(fz, l, w)
    y_in = step_y(jnp.where(last_y(), read(fy, uy, w), y_own))
    z_in = step_z(jnp.where(last_z(), read(fz, uz, w), z_own))
    return (y_in - y_own) + (z_in - z_own)


def coalesce_all(begin, end, count, block_at, second, q2, sym, out):
    @pl.when((begin == 0) & (end > 0))
    def _():
        for j in range(PRODUCTS):
            second(block_at(j))

    def step(k, _):
        i = begin + k * PRODUCTS
        at = [block_at(i + j) for j in range(PRODUCTS)]
        for l in at:
            out[l] = coalesce(q2[l], sym)[0:BINS]
        for j in range(PRODUCTS):
            second(block_at(jnp.minimum(i + PRODUCTS + j, count - 1)))
        return 0

    lax.fori_loop(0, lax.div(end - begin, PRODUCTS), step, 0)


def upper_kernel(moved, scal, table, spectra, courant, sym, *rest):
    rest_out = rest[6 if moved else 0 :]
    low_q1, low_c, face, out, scal_out = rest_out[:5]
    pair, other = rest_out[5:7] if moved else (None, None)
    q0, cs, q1, fy, fz, q2, sems = rest_out[7 if moved else 5 :]
    for k in range(SCALARS):
        scal_out[k] = scal[k]
    here0, here = scal[HERE0], scal[HERE1] - scal[HERE0]
    count = scal[MID1] - scal[MID0] - here if moved else here

    def block_at(i):
        return i + jnp.where(i >= here0, here, 0) if moved else i + here0

    def gather(i, _):
        l = block_at(i)
        fetch(scal[MID0] + l, scal, spectra, courant, rest[:2] if moved else (), slice(0, CELLS), q0, cs, l)
        low_c[l] = cs[l, :, 0:HALF]
        return 0

    lax.fori_loop(0, count, gather, 0)

    def first(i):
        l = block_at(i)
        _, uy, uz = neighbours(table, l)
        q_prev = cx_prev = None
        for v in range(4):
            new = donor(q0, cs, l, v, q_prev, cx_prev, uy, uz)
            q_prev, cx_prev = read(q0, l, v), speed(cs, l, 0, v)
            if v < 2:
                low_q1[l, :, span(v)] = flat(new)
            else:
                q1[l, :, span(v - 2)] = flat(new)
        other = swap(new)
        face[RUN + l, 0:PACKED] = flat(jnp.where(upper(), limited(new, cx_prev, other), other))
        face[RUN + l, PACKED : 2 * PACKED] = flat(cx_prev * q_prev)

    several(0, count, first, STENCILS)
    cross_flux(count, block_at, table, q1, cs, fy, fz, 0, 2)

    def second(l):
        q_prev = read(low_q1, l, 1)
        f_prev = limited(q_prev, speed(cs, l, 0, 1), swap(q_prev))
        for w in range(2):
            q = read(q1, l, w)
            f = limited(q, speed(cs, l, 0, w + 2), swap(jnp.where(upper(), q_prev, q)))
            new = q - f + swap(jnp.where(upper(), f_prev, f)) + cross(table, l, fy, fz, w)
            q2[l, :, span(w)] = flat(new)
            q_prev, f_prev = q, f

    coalesce_all(0, count, count, block_at, second, q2, sym, out)
    if not moved:
        return
    whole = scal[MID1] - scal[MID0]

    def leave(act):
        def down(ref):
            act(pltpu.make_async_copy(out.at[pl.ds(0, RUN)], ref, sems.at[0]))

        def up(ref):
            act(pltpu.make_async_copy(out.at[pl.ds(whole - RUN, RUN)], ref, sems.at[1]))

        by_side(scal, pair, other, down, up, whole > 0, whole > 0)

    leave(lambda copy: copy.start())
    leave(lambda copy: copy.wait())


def upper_half(scal, table, spectra, courant, sym, *moved):
    capacity = spectra.shape[0]
    held = (capacity, PACKED, HALF)
    shapes = [held, (capacity, 24, HALF), (capacity + 2 * RUN, 2 * PACKED, LANES), (capacity, BINS, HALF)]
    return pl.pallas_call(
        functools.partial(upper_kernel, bool(moved)),
        in_specs=[SMEM, SMEM] + [VMEM] * 3 + ([VMEM] * 6 if moved else []),
        out_specs=[VMEM] * 4 + [SMEM] + ([ANY] * 2 if moved else []),
        out_shape=[jax.ShapeDtypeStruct(shape, F32) for shape in shapes]
        + [jax.ShapeDtypeStruct((SCALARS,), jnp.int32)]
        + ([jax.ShapeDtypeStruct((RUN, BINS, HALF), F32)] * 2 if moved else []),
        scratch_shapes=[pltpu.VMEM((capacity, PACKED, CELLS), F32), pltpu.VMEM((capacity, 24, CELLS), F32)]
        + [pltpu.VMEM(held, F32)] * 4
        + [pltpu.SemaphoreType.DMA((2,))],
        input_output_aliases={7: 0, 8: 1, 9: 2, 10: 3} if moved else {},
        compiler_params=params(28),
        cost_estimate=pl.CostEstimate(flops=4 * 10**9, bytes_accessed=20 * 10**6, transcendentals=0),
    )(scal, table, spectra, courant, sym, *moved)


def lower_kernel(scal, table, _, cs, __, high_cells, in_pair, in_other, sym, result, pair, other, q1, face, low_cells, fy, fz, q2, blank, sems, blank_sems):
    count = scal[MID1] - scal[MID0]
    runs = lax.div(count, RUN)
    shift, slots = scal[MID0] - scal[NEW0], scal[NEW1] - scal[NEW0]

    def leave(half, act):
        source = (low_cells, high_cells)[half]
        cells = pl.ds(half * HALF, HALF)

        def body(r, _):
            first = r * RUN
            block = source.at[pl.ds(first, RUN)]

            def down(ref):
                act(pltpu.make_async_copy(block, ref, sems.at[half, 0]))

            def up(ref):
                act(pltpu.make_async_copy(block, ref, sems.at[half, 1]))

            if half == 0:
                by_side(scal, pair, other, down, up, r == 0, r == runs - 1)

            slot = first + shift
            fits = (slot >= 0) & (slot + RUN <= slots)

            @pl.when(fits)
            def _():
                act(pltpu.make_async_copy(block, result.at[pl.ds(slot, RUN), :, cells], sems.at[half, 2 + first]))

            def one(l, _):
                @pl.when((l + shift >= 0) & (l + shift < slots))
                def _():
                    act(pltpu.make_async_copy(source.at[l], result.at[l + shift, :, cells], sems.at[half, 2 + l]))

                return 0

            @pl.when(jnp.logical_not(fits))
            def _():
                lax.fori_loop(first, first + RUN, one, 0)

            return 0

        return body

    def start(copy):
        copy.start()

    def wait(copy):
        copy.wait()

    def clear(act):
        many = blank.shape[0]
        dead = result.shape[0] - slots
        whole = lax.div(dead, many)

        def chunk(k, _):
            at = slots + k * many
            act(pltpu.make_async_copy(blank, result.at[pl.ds(at, many)], blank_sems.at[k]))
            return 0

        lax.fori_loop(0, whole, chunk, 0)

        def one(s, _):
            act(pltpu.make_async_copy(blank.at[0], result.at[s], blank_sems.at[s]))
            return 0

        lax.fori_loop(slots + whole * many, result.shape[0], one, 0)

    lax.fori_loop(0, runs, leave(1, start), 0)
    blank[...] = jnp.zeros(blank.shape, F32)
    clear(start)

    def expand(base, ref):
        for i in range(RUN // 2):
            flux = ref[RUN + i]
            for k in (2 * i, 2 * i + 1):
                face[base + k, 0:PACKED] = ref[k]
            face[base + 2 * i, PACKED : 2 * PACKED] = pltpu.roll(flux, 64, 1)
            face[base + 2 * i + 1, PACKED : 2 * PACKED] = flux

    always = count > 0
    at_high = functools.partial(expand, count + RUN)
    by_side(scal, in_pair, in_other, functools.partial(expand, 0), at_high, always, always)

    def fix(l):
        ux, _, _ = neighbours(table, l)
        flux = swap(view(face[RUN + ux, PACKED : 2 * PACKED]))
        q1[l, :, span(0)] += flat(jnp.where(upper(), 0.0, flux))

    several(0, count, fix, STENCILS)
    cross_flux(count, lambda i: i, table, q1, cs, fy, fz, 0, 0)

    def second(l):
        side = view(face[RUN + neighbours(table, l)[0], 0:PACKED])
        q = read(q1, l, 0)
        f = limited(q, speed(cs, l, 0, 0), jnp.where(upper(), swap(q), side))
        q2[l, :, span(0)] = flat(q - f + swap(jnp.where(upper(), side, f)) + cross(table, l, fy, fz, 0))
        q_prev, f_prev = q, f
        q = read(q1, l, 1)
        f = limited(q, speed(cs, l, 0, 1), swap(jnp.where(upper(), q_prev, q)))
        q2[l, :, span(1)] = flat(q - f + swap(jnp.where(upper(), f_prev, f)) + cross(table, l, fy, fz, 1))

    def one_run(r, _):
        coalesce_all(r * RUN, r * RUN + RUN, count, lambda i: i, second, q2, sym, low_cells)
        leave(0, start)(r, 0)
        return 0

    lax.fori_loop(0, runs, one_run, 0)
    lax.fori_loop(0, runs, leave(0, wait), 0)
    lax.fori_loop(0, runs, leave(1, wait), 0)
    clear(wait)


def lower_half(scal, table, arrays, in_pair, in_other, sym):
    capacity = arrays[0].shape[0]
    whole = jax.ShapeDtypeStruct((capacity, BINS, CELLS), F32)
    sent = jax.ShapeDtypeStruct((RUN, BINS, HALF), F32)
    held = pltpu.VMEM((capacity, PACKED, HALF), F32)
    return pl.pallas_call(
        lower_kernel,
        in_specs=[SMEM, SMEM] + [VMEM] * 7,
        out_specs=[ANY] * 3 + [VMEM] * 2,
        out_shape=[whole, sent, sent] + [jax.ShapeDtypeStruct(x.shape, F32) for x in (arrays[0], arrays[2])],
        input_output_aliases={2: 3, 4: 4},
        scratch_shapes=[
            pltpu.VMEM((capacity, BINS, HALF), F32),
            held,
            held,
            held,
            pltpu.VMEM((4, BINS, CELLS), F32),
            pltpu.SemaphoreType.DMA((2, capacity + 2)),
            pltpu.SemaphoreType.DMA((capacity,)),
        ],
        compiler_params=params(30),
        cost_estimate=pl.CostEstimate(flops=8 * 10**9, bytes_accessed=20 * 10**6, transcendentals=0),
    )(scal, table, *arrays, in_pair, in_other, sym)[:3]


def place_moved_kernel(scal, *rest):
    halves, out, sems = (rest[0:2], rest[2:4]), rest[5], rest[6]
    first, end = scal[NEW0], scal[NEW1]

    def copies(act):
        for half in range(2):
            cells = pl.ds(half * HALF, HALF)
            for k in range(RUN):
                low, high = scal[MID0] - RUN + k, scal[MID1] + k

                def put(side, block, ref, k=k, half=half, cells=cells):
                    act(pltpu.make_async_copy(ref.at[k], out.at[block - first, :, cells], sems.at[half, side, k]))

                low_in = (low >= first) & (low < end)
                high_in = (high >= first) & (high < end)
                from_low, from_high = functools.partial(put, 0, low), functools.partial(put, 1, high)
                by_side(scal, *halves[half], from_low, from_high, low_in, high_in)

    copies(lambda copy: copy.start())
    copies(lambda copy: copy.wait())


def place_moved(scal, lower, upper_, out):
    return pl.pallas_call(
        place_moved_kernel,
        in_specs=[SMEM] + [VMEM] * 4 + [ANY],
        out_specs=ANY,
        out_shape=jax.ShapeDtypeStruct(out.shape, F32),
        scratch_shapes=[pltpu.SemaphoreType.DMA((2, 2, RUN))],
        input_output_aliases={5: 0},
        compiler_params=params(8),
    )(scal, *lower, *upper_, out)


def bounds_kernel(device, old_count, new_count, out):
    ids = lax.broadcasted_iota(jnp.int32, old_count.shape, 1)

    def total(counts, p):
        return jnp.sum(jnp.where(ids < p, counts[...], 0).astype(F32)).astype(jnp.int32)

    def start(p):
        old, new = total(old_count, p), total(new_count, p)
        least = lax.div(jnp.maximum(old, new) + RUN - 1, RUN) * RUN - RUN
        most = lax.div(jnp.minimum(old, new), RUN) * RUN + RUN
        return old, jnp.clip(2 * RUN * p, least, most), new

    old0, mid0, new0 = start(device[0])
    old1, mid1, new1 = start(device[0] + 1)
    out[OLD0], out[OLD1], out[MID0], out[MID1], out[NEW0], out[NEW1] = old0, old1, mid0, mid1, new0, new1
    here0 = lax.div(jnp.maximum(old0 - mid0, 0) + RUN - 1, RUN) * RUN
    here1 = lax.div(jnp.minimum(old1, mid1) - mid0, RUN) * RUN
    out[ODD] = lax.rem(device[0], 2)
    out[HERE0], out[HERE1] = here0, jnp.clip(here1, here0, here0 + RUN)


def bounds(device, old_count, new_count):
    return pl.pallas_call(
        bounds_kernel,
        in_specs=[SMEM, VMEM, VMEM],
        out_specs=SMEM,
        out_shape=jax.ShapeDtypeStruct((SCALARS,), jnp.int32),
    )(device, old_count.reshape(1, -1), new_count.reshape(1, -1))


def on_device(devices, spectra, courant, kernel, old_count, new_count, upwind):
    device = lax.axis_index("blocks").astype(jnp.int32).reshape(1)
    pairs = [(i, i ^ 1) for i in range(devices)]
    others = [(i, i + 1) for i in range(1, devices - 1, 2)]
    others += [(j, i) for i, j in others]
    ends = [(devices - 1, 0), (0, devices - 1)]

    def exchange(pair, other, route):
        from_other = lax.ppermute(other, "blocks", route)
        return lax.ppermute(pair, "blocks", pairs), from_other

    courant = jnp.swapaxes(courant, 0, 1)
    moved = exchange(*pack(old_count, device, spectra, courant), others)
    scal = bounds(device, old_count, new_count)
    table = upwind[RUN : 2 * RUN].reshape(-1)
    sym = symmetric_kernel(kernel)
    *early, scal = upper_half(scal, table, spectra, courant, sym)
    *sides, scal = faces(scal, table, spectra, courant, *moved, early[2])
    sides = exchange(*sides, others + ends)
    *arrays, scal, pair, other = upper_half(scal, table, spectra, courant, sym, *moved, *early)
    upper_results = exchange(pair, other, others)
    result, *results = lower_half(scal, table, arrays, *sides, sym)
    return place_moved(scal, exchange(*results, others), upper_results, result)


def solution(mesh):
    in_specs = (P("blocks", None, None), P("blocks", None, None), P(), P(), P(), P())
    out_specs = P("blocks", None, None)
    return jax.shard_map(
        functools.partial(on_device, mesh.shape["blocks"]),
        mesh=mesh,
        in_specs=in_specs,
        out_specs=out_specs,
        check_vma=False,
    )
```

```python
import functools

import jax
import jax.numpy as jnp
import numpy as np
from jax import lax
from jax.experimental import pallas as pl
from jax.experimental.pallas import tpu as pltpu
from jax.sharding import PartitionSpec as P

RUN = 12
BINS = 66
CELLS = 512
HALF = 256
LANES = 128
PACKED = 72
FULL = 64
TERMS = 2304
GROUPS = 9
STENCILS = 12
PRODUCTS = 3
FACES = 18
F32 = jnp.float32
VMEM = pl.BlockSpec(memory_space=pltpu.VMEM)
SMEM = pl.BlockSpec(memory_space=pltpu.SMEM)
OLD0, OLD1, MID0, MID1, NEW0, NEW1, HERE0, HERE1, ODD = range(9)
SCALARS = 9
ANY = pl.BlockSpec(memory_space=pl.ANY)


def params(mib):
    return pltpu.CompilerParams(vmem_limit_bytes=mib * 2**20)


def lanes():
    return lax.broadcasted_iota(jnp.int32, (8, LANES), 1)


def span(v):
    return slice(v * LANES, (v + 1) * LANES)


def upper():
    return lanes() >= 64


def last_y():
    return lanes() // 8 % 8 == 7


def last_z():
    return lanes() % 8 == 7


def view(x):
    return x.reshape(GROUPS, 8, LANES)


def flat(x):
    return x.reshape(PACKED, LANES)


def swap(x):
    return pltpu.roll(flat(x), 64, 1).reshape(x.shape)


def permuted(x, source):
    return view(jnp.take_along_axis(flat(x), source, axis=1, mode="promise_in_bounds"))


def wide_lanes():
    return lax.broadcasted_iota(jnp.int32, (PACKED, LANES), 1)


def step_y(x):
    at = wide_lanes()
    return permuted(x, jnp.where(at // 8 % 8 == 0, at + 56, at - 8))


def step_z(x):
    at = wide_lanes()
    return permuted(x, jnp.where(at % 8 == 0, at + 7, at - 1))


def minmod(a, e):
    return jnp.maximum(jnp.minimum(a, e), 0.0)


def limited(q, c, before):
    return c * (q + (0.5 * (1.0 - c)) * minmod(q - before, q))


def upwind_of(table, position):
    back = table[3 * position] < RUN + position
    return back, table[3 * position + 1] - RUN, table[3 * position + 2] - RUN


def by_side(scal, pair, other, act_low, act_high, is_low, is_high):
    odd = scal[ODD] == 1
    for mine, low, high in ((odd, pair, other), (jnp.logical_not(odd), other, pair)):
        pl.when(mine & is_low)(functools.partial(act_low, low))
        pl.when(mine & is_high)(functools.partial(act_high, high))


def read(ref, l, v):
    return view(ref[l, :, span(v)])


def speed(ref, l, d, v):
    return ref[l, 8 * d : 8 * d + 8, span(v)]


def donor(q0, cs, l, v, q_prev, cx_prev, uy, uz):
    q, cx, cy, cz = read(q0, l, v), speed(cs, l, 0, v), speed(cs, l, 1, v), speed(cs, l, 2, v)
    up, ly, lz = upper(), last_y(), last_z()
    in_x = swap(jnp.where(up, 0.0 if q_prev is None else cx_prev * q_prev, cx * q))
    in_y = step_y(jnp.where(ly, speed(cs, uy, 1, v), cy) * jnp.where(ly, read(q0, uy, v), q))
    in_z = step_z(jnp.where(lz, speed(cs, uz, 2, v), cz) * jnp.where(lz, read(q0, uz, v), q))
    return (1.0 - (cx + cy + cz)) * q + in_x + in_y + in_z


def fetch(block, scal, spectra, courant, moved, cells, q_dst, c_dst, at):
    own0, own1 = scal[OLD0], scal[OLD1]

    def spread(d, row):
        c_dst[at, 8 * d : 8 * d + 8] = jnp.broadcast_to(row, (8, row.shape[1]))

    def owned():
        q_dst[at, 0:BINS] = spectra[block - own0, :, cells]
        for d in range(3):
            spread(d, courant[d, pl.ds(block - own0, 1), cells])

    if not moved:
        owned()
        return
    pl.when((block >= own0) & (block < own1))(owned)

    def received(i, ref):
        q_dst[at] = ref[i, :, cells]
        for d in range(3):
            spread(d, ref[i, BINS + d : BINS + d + 1, cells])

    from_low = functools.partial(received, block - own0 + RUN)
    from_high = functools.partial(received, block - own1)
    by_side(scal, *moved, from_low, from_high, block < own0, block >= own1)


def pack_kernel(old_count, device, spectra, courant, pair, other, raw, speeds, joined, c_sem, in_sems, out_sems):
    tail = old_count[device[0]] - RUN
    odd = lax.rem(device[0], 2) == 1
    all_speeds = pltpu.make_async_copy(courant, speeds, c_sem)
    all_speeds.start()
    steps = [(k, side) for k in range(0, RUN, 2) for side in (0, 1)]
    starts = (tail, 0)

    def arrival(k, side):
        return pltpu.make_async_copy(
            spectra.at[pl.ds(starts[side] + k, 2)], raw.at[side, pl.ds(k, 2)], in_sems.at[side, k]
        )

    def leave(k, side, act):
        def to(out):
            act(pltpu.make_async_copy(joined.at[side, pl.ds(k, 2)], out.at[pl.ds(k, 2)], out_sems.at[side, k]))

        pl.when(odd)(functools.partial(to, (other, pair)[side]))
        pl.when(jnp.logical_not(odd))(functools.partial(to, (pair, other)[side]))

    for k, side in steps:
        arrival(k, side).start()
    all_speeds.wait()
    for k, side in steps:
        arrival(k, side).wait()
        for i in (k, k + 1):
            joined[side, i, 0:BINS] = raw[side, i]
            for d in range(3):
                joined[side, i, BINS + d : BINS + d + 1] = speeds[d, pl.ds(starts[side] + i, 1)]
        leave(k, side, lambda copy: copy.start())
    for k, side in steps:
        leave(k, side, lambda copy: copy.wait())


def pack(old_count, device, spectra, courant):
    sent = jax.ShapeDtypeStruct((RUN, PACKED, CELLS), F32)
    return pl.pallas_call(
        pack_kernel,
        in_specs=[SMEM, SMEM, ANY, ANY],
        out_specs=[ANY, ANY],
        out_shape=[sent, sent],
        scratch_shapes=[
            pltpu.VMEM((2, RUN, BINS, CELLS), F32),
            pltpu.VMEM(courant.shape, F32),
            pltpu.VMEM((2, RUN, PACKED, CELLS), F32),
            pltpu.SemaphoreType.DMA(()),
            pltpu.SemaphoreType.DMA((2, RUN)),
            pltpu.SemaphoreType.DMA((2, RUN)),
        ],
        compiler_params=params(56),
    )(old_count, device, spectra, courant)


def face_kernel(scal, table, spectra, courant, in_pair, in_other, early, pair, other, scal_out, q0, cs, up, down):
    count = scal[MID1] - scal[MID0]
    for k in range(SCALARS):
        scal_out[k] = scal[k]

    def face(j):
        _, y, z = upwind_of(table, j)
        q1 = donor(q0, cs, j, 1, read(q0, j, 0), speed(cs, j, 0, 0), y, z)
        side = swap(q1)
        c = speed(cs, j, 0, 1)
        return jnp.where(upper(), limited(q1, c, side), side), c * read(q0, j, 1)

    def one_run(start, out):
        was_early = (start >= scal[HERE0]) & (start < scal[HERE1])

        def put(i, a0, b0, a1, b1):
            out[2 * i] = flat(a0)
            out[2 * i + 1] = flat(a1)
            out[RUN + i] = flat(jnp.where(upper(), b1, swap(b0)))

        def take(i, _):
            at = start + 2 * i
            parts = [view(early[RUN + l, k : k + PACKED]) for l in (at, at + 1) for k in (0, PACKED)]
            put(i, *parts)
            return 0

        def gather(j, _):
            block = scal[MID0] + start + j
            fetch(block, scal, spectra, courant, (in_pair, in_other), slice(HALF, CELLS), q0, cs, j)
            return 0

        def make(i, _):
            put(i, *face(2 * i), *face(2 * i + 1))
            return 0

        @pl.when(was_early)
        def _():
            lax.fori_loop(0, RUN // 2, take, 0)

        @pl.when(jnp.logical_not(was_early))
        def _():
            lax.fori_loop(0, RUN, gather, 0)
            lax.fori_loop(0, RUN // 2, make, 0)

    one_run(0, down)
    one_run(count - RUN, up)
    odd = scal[ODD] == 1

    @pl.when(odd)
    def _():
        pair[...] = down[...]
        other[...] = up[...]

    @pl.when(jnp.logical_not(odd))
    def _():
        pair[...] = up[...]
        other[...] = down[...]


def faces(scal, table, spectra, courant, in_pair, in_other, early):
    sent = jax.ShapeDtypeStruct((FACES, PACKED, LANES), F32)
    return pl.pallas_call(
        face_kernel,
        in_specs=[SMEM, SMEM] + [VMEM] * 5,
        out_specs=[VMEM, VMEM, SMEM],
        out_shape=[sent, sent, jax.ShapeDtypeStruct((SCALARS,), jnp.int32)],
        scratch_shapes=[
            pltpu.VMEM((RUN, PACKED, HALF), F32),
            pltpu.VMEM((RUN, 24, HALF), F32),
            pltpu.VMEM(sent.shape, F32),
            pltpu.VMEM(sent.shape, F32),
        ],
        compiler_params=params(10),
    )(scal, table, spectra, courant, in_pair, in_other, early)


def pair_terms(q):
    wide = q.shape[1]
    group = [q[8 * g : 8 * g + 8, :] for g in range(8)]
    row = [jnp.broadcast_to(q[i : i + 1, :], (8, wide)) for i in range(BINS)]
    out = [row[i] * group[g] for i in range(56) for g in range(i // 8 + 1, 8)]
    out += [row[i] * group[g] for i in (64, 65) for g in range(8)]
    for s in range(5):
        out += [x * (pltpu.roll(x, s, 0) if s else x) for x in group]
    at = lax.broadcasted_iota(jnp.int32, (8, wide), 0)
    rest = jnp.where(at < 2, row[64], row[65]) * jnp.where(at < 1, row[64], row[65])
    out.append(jnp.where(at < 3, rest, 0.0))
    return out + [jnp.zeros((8, wide), F32)] * (TERMS // 8 - len(out))


def pair_columns():
    pairs = [(i, j) for i in range(56) for j in range(i // 8 * 8 + 8, FULL)]
    pairs += [(i, j) for i in (64, 65) for j in range(FULL)]
    for s in range(5):
        for g in range(0, FULL, 8):
            pairs += [(g + r, g + (r - s) % 8) if s < 4 or r < 4 else None for r in range(8)]
    pairs += [(64, 64), (64, 65), (65, 65)]
    pairs += [None] * (TERMS - len(pairs))
    one = [p[0] * BINS + p[1] if p else -1 for p in pairs]
    two = [p[1] * BINS + p[0] if p and p[0] != p[1] else -1 for p in pairs]
    return np.array([one, two], np.int32)


def symmetric_kernel_body(columns, kernel, out):
    width = out.shape[1]
    row = lax.broadcasted_iota(jnp.int32, (256, width), 0).astype(F32).astype(jnp.bfloat16)
    picks = []
    for base in range(0, kernel.shape[1], 256):
        near = jnp.clip(columns[...] - base, -1, 256).astype(F32).astype(jnp.bfloat16)
        hit = (row == near[0:1]) | (row == near[1:2])
        picks.append(jnp.where(hit, jnp.bfloat16(1), jnp.bfloat16(0)))
    total = jnp.dot(kernel[...], jnp.concatenate(picks, axis=0), preferred_element_type=F32)
    out[...] = total.astype(jnp.bfloat16)


def symmetric_kernel(kernel):
    wide = -(-kernel.shape[1] // 256) * 256
    padded = jnp.pad(kernel, ((0, 80 - BINS), (0, wide - kernel.shape[1])))
    return pl.pallas_call(
        symmetric_kernel_body,
        grid=(TERMS // 256,),
        in_specs=[
            pl.BlockSpec((2, 256), lambda i: (0, i)),
            pl.BlockSpec((80, wide), lambda i: (0, 0)),
        ],
        out_specs=pl.BlockSpec((80, 256), lambda i: (0, i)),
        out_shape=jax.ShapeDtypeStruct((80, TERMS), jnp.bfloat16),
        compiler_params=params(16),
        cost_estimate=pl.CostEstimate(flops=2 * 10**9, bytes_accessed=10**6, transcendentals=0),
    )(jnp.asarray(pair_columns()), padded)


def coalesce(q, sym):
    terms = pair_terms(q)
    packed = [
        jnp.concatenate(terms[2 * r : 2 * r + 2], axis=0).astype(jnp.bfloat16) for r in range(TERMS // 16)
    ]
    gained = jnp.dot(sym[...], jnp.concatenate(packed, axis=0), preferred_element_type=F32)
    return q + gained[0:PACKED]


def several(begin, end, body, at_once):
    def step(k, _):
        for j in range(at_once):
            body(begin + k * at_once + j)
        return 0

    lax.fori_loop(0, lax.div(end - begin, at_once), step, 0)


def neighbours(table, l):
    position = lax.rem(l, RUN)
    back, y, z = upwind_of(table, position)
    return jnp.where(back, l - RUN, l + RUN), y + (l - position), z + (l - position)


def cross_flux(count, block_at, table, q1, cs, fy, fz, v0, vf):
    def cross_body(i):
        l = block_at(i)
        _, uy, uz = neighbours(table, l)
        for w in range(2):
            q = read(q1, l, v0 + w)
            before_y = step_y(jnp.where(last_y(), read(q1, uy, v0 + w), q))
            before_z = step_z(jnp.where(last_z(), read(q1, uz, v0 + w), q))
            fy[l, :, span(w)] = flat(limited(q, speed(cs, l, 1, vf + w), before_y))
            fz[l, :, span(w)] = flat(limited(q, speed(cs, l, 2, vf + w), before_z))

    several(0, count, cross_body, STENCILS)


def cross(table, l, fy, fz, w):
    _, uy, uz = neighbours(table, l)
    y_own, z_own = read(fy, l, w), read(fz, l, w)
    y_in = step_y(jnp.where(last_y(), read(fy, uy, w), y_own))
    z_in = step_z(jnp.where(last_z(), read(fz, uz, w), z_own))
    return (y_in - y_own) + (z_in - z_own)


def coalesce_all(begin, end, count, block_at, second, q2, sym, out):
    @pl.when((begin == 0) & (end > 0))
    def _():
        for j in range(PRODUCTS):
            second(block_at(j))

    def step(k, _):
        i = begin + k * PRODUCTS
        at = [block_at(i + j) for j in range(PRODUCTS)]
        for l in at:
            out[l] = coalesce(q2[l], sym)[0:BINS]
        for j in range(PRODUCTS):
            second(block_at(jnp.minimum(i + PRODUCTS + j, count - 1)))
        return 0

    lax.fori_loop(0, lax.div(end - begin, PRODUCTS), step, 0)


def upper_kernel(moved, scal, table, spectra, courant, sym, *rest):
    rest_out = rest[6 if moved else 0 :]
    low_q1, low_c, face, out, scal_out = rest_out[:5]
    pair, other = rest_out[5:7] if moved else (None, None)
    q0, cs, q1, fy, fz, q2, sems = rest_out[7 if moved else 5 :]
    for k in range(SCALARS):
        scal_out[k] = scal[k]
    here0, here = scal[HERE0], scal[HERE1] - scal[HERE0]
    count = scal[MID1] - scal[MID0] - here if moved else here

    def block_at(i):
        return i + jnp.where(i >= here0, here, 0) if moved else i + here0

    def gather(i, _):
        l = block_at(i)
        fetch(scal[MID0] + l, scal, spectra, courant, rest[:2] if moved else (), slice(0, CELLS), q0, cs, l)
        low_c[l] = cs[l, :, 0:HALF]
        return 0

    lax.fori_loop(0, count, gather, 0)

    def first(i):
        l = block_at(i)
        _, uy, uz = neighbours(table, l)
        q_prev = cx_prev = None
        for v in range(4):
            new = donor(q0, cs, l, v, q_prev, cx_prev, uy, uz)
            q_prev, cx_prev = read(q0, l, v), speed(cs, l, 0, v)
            if v < 2:
                low_q1[l, :, span(v)] = flat(new)
            else:
                q1[l, :, span(v - 2)] = flat(new)
        other = swap(new)
        face[RUN + l, 0:PACKED] = flat(jnp.where(upper(), limited(new, cx_prev, other), other))
        face[RUN + l, PACKED : 2 * PACKED] = flat(cx_prev * q_prev)

    several(0, count, first, STENCILS)
    cross_flux(count, block_at, table, q1, cs, fy, fz, 0, 2)

    def second(l):
        q_prev = read(low_q1, l, 1)
        f_prev = limited(q_prev, speed(cs, l, 0, 1), swap(q_prev))
        for w in range(2):
            q = read(q1, l, w)
            f = limited(q, speed(cs, l, 0, w + 2), swap(jnp.where(upper(), q_prev, q)))
            new = q - f + swap(jnp.where(upper(), f_prev, f)) + cross(table, l, fy, fz, w)
            q2[l, :, span(w)] = flat(new)
            q_prev, f_prev = q, f

    coalesce_all(0, count, count, block_at, second, q2, sym, out)
    if not moved:
        return
    whole = scal[MID1] - scal[MID0]

    def leave(act):
        def down(ref):
            act(pltpu.make_async_copy(out.at[pl.ds(0, RUN)], ref, sems.at[0]))

        def up(ref):
            act(pltpu.make_async_copy(out.at[pl.ds(whole - RUN, RUN)], ref, sems.at[1]))

        by_side(scal, pair, other, down, up, whole > 0, whole > 0)

    leave(lambda copy: copy.start())
    leave(lambda copy: copy.wait())


def upper_half(scal, table, spectra, courant, sym, *moved):
    capacity = spectra.shape[0]
    held = (capacity, PACKED, HALF)
    shapes = [held, (capacity, 24, HALF), (capacity + 2 * RUN, 2 * PACKED, LANES), (capacity, BINS, HALF)]
    return pl.pallas_call(
        functools.partial(upper_kernel, bool(moved)),
        in_specs=[SMEM, SMEM] + [VMEM] * 3 + ([VMEM] * 6 if moved else []),
        out_specs=[VMEM] * 4 + [SMEM] + ([ANY] * 2 if moved else []),
        out_shape=[jax.ShapeDtypeStruct(shape, F32) for shape in shapes]
        + [jax.ShapeDtypeStruct((SCALARS,), jnp.int32)]
        + ([jax.ShapeDtypeStruct((RUN, BINS, HALF), F32)] * 2 if moved else []),
        scratch_shapes=[pltpu.VMEM((capacity, PACKED, CELLS), F32), pltpu.VMEM((capacity, 24, CELLS), F32)]
        + [pltpu.VMEM(held, F32)] * 4
        + [pltpu.SemaphoreType.DMA((2,))],
        input_output_aliases={7: 0, 8: 1, 9: 2, 10: 3} if moved else {},
        compiler_params=params(28),
        cost_estimate=pl.CostEstimate(flops=4 * 10**9, bytes_accessed=20 * 10**6, transcendentals=0),
    )(scal, table, spectra, courant, sym, *moved)


def lower_kernel(scal, table, _, cs, __, high_cells, in_pair, in_other, sym, result, pair, other, q1, face, low_cells, fy, fz, q2, blank, sems, blank_sems):
    count = scal[MID1] - scal[MID0]
    runs = lax.div(count, RUN)
    shift, slots = scal[MID0] - scal[NEW0], scal[NEW1] - scal[NEW0]

    def leave(half, act):
        source = (low_cells, high_cells)[half]
        cells = pl.ds(half * HALF, HALF)

        def body(r, _):
            first = r * RUN
            block = source.at[pl.ds(first, RUN)]

            def down(ref):
                act(pltpu.make_async_copy(block, ref, sems.at[half, 0]))

            def up(ref):
                act(pltpu.make_async_copy(block, ref, sems.at[half, 1]))

            if half == 0:
                by_side(scal, pair, other, down, up, r == 0, r == runs - 1)

            slot = first + shift
            fits = (slot >= 0) & (slot + RUN <= slots)

            @pl.when(fits)
            def _():
                act(pltpu.make_async_copy(block, result.at[pl.ds(slot, RUN), :, cells], sems.at[half, 2 + first]))

            def one(l, _):
                @pl.when((l + shift >= 0) & (l + shift < slots))
                def _():
                    act(pltpu.make_async_copy(source.at[l], result.at[l + shift, :, cells], sems.at[half, 2 + l]))

                return 0

            @pl.when(jnp.logical_not(fits))
            def _():
                lax.fori_loop(first, first + RUN, one, 0)

            return 0

        return body

    def start(copy):
        copy.start()

    def wait(copy):
        copy.wait()

    def clear(act):
        many = blank.shape[0]
        dead = result.shape[0] - slots
        whole = lax.div(dead, many)

        def chunk(k, _):
            at = slots + k * many
            act(pltpu.make_async_copy(blank, result.at[pl.ds(at, many)], blank_sems.at[k]))
            return 0

        lax.fori_loop(0, whole, chunk, 0)

        def one(s, _):
            act(pltpu.make_async_copy(blank.at[0], result.at[s], blank_sems.at[s]))
            return 0

        lax.fori_loop(slots + whole * many, result.shape[0], one, 0)

    lax.fori_loop(0, runs, leave(1, start), 0)
    blank[...] = jnp.zeros(blank.shape, F32)
    clear(start)

    def expand(base, ref):
        for i in range(RUN // 2):
            flux = ref[RUN + i]
            for k in (2 * i, 2 * i + 1):
                face[base + k, 0:PACKED] = ref[k]
            face[base + 2 * i, PACKED : 2 * PACKED] = pltpu.roll(flux, 64, 1)
            face[base + 2 * i + 1, PACKED : 2 * PACKED] = flux

    always = count > 0
    at_high = functools.partial(expand, count + RUN)
    by_side(scal, in_pair, in_other, functools.partial(expand, 0), at_high, always, always)

    def fix(l):
        ux, _, _ = neighbours(table, l)
        flux = swap(view(face[RUN + ux, PACKED : 2 * PACKED]))
        q1[l, :, span(0)] += flat(jnp.where(upper(), 0.0, flux))

    several(0, count, fix, STENCILS)
    cross_flux(count, lambda i: i, table, q1, cs, fy, fz, 0, 0)

    def second(l):
        side = view(face[RUN + neighbours(table, l)[0], 0:PACKED])
        q = read(q1, l, 0)
        f = limited(q, speed(cs, l, 0, 0), jnp.where(upper(), swap(q), side))
        q2[l, :, span(0)] = flat(q - f + swap(jnp.where(upper(), side, f)) + cross(table, l, fy, fz, 0))
        q_prev, f_prev = q, f
        q = read(q1, l, 1)
        f = limited(q, speed(cs, l, 0, 1), swap(jnp.where(upper(), q_prev, q)))
        q2[l, :, span(1)] = flat(q - f + swap(jnp.where(upper(), f_prev, f)) + cross(table, l, fy, fz, 1))

    def one_run(r, _):
        coalesce_all(r * RUN, r * RUN + RUN, count, lambda i: i, second, q2, sym, low_cells)
        leave(0, start)(r, 0)
        return 0

    lax.fori_loop(0, runs, one_run, 0)
    lax.fori_loop(0, runs, leave(0, wait), 0)
    lax.fori_loop(0, runs, leave(1, wait), 0)
    clear(wait)


def lower_half(scal, table, arrays, in_pair, in_other, sym):
    capacity = arrays[0].shape[0]
    whole = jax.ShapeDtypeStruct((capacity, BINS, CELLS), F32)
    sent = jax.ShapeDtypeStruct((RUN, BINS, HALF), F32)
    held = pltpu.VMEM((capacity, PACKED, HALF), F32)
    return pl.pallas_call(
        lower_kernel,
        in_specs=[SMEM, SMEM] + [VMEM] * 7,
        out_specs=[ANY] * 3 + [VMEM] * 2,
        out_shape=[whole, sent, sent] + [jax.ShapeDtypeStruct(x.shape, F32) for x in (arrays[0], arrays[2])],
        input_output_aliases={2: 3, 4: 4},
        scratch_shapes=[
            pltpu.VMEM((capacity, BINS, HALF), F32),
            held,
            held,
            held,
            pltpu.VMEM((4, BINS, CELLS), F32),
            pltpu.SemaphoreType.DMA((2, capacity + 2)),
            pltpu.SemaphoreType.DMA((capacity,)),
        ],
        compiler_params=params(30),
        cost_estimate=pl.CostEstimate(flops=8 * 10**9, bytes_accessed=20 * 10**6, transcendentals=0),
    )(scal, table, *arrays, in_pair, in_other, sym)[:3]


def place_moved_kernel(scal, *rest):
    halves, out, sems = (rest[0:2], rest[2:4]), rest[5], rest[6]
    first, end = scal[NEW0], scal[NEW1]

    def copies(act):
        for half in range(2):
            cells = pl.ds(half * HALF, HALF)
            for k in range(RUN):
                low, high = scal[MID0] - RUN + k, scal[MID1] + k

                def put(side, block, ref, k=k, half=half, cells=cells):
                    act(pltpu.make_async_copy(ref.at[k], out.at[block - first, :, cells], sems.at[half, side, k]))

                low_in = (low >= first) & (low < end)
                high_in = (high >= first) & (high < end)
                from_low, from_high = functools.partial(put, 0, low), functools.partial(put, 1, high)
                by_side(scal, *halves[half], from_low, from_high, low_in, high_in)

    copies(lambda copy: copy.start())
    copies(lambda copy: copy.wait())


def place_moved(scal, lower, upper_, out):
    return pl.pallas_call(
        place_moved_kernel,
        in_specs=[SMEM] + [VMEM] * 4 + [ANY],
        out_specs=ANY,
        out_shape=jax.ShapeDtypeStruct(out.shape, F32),
        scratch_shapes=[pltpu.SemaphoreType.DMA((2, 2, RUN))],
        input_output_aliases={5: 0},
        compiler_params=params(8),
    )(scal, *lower, *upper_, out)


def bounds_kernel(device, old_count, new_count, out):
    ids = lax.broadcasted_iota(jnp.int32, old_count.shape, 1)

    def total(counts, p):
        return jnp.sum(jnp.where(ids < p, counts[...], 0).astype(F32)).astype(jnp.int32)

    def start(p):
        old, new = total(old_count, p), total(new_count, p)
        least = lax.div(jnp.maximum(old, new) + RUN - 1, RUN) * RUN - RUN
        most = lax.div(jnp.minimum(old, new), RUN) * RUN + RUN
        return old, jnp.clip(2 * RUN * p, least, most), new

    old0, mid0, new0 = start(device[0])
    old1, mid1, new1 = start(device[0] + 1)
    out[OLD0], out[OLD1], out[MID0], out[MID1], out[NEW0], out[NEW1] = old0, old1, mid0, mid1, new0, new1
    here0 = lax.div(jnp.maximum(old0 - mid0, 0) + RUN - 1, RUN) * RUN
    here1 = lax.div(jnp.minimum(old1, mid1) - mid0, RUN) * RUN
    out[ODD] = lax.rem(device[0], 2)
    out[HERE0], out[HERE1] = here0, jnp.clip(here1, here0, here0 + RUN)


def bounds(device, old_count, new_count):
    return pl.pallas_call(
        bounds_kernel,
        in_specs=[SMEM, VMEM, VMEM],
        out_specs=SMEM,
        out_shape=jax.ShapeDtypeStruct((SCALARS,), jnp.int32),
    )(device, old_count.reshape(1, -1), new_count.reshape(1, -1))


def on_device(devices, spectra, courant, kernel, old_count, new_count, upwind):
    device = lax.axis_index("blocks").astype(jnp.int32).reshape(1)
    pairs = [(i, i ^ 1) for i in range(devices)]
    others = [(i, i + 1) for i in range(1, devices - 1, 2)]
    others += [(j, i) for i, j in others]
    ends = [(devices - 1, 0), (0, devices - 1)]

    def exchange(pair, other, route):
        from_other = lax.ppermute(other, "blocks", route)
        return lax.ppermute(pair, "blocks", pairs), from_other

    courant = jnp.swapaxes(courant, 0, 1)
    moved = exchange(*pack(old_count, device, spectra, courant), others)
    scal = bounds(device, old_count, new_count)
    table = upwind[RUN : 2 * RUN].reshape(-1)
    sym = symmetric_kernel(kernel)
    *early, scal = upper_half(scal, table, spectra, courant, sym)
    *sides, scal = faces(scal, table, spectra, courant, *moved, early[2])
    sides = exchange(*sides, others + ends)
    *arrays, scal, pair, other = upper_half(scal, table, spectra, courant, sym, *moved, *early)
    upper_results = exchange(pair, other, others)
    result, *results = lower_half(scal, table, arrays, *sides, sym)
    return place_moved(scal, exchange(*results, others), upper_results, result)


def solution(mesh):
    in_specs = (P("blocks", None, None), P("blocks", None, None), P(), P(), P(), P())
    out_specs = P("blocks", None, None)
    return jax.shard_map(
        functools.partial(on_device, mesh.shape["blocks"]),
        mesh=mesh,
        in_specs=in_specs,
        out_specs=out_specs,
        check_vma=False,
    )
```
